128 devices in a mesh: scen: 32 (over x, z, core), col: 4 (over y).
Axes of the slice: x: 4, y: 4, z: 4, core: 2. Of those that a mesh axis runs over, the one named last changes fastest.
Arguments:
- tile_values: float32 [32, 4, 64, 256, 256], P('scen', 'col'), may hold values from -1100 to 1100
- tile_rows: int32 [32, 4, 64], P('scen', 'col'), may hold values from 0 to 127, as said below
- tile_cols: int32 [32, 4, 64], P('scen', 'col'), may hold values from 0 to 263, as said below
- cost_local: float32 [32, 4, 8, 256], P('scen', 'col'), may hold values from -12 to 12
- cost_link: float32 [4, 256, 256], P('col'), may hold values from -5 to 5
- bound_local: float32 [32, 4, 8, 256], P('scen', 'col'), may hold values from 0.5 to 4
- bound_link: float32 [4, 256, 256], P('col'), may hold values from 0.5 to 4
- rhs: float32 [32, 128, 256], P('scen', 'col'), may hold values from -12 to 12
- start_local: float32 [32, 4, 8, 256], P('scen', 'col'), may hold values from 0 to 1
- start_link: float32 [4, 256, 256], P('col'), may hold values from 0 to 1
- start_dual: float32 [32, 128, 256], P('scen', 'col'), may hold values from -5 to 5
Outputs:
- solution_local: float32 [32, 4, 8, 256], P('scen', 'col')
- solution_link: float32 [4, 256, 256], P('col')
- multipliers: float32 [32, 128, 256], P('scen', 'col')
The draws below stay inside these ranges and needn't reach their ends.
Inputs may be any that keep to these rules, and one draw needn't show every extreme that they name: Within one block the tiles stand at distinct positions, listed in increasing order of tile_rows * 264 + tile_cols. Every tile row of a scenario has a tile in some block of that scenario, every one of a block's first 8 tile columns has a tile in that block, and every linking tile column has a tile in some block of that index of col. `tile_cols`: tile columns below 8 are the block's scenario columns, the others linking tile columns.
All inputs are finite; a program needn't handle non-finite values.
Results may differ from the reference program's by a relative error of at most 0.0003.
Values sent between devices are 32-bit elements; how exact they have to be, the bound alone decides.
No kernel may reach another device: no remote copies, remote signals or barrier semaphores. Data moves between devices by JAX's collectives and lax.ppermute only.
A program may use at most 64 MiB of HBM per device.

```python
import math
import jax
import jax.numpy as jnp
from jax import lax

TILE = 256
RT = 128
CT = 8
LT = 256
ITERS = 3
SCEN = 32
NT = 64
N_COL = 4


def rising(count):
    return 1.0 + 2.0 * jnp.arange(count, dtype=jnp.float32) / max(count - 1, 1)


def tile_layout(key):
    band_rows = RT // N_COL
    per_scen = LT // SCEN
    width_tiles = CT + LT
    cell_count = RT * width_tiles
    scen_pos = jnp.arange(SCEN, dtype=jnp.int32)[:, None, None]
    col_pos = jnp.arange(N_COL, dtype=jnp.int32)[None, :, None]
    steps_row = jnp.arange(band_rows, dtype=jnp.int32)[None, None, :]
    row_cells = (col_pos * band_rows + steps_row) * width_tiles + steps_row % CT
    steps_link = jnp.arange(per_scen, dtype=jnp.int32)[None, None, :]
    link_cells = (col_pos * band_rows + steps_link % band_rows) * width_tiles + CT + scen_pos * per_scen + steps_link
    base_cells = jnp.concatenate([jnp.broadcast_to(row_cells, (SCEN, N_COL, band_rows)), jnp.broadcast_to(link_cells, (SCEN, N_COL, per_scen))], axis=2)
    base_cells = base_cells.reshape(SCEN * N_COL, band_rows + per_scen)
    device_keys = jax.random.split(key, SCEN * N_COL)

    def choose_cells(one_key, own_base):
        rank_order = jax.random.permutation(one_key, cell_count).astype(jnp.int32)
        marked = jnp.zeros((cell_count,), jnp.int32).at[own_base].set(1)
        scores = jnp.where(marked > 0, rank_order - cell_count, rank_order)
        chosen = jnp.argsort(scores, stable=True)[:NT]
        return jnp.sort(chosen).astype(jnp.int32)
    chosen = jax.vmap(choose_cells)(device_keys, base_cells).reshape(SCEN, N_COL, NT)
    return ((chosen // width_tiles).astype(jnp.int32), (chosen % width_tiles).astype(jnp.int32))


def draw_tile_rows(key, part):
    return tile_layout(key)[0]


def draw_tile_cols(key, part):
    return tile_layout(key)[1]


def draw_tile_values(key, part):
    key = jax.random.fold_in(key, 11)
    first, second, third, fourth = jax.random.split(key, 4)
    shape = (SCEN, N_COL, NT, TILE, TILE)
    magnitude = jnp.minimum(jnp.abs(jax.random.normal(first, shape, jnp.float32)), 4.0)
    top_scale = 10.0
    flips = jnp.where(jax.random.uniform(fourth, shape, jnp.float32) < 0.125, -1.0, 1.0)
    row_factor = jnp.exp(jax.random.uniform(second, (SCEN, N_COL, NT, TILE, 1), jnp.float32) * jnp.log(top_scale))
    col_factor = jnp.exp(jax.random.uniform(third, (SCEN, N_COL, NT, 1, TILE), jnp.float32) * jnp.log(top_scale))
    return flips * magnitude * row_factor * col_factor


def draw_cost_local(key, part):
    key = jax.random.fold_in(key, 21)
    shape = (SCEN, N_COL, CT, TILE)
    values = jnp.clip(jax.random.normal(key, shape, jnp.float32), -4.0, 4.0)
    return values * rising(SCEN)[:, None, None, None]


def draw_rhs(key, part):
    key = jax.random.fold_in(key, 31)
    shape = (SCEN, RT, TILE)
    values = jnp.clip(jax.random.normal(key, shape, jnp.float32), -4.0, 4.0)
    return values * rising(SCEN)[:, None, None]


def block_levels(key, shape, shards, smallest, largest):
    def one(axis_at, shards_of):
        steps = jax.random.uniform(jax.random.fold_in(jax.random.fold_in(key, 6), axis_at), (shards_of,), jnp.float32, smallest / len(shards), largest / len(shards))
        return jnp.repeat(jnp.exp(steps), shape[axis_at] // shards_of).reshape((-1,) + (1,) * (len(shape) - axis_at - 1))

    gain = one(*shards[0])
    for cut in shards[1:]:
        gain = gain * one(*cut)
    return gain


def scatter_about(rng, dims, spread, reach, cuts=(), kind=jnp.bfloat16):
    factor_of = block_levels(rng, dims, cuts, -0.22, 0.18) if cuts else 1.0
    drawn = jax.random.normal(rng, dims, jnp.float32) * spread * factor_of
    return jnp.minimum(jnp.maximum(drawn, -reach), reach).astype(kind)


def setup_inputs(seed: int = 0) -> dict:
    arg_keys = jax.random.split(jax.random.key(seed), 12)
    return {
        "tile_values": draw_tile_values(jax.random.fold_in(arg_keys[11], 71), 0),
        "tile_rows": draw_tile_rows(jax.random.fold_in(arg_keys[11], 71), 0),
        "tile_cols": draw_tile_cols(jax.random.fold_in(arg_keys[11], 71), 0),
        "cost_local": draw_cost_local(jax.random.fold_in(arg_keys[11], 71), 0),
        "cost_link": scatter_about(arg_keys[4], (N_COL, LT, TILE), 1.0, 5.0, ((0, 4),), jnp.float32),
        "bound_local": jnp.clip(jnp.exp(math.log(4.0) - 2.0794415 * jax.random.uniform(arg_keys[5], (SCEN, N_COL, CT, TILE), jnp.float32) ** block_levels(arg_keys[5], (SCEN, N_COL, CT, TILE), ((0, 32), (1, 4)), -0.2, 0.2)), 0.5, 4.0),
        "bound_link": jnp.clip(jnp.exp(math.log(4.0) - 2.0794415 * jax.random.uniform(arg_keys[6], (N_COL, LT, TILE), jnp.float32) ** block_levels(arg_keys[6], (N_COL, LT, TILE), ((0, 4),), -0.2, 0.2)), 0.5, 4.0),
        "rhs": draw_rhs(jax.random.fold_in(arg_keys[11], 71), 0),
        "start_local": jnp.clip(1.0 * jax.random.uniform(arg_keys[8], (SCEN, N_COL, CT, TILE), jnp.float32) ** block_levels(arg_keys[8], (SCEN, N_COL, CT, TILE), ((0, 32), (1, 4)), -0.2, 0.2), 0.0, 1.0),
        "start_link": jnp.clip(1.0 * jax.random.uniform(arg_keys[9], (N_COL, LT, TILE), jnp.float32) ** block_levels(arg_keys[9], (N_COL, LT, TILE), ((0, 4),), -0.2, 0.2), 0.0, 1.0),
        "start_dual": scatter_about(arg_keys[10], (SCEN, RT, TILE), 1.0, 5.0, ((0, 32), (1, 4)), jnp.float32),
    }


EPS = 1e-06
STEP = 0.9
HIGH = lax.Precision.HIGHEST

def indicator_tables(row_ids, col_ids):
    row_table = (jnp.arange(RT, dtype=jnp.int32)[:, None] == row_ids[None, :]).astype(jnp.float32)
    col_table = (jnp.arange(CT + LT, dtype=jnp.int32)[:, None] == col_ids[None, :]).astype(jnp.float32)
    return (row_table, col_table)

def block_stats(blocks, row_table, col_table, row_factor, col_factor, use_max):
    magnitude = jnp.abs(blocks) * row_factor[:, :, None] * col_factor[:, None, :]
    if use_max:
        row_part = lax.optimization_barrier(jnp.max(magnitude, axis=2))
        col_part = lax.optimization_barrier(jnp.max(magnitude, axis=1))
        row_stat = lax.optimization_barrier(jnp.max(jnp.where(row_table[:, :, None] > 0, row_part[None], 0.0), axis=1))
        col_stat = lax.optimization_barrier(jnp.max(jnp.where(col_table[:, :, None] > 0, col_part[None], 0.0), axis=1))
    else:
        row_stat = jnp.dot(row_table, lax.optimization_barrier(jnp.sum(magnitude, axis=2)), precision=HIGH)
        col_stat = jnp.dot(col_table, lax.optimization_barrier(jnp.sum(magnitude, axis=1)), precision=HIGH)
    return (row_stat, col_stat)

def apply_forward(blocks, row_table, col_ids, col_factor, values):
    picked = jnp.take(col_factor * values, col_ids, axis=0)
    product = jnp.einsum('nab,nb->na', blocks, picked, precision=HIGH)
    return jnp.dot(row_table, product, precision=HIGH)

def apply_backward(blocks, col_table, row_ids, row_factor, values):
    picked = jnp.take(row_factor * values, row_ids, axis=0)
    product = jnp.einsum('nab,na->nb', blocks, picked, precision=HIGH)
    return jnp.dot(col_table, product, precision=HIGH)

def reference(tile_values, tile_rows, tile_cols, cost_local, cost_link, bound_local, bound_link, rhs, start_local, start_link, start_dual):
    scen_count = tile_values.shape[0]
    scen_ids = jnp.arange(scen_count, dtype=jnp.int32)
    row_scale = jnp.ones(rhs.shape, jnp.float32)
    local_scale = jnp.ones(cost_local.shape, jnp.float32)
    link_scale = jnp.ones(cost_link.shape, jnp.float32)
    for sweep_index in range(3):
        use_max = sweep_index < 2

        def scenario_stats(scen_index):
            col_blocks = jnp.concatenate([local_scale[scen_index], link_scale], axis=1)
            scen_rows = row_scale[scen_index]

            def one_block(tile_block, row_block, col_block, scale_block):
                row_table, col_table = indicator_tables(row_block, col_block)
                return block_stats(tile_block, row_table, col_table, jnp.take(scen_rows, row_block, axis=0), jnp.take(scale_block, col_block, axis=0), use_max)
            return jax.vmap(one_block)(tile_values[scen_index], tile_rows[scen_index], tile_cols[scen_index], col_blocks)
        row_parts, col_parts = lax.map(scenario_stats, scen_ids)
        if use_max:
            row_stat = lax.optimization_barrier(jnp.max(row_parts, axis=1))
            link_stat = lax.optimization_barrier(jnp.max(col_parts[:, :, CT:], axis=0))
        else:
            row_stat = lax.optimization_barrier(jnp.sum(row_parts, axis=1))
            link_stat = lax.optimization_barrier(jnp.sum(col_parts[:, :, CT:], axis=0))
        row_scale = row_scale / jnp.sqrt(row_stat + EPS)
        local_scale = local_scale / jnp.sqrt(col_parts[:, :, :CT] + EPS)
        link_scale = link_scale / jnp.sqrt(link_stat + EPS)
    cost_loc = local_scale * cost_local
    cost_lnk = link_scale * cost_link
    upper_loc = bound_local / local_scale
    upper_lnk = bound_link / link_scale
    rhs_scaled = row_scale * rhs
    primal_loc = start_local / local_scale
    primal_lnk = start_link / link_scale
    dual_scaled = start_dual / row_scale
    cost_square = jnp.sum(cost_loc * cost_loc) + jnp.sum(cost_lnk * cost_lnk)
    rhs_square = jnp.sum(rhs_scaled * rhs_scaled)
    weight_ratio = jnp.sqrt((cost_square + EPS) / (rhs_square + EPS))
    primal_step = STEP / weight_ratio
    dual_step = STEP * weight_ratio
    for step_index in range(ITERS):

        def scenario_backward(scen_index):
            scen_rows = row_scale[scen_index]
            scen_dual = dual_scaled[scen_index]

            def one_block(tile_block, row_block, col_block):
                row_table, col_table = indicator_tables(row_block, col_block)
                return apply_backward(tile_block, col_table, row_block, scen_rows, scen_dual)
            return jax.vmap(one_block)(tile_values[scen_index], tile_rows[scen_index], tile_cols[scen_index])
        backward_sums = lax.map(scenario_backward, scen_ids)
        grad_loc = local_scale * backward_sums[:, :, :CT]
        grad_lnk = link_scale * lax.optimization_barrier(jnp.sum(backward_sums[:, :, CT:], axis=0))
        fresh_loc = jnp.clip(primal_loc - primal_step * (cost_loc - grad_loc), 0.0, upper_loc)
        fresh_lnk = jnp.clip(primal_lnk - primal_step * (cost_lnk - grad_lnk), 0.0, upper_lnk)
        bar_loc = 2.0 * fresh_loc - primal_loc
        bar_lnk = 2.0 * fresh_lnk - primal_lnk

        def scenario_forward(scen_index):
            col_blocks = jnp.concatenate([local_scale[scen_index], link_scale], axis=1)
            bar_blocks = jnp.concatenate([bar_loc[scen_index], bar_lnk], axis=1)

            def one_block(tile_block, row_block, col_block, scale_block, bar_block):
                row_table, col_table = indicator_tables(row_block, col_block)
                return apply_forward(tile_block, row_table, col_block, scale_block, bar_block)
            parts = jax.vmap(one_block)(tile_values[scen_index], tile_rows[scen_index], tile_cols[scen_index], col_blocks, bar_blocks)
            return lax.optimization_barrier(jnp.sum(parts, axis=0))
        forward_sums = lax.map(scenario_forward, scen_ids)
        dual_scaled = dual_scaled + dual_step * (rhs_scaled - row_scale * forward_sums)
        primal_loc = fresh_loc
        primal_lnk = fresh_lnk
    return (local_scale * primal_loc, link_scale * primal_lnk, row_scale * dual_scaled)
```

```python
import functools

import jax
import jax.numpy as jnp
from jax import lax
from jax.experimental import pallas as pl
from jax.experimental.pallas import tpu as pltpu
from jax.sharding import PartitionSpec as P

TILE = 256
RT = 128
CT = 8
LT = 256
ITERS = 3
NT = 64
HALF = LT // 2
CW = CT + LT
GROUP = 8
STEPS = NT // GROUP

EPS = 1e-06
STEP = 0.9
F32 = jnp.float32
LANES = 128


def swap_core(x):
    return lax.ppermute(x, "scen", [(i, i ^ 1) for i in range(32)])


def swap_z(x, k):
    return lax.ppermute(x, "scen", [(i, i ^ (k << 1)) for i in range(32)])


def swap_x(x, k):
    return lax.ppermute(x, "scen", [(i, i ^ (k << 3)) for i in range(32)])


def swap_y(x, k):
    return lax.ppermute(x, "col", [(i, i ^ k) for i in range(4)])


def tree(op, own, got):
    return op(op(own, got[0]), op(got[1], got[2]))


def row_pass(tiles_ref, t, col, row, colf_ref, rowout_ref, op, magnitude):
    for h in range(2):
        a = tiles_ref[t, h * LANES : (h + 1) * LANES, 0:LANES]
        b = tiles_ref[t, h * LANES : (h + 1) * LANES, LANES:TILE]
        if magnitude:
            a, b = jnp.abs(a), jnp.abs(b)
        if colf_ref is not None:
            a = a * colf_ref[0, pl.ds(col, 1), :]
            b = b * colf_ref[1, pl.ds(col, 1), :]
        m = op(a, b).T
        s = jnp.max(m, axis=0, keepdims=True) if op is jnp.maximum else jnp.sum(m, axis=0, keepdims=True)
        at = (h, pl.ds(row, 1), slice(None))
        rowout_ref[at] = op(rowout_ref[at], s)


def col_pass(tiles_ref, t, col, row, rowf_ref, colout_ref, op, magnitude):
    parts = [None, None]
    for h in range(2):
        if rowf_ref is not None:
            f = jnp.broadcast_to(rowf_ref[h, pl.ds(row, 1), :], (LANES, LANES)).T
        for w in range(2):
            a = tiles_ref[t, h * LANES : (h + 1) * LANES, w * LANES : (w + 1) * LANES]
            if magnitude:
                a = jnp.abs(a)
            if rowf_ref is not None:
                a = a * f
            a = a.reshape(16, 8, LANES)
            s = jnp.max(a, axis=0) if op is jnp.maximum else jnp.sum(a, axis=0)
            parts[w] = s if parts[w] is None else op(parts[w], s)
    for w in range(2):
        s = parts[w]
        s = jnp.max(s, axis=0, keepdims=True) if op is jnp.maximum else jnp.sum(s, axis=0, keepdims=True)
        at = (w, pl.ds(col, 1), slice(None))
        colout_ref[at] = op(colout_ref[at], s)


def split_to(ref, value, lo=0):
    for w in range(2):
        ref[w, lo : lo + value.shape[0], :] = value[:, w * LANES : (w + 1) * LANES]


def join_from(ref, out):
    for w in range(2):
        out[:, w * LANES : (w + 1) * LANES] = ref[w]


ROWS = pltpu.VMEM((2, RT, LANES), F32)
COLS = pltpu.VMEM((2, CW, LANES), F32)


def tile_call(kernel, ids, tiles, operands, outs, scratch=()):
    def spec(x):
        if x.shape[0] == 1:
            return pl.BlockSpec(memory_space=pltpu.SMEM)
        return pl.BlockSpec(x.shape, lambda i, *_: (0,) * len(x.shape))

    return pl.pallas_call(
        kernel,
        out_shape=tuple(jax.ShapeDtypeStruct(s, F32) for s in outs),
        grid_spec=pltpu.PrefetchScalarGridSpec(
            num_scalar_prefetch=2,
            grid=(STEPS,),
            in_specs=[pl.BlockSpec((GROUP, TILE, TILE), lambda i, *_: (i, 0, 0))]
            + [spec(x) for x in operands],
            out_specs=tuple(pl.BlockSpec(s, lambda i, *_: (0, 0)) for s in outs),
            scratch_shapes=list(scratch),
        ),
        compiler_params=pltpu.CompilerParams(vmem_limit_bytes=40 * 1024 * 1024),
    )(*ids, tiles, *operands)


def each_tile(rows_ref, cols_ref, visit):
    base = pl.program_id(0) * GROUP
    for t in range(GROUP):
        visit(t, cols_ref[base + t], rows_ref[base + t])


def at_first(fn):
    pl.when(pl.program_id(0) == 0)(fn)


def at_last(fn):
    pl.when(pl.program_id(0) == STEPS - 1)(fn)


def first_stats_kernel(rows_ref, cols_ref, tiles_ref, rowout, colout, racc, cacc):
    @at_first
    def _():
        racc[...] = jnp.zeros_like(racc)
        cacc[...] = jnp.zeros_like(cacc)

    def visit(t, col, row):
        row_pass(tiles_ref, t, col, row, None, racc, jnp.maximum, True)
        col_pass(tiles_ref, t, col, row, None, cacc, jnp.maximum, True)

    each_tile(rows_ref, cols_ref, visit)

    @at_last
    def _():
        join_from(racc, rowout)
        join_from(cacc, colout)


def next_stats_kernel(
    op, first, rows_ref, cols_ref, tiles_ref, r0, r1, r2, r3, loc, mine, other, *rest
):
    if first:
        rowout, colout, rownew, colnew, racc, cacc, rowf, colf = rest
    else:
        rowold, colold, rowout, colout, rownew, colnew, racc, cacc, rowf, colf = rest

    @at_first
    def _():
        row = tree(jnp.maximum, r0[...], (r1[...], r2[...], r3[...]))
        if first:
            new = 1.0 / jnp.sqrt(row + EPS)
        else:
            old = rowold[...]
            new = old / jnp.sqrt(old * row + EPS)
        rownew[...] = new
        split_to(rowf, new)
        for lo, hi, src in ((0, CT, loc), (CT, CT + HALF, mine), (CT + HALF, CW, other)):
            stat = src[0 : hi - lo]
            if first:
                new = 1.0 / jnp.sqrt(stat + EPS)
            else:
                old = colold[lo:hi]
                new = old / jnp.sqrt(old * stat + EPS)
            colnew[lo:hi] = new
            split_to(colf, new, lo)
        racc[...] = jnp.zeros_like(racc)
        cacc[...] = jnp.zeros_like(cacc)

    def visit(t, col, row):
        row_pass(tiles_ref, t, col, row, colf, racc, op, True)
        col_pass(tiles_ref, t, col, row, rowf, cacc, op, True)

    each_tile(rows_ref, cols_ref, visit)

    @at_last
    def _():
        join_from(racc, rowout)
        join_from(cacc, colout)


def first_backward_kernel(rows_ref, cols_ref, tiles_ref, dual, colout, cacc, work):
    @at_first
    def _():
        split_to(work, dual[...])
        cacc[...] = jnp.zeros_like(cacc)

    def visit(t, col, row):
        col_pass(tiles_ref, t, col, row, work, cacc, jnp.add, False)

    each_tile(rows_ref, cols_ref, visit)

    @at_last
    def _():
        join_from(cacc, colout)


def backward_kernel(
    rows_ref, cols_ref, tiles_ref, scalars, r0, r1, r2, r3, dual, rhs, rowf, colout, dualnew, cacc, work
):
    @at_first
    def _():
        total = tree(jnp.add, r0[...], (r1[...], r2[...], r3[...]))
        new = dual[...] + scalars[0, 1] * (rhs[...] - rowf[...] * total)
        dualnew[...] = new
        split_to(work, rowf[...] * new)
        cacc[...] = jnp.zeros_like(cacc)

    def visit(t, col, row):
        col_pass(tiles_ref, t, col, row, work, cacc, jnp.add, False)

    each_tile(rows_ref, cols_ref, visit)

    @at_last
    def _():
        join_from(cacc, colout)


def forward_kernel(
    rows_ref, cols_ref, tiles_ref, scalars, loc, mine, other, primal, cost, upper, colf, rowout, fresh, racc, work
):
    @at_first
    def _():
        for lo, hi, src in ((0, CT, loc), (CT, CT + HALF, mine), (CT + HALF, CW, other)):
            at = slice(lo, hi)
            x, scale = primal[at], colf[at]
            grad = scale * src[0 : hi - lo]
            new = jnp.clip(x - scalars[0, 0] * (cost[at] - grad), 0.0, upper[at])
            fresh[at] = new
            split_to(work, scale * (2.0 * new - x), lo)
        racc[...] = jnp.zeros_like(racc)

    def visit(t, col, row):
        row_pass(tiles_ref, t, col, row, work, racc, jnp.add, False)

    each_tile(rows_ref, cols_ref, visit)

    @at_last
    def _():
        join_from(racc, rowout)


def body(
    tile_values,
    tile_rows,
    tile_cols,
    cost_local,
    cost_link,
    bound_local,
    bound_link,
    rhs,
    start_local,
    start_link,
    start_dual,
):
    tiles = tile_values[0, 0]
    scen = lax.axis_index("scen")
    y_at = lax.axis_index("col")
    x_at = scen // 8
    core = scen % 2
    share = RT // 4
    chunk = HALF // 4

    raw_cols = tile_cols[0, 0]
    turned = CT + ((raw_cols - CT) ^ (core * HALF))
    ids = (tile_rows[0, 0], jnp.where(raw_cols < CT, raw_cols, turned))

    def turn(x):
        return jnp.where(core == 0, x, jnp.concatenate([x[HALF:], x[:HALF]], axis=0))

    def whole_columns(local, link):
        return jnp.concatenate([local[0, 0], turn(link[0])], axis=0)

    def halves(x):
        return x[CT : CT + HALF], x[CT + HALF :]

    pair = jnp.concatenate([rhs[0], start_dual[0]], axis=0)
    parts = jnp.stack([pair] + [swap_y(pair, k) for k in (1, 2, 3)])
    parts = jnp.take(parts, y_at ^ jnp.arange(4), axis=0)
    rhs_rows = parts[:, :share].reshape(RT, TILE)
    dual_rows = parts[:, share:].reshape(RT, TILE)

    row_part, col_part = tile_call(
        first_stats_kernel, ids, tiles, (), ((RT, TILE), (CW, TILE)), (ROWS, COLS)
    )
    mine, other = halves(col_part)
    rows_got = [swap_y(row_part, k) for k in (1, 2, 3)]
    link = jnp.maximum(mine, swap_core(other))
    link = tree(jnp.maximum, link, [swap_x(link, k) for k in (1, 2, 3)])
    link = tree(jnp.maximum, link, [swap_z(link, k) for k in (1, 2, 3)])
    (grad0,) = tile_call(first_backward_kernel, ids, tiles, (dual_rows,), ((CW, TILE),), (COLS, ROWS))
    grad_mine, grad_other = halves(grad0)
    grad_half = grad_mine + swap_core(grad_other)

    def scales(row_total, loc, mine, other, row_old, col_old):
        row = row_old / jnp.sqrt(row_old * row_total + EPS)
        stat = jnp.concatenate([loc, mine, other], axis=0)
        return row, col_old / jnp.sqrt(col_old * stat + EPS)

    operands = (row_part, *rows_got, col_part, link, swap_core(link))
    row_part, col_part, row_scale, col_scale = tile_call(
        functools.partial(next_stats_kernel, jnp.maximum, True),
        ids,
        tiles,
        operands,
        ((RT, TILE), (CW, TILE), (RT, TILE), (CW, TILE)),
        (ROWS, COLS, ROWS, COLS),
    )
    mine, other = halves(col_part)
    rows_got = [swap_y(row_part, k) for k in (1, 2, 3)]
    link = jnp.maximum(mine, swap_core(other))
    got = [
        swap_x(
            jnp.concatenate(
                [link, lax.dynamic_slice_in_dim(grad_half, (x_at ^ k) * chunk, chunk, 0)], axis=0
            ),
            k,
        )
        for k in (1, 2, 3)
    ]
    link = tree(jnp.maximum, link, [g[:HALF] for g in got])
    grad_chunk = tree(
        jnp.add,
        lax.dynamic_slice_in_dim(grad_half, x_at * chunk, chunk, 0),
        [g[HALF:] for g in got],
    )
    both = jnp.concatenate([link, grad_chunk], axis=0)
    got = [swap_z(both, k) for k in (1, 2, 3)]
    link = tree(jnp.maximum, link, [g[:HALF] for g in got])
    grad_chunk = tree(jnp.add, grad_chunk, [g[HALF:] for g in got])

    operands = (row_part, *rows_got, col_part, link, swap_core(link), row_scale, col_scale)
    row_part, col_part, row_scale, col_scale = tile_call(
        functools.partial(next_stats_kernel, jnp.add, False),
        ids,
        tiles,
        operands,
        ((RT, TILE), (CW, TILE), (RT, TILE), (CW, TILE)),
        (ROWS, COLS, ROWS, COLS),
    )
    mine, other = halves(col_part)
    rows_got = [swap_y(row_part, k) for k in (1, 2, 3)]
    link = mine + swap_core(other)
    both = jnp.concatenate([link, grad_chunk], axis=0)
    got = [swap_x(both, k) for k in (1, 2, 3)]
    link = tree(jnp.add, link, [g[:HALF] for g in got])
    parts = jnp.stack([grad_chunk] + [g[HALF:] for g in got])
    grad_half = jnp.take(parts, x_at ^ jnp.arange(4), axis=0).reshape(HALF, TILE)
    row_total = tree(jnp.add, row_part, rows_got)
    row_scale = row_scale / jnp.sqrt(row_scale * row_total + EPS)
    rhs_scaled = row_scale * rhs_rows
    dual_scaled = dual_rows / row_scale
    rhs_square = jnp.sum((rhs_scaled * rhs_scaled).reshape(16, 8, TILE), axis=0)
    local_old = col_scale[:CT]
    cost_loc = local_old / jnp.sqrt(local_old * col_part[:CT] + EPS) * cost_local[0, 0]
    squares = jnp.concatenate([rhs_square, cost_loc * cost_loc], axis=0)
    both = jnp.concatenate([link, squares], axis=0)
    got = [swap_z(both, k) for k in (1, 2, 3)]
    both = tree(jnp.add, both, got)
    back = swap_core(jnp.concatenate([both, grad_half], axis=0))
    squares = both[HALF:] + back[HALF : HALF + 2 * CT]
    stat = jnp.concatenate([col_part[:CT], both[:HALF], back[:HALF]], axis=0)
    col_scale = col_scale / jnp.sqrt(col_scale * stat + EPS)
    grads = (grad0, grad_half, back[HALF + 2 * CT :])
    cost = col_scale * whole_columns(cost_local, cost_link)
    upper = whole_columns(bound_local, bound_link) / col_scale
    primal = whole_columns(start_local, start_link) / col_scale

    link_square = jnp.sum((cost[CT:] * cost[CT:]).reshape(LT // 8, 8, TILE), axis=0)
    by_x = tree(jnp.add, squares, [swap_x(squares, k) for k in (1, 2, 3)])
    cost_part = by_x[CT:] + link_square
    cost_total = tree(jnp.add, cost_part, [swap_y(cost_part, k) for k in (1, 2, 3)])
    weight_ratio = jnp.sqrt((jnp.sum(cost_total) + EPS) / (jnp.sum(by_x[:CT]) + EPS))
    steps = jnp.stack([STEP / weight_ratio, STEP * weight_ratio])[None]

    for index in range(ITERS):
        row_part, primal = tile_call(
            forward_kernel,
            ids,
            tiles,
            (steps, *grads, primal, cost, upper, col_scale),
            ((RT, TILE), (CW, TILE)),
            (ROWS, COLS),
        )
        if index == ITERS - 1:
            break
        rows_got = [swap_y(row_part, k) for k in (1, 2, 3)]
        col_part, dual_scaled = tile_call(
            backward_kernel,
            ids,
            tiles,
            (steps, row_part, *rows_got, dual_scaled, rhs_scaled, row_scale),
            ((CW, TILE), (RT, TILE)),
            (COLS, ROWS),
        )
        mine, other = halves(col_part)
        link = mine + swap_core(other)
        link = tree(jnp.add, link, [swap_x(link, k) for k in (1, 2, 3)])
        link = tree(jnp.add, link, [swap_z(link, k) for k in (1, 2, 3)])
        grads = (col_part, link, swap_core(link))

    def piece(x, k):
        return lax.dynamic_slice_in_dim(x, (y_at ^ k) * share, share, 0)

    total = tree(jnp.add, piece(row_part, 0), [swap_y(piece(row_part, k), k) for k in (1, 2, 3)])
    scale = piece(row_scale, 0)
    dual = piece(dual_scaled, 0) + steps[0, 1] * (piece(rhs_scaled, 0) - scale * total)
    solved = col_scale * primal
    return (
        solved[:CT][None, None],
        turn(solved[CT:])[None],
        (scale * dual)[None],
    )


def solution(mesh):
    placed = (
        P("scen", "col", None, None, None),
        P("scen", "col", None),
        P("scen", "col", None),
        P("scen", "col", None, None),
        P("col", None, None),
        P("scen", "col", None, None),
        P("col", None, None),
        P("scen", "col", None),
        P("scen", "col", None, None),
        P("col", None, None),
        P("scen", "col", None),
    )
    return jax.shard_map(
        body,
        mesh=mesh,
        in_specs=placed,
        out_specs=(P("scen", "col", None, None), P("col", None, None), P("scen", "col", None)),
        check_vma=False,
    )
```

```python
import functools

import jax
import jax.numpy as jnp
from jax import lax
from jax.experimental import pallas as pl
from jax.experimental.pallas import tpu as pltpu
from jax.sharding import PartitionSpec as P

TILE = 256
RT = 128
CT = 8
LT = 256
ITERS = 3
NT = 64
HALF = LT // 2
SHARE = RT // 4
CW = CT + LT
GROUP = 8
STEPS = NT // GROUP

EPS = 1e-06
STEP = 0.9
F32 = jnp.float32
LANES = 128
VMEM_LIMIT = 24 * 1024 * 1024


def swap_core(x):
    return lax.ppermute(x, "scen", [(i, i ^ 1) for i in range(32)])


def swap_z(x, k):
    return lax.ppermute(x, "scen", [(i, i ^ (k << 1)) for i in range(32)])


def swap_x(x, k):
    return lax.ppermute(x, "scen", [(i, i ^ (k << 3)) for i in range(32)])


def swap_y(x, k):
    return lax.ppermute(x, "col", [(i, i ^ k) for i in range(4)])


def tree(op, own, got):
    return op(op(own, got[0]), op(got[1], got[2]))


def row_pass(tiles_ref, t, col, row, colf_ref, rowout_ref, op, magnitude):
    for h in range(2):
        a = tiles_ref[t, h * LANES : (h + 1) * LANES, 0:LANES]
        b = tiles_ref[t, h * LANES : (h + 1) * LANES, LANES:TILE]
        if magnitude:
            a, b = jnp.abs(a), jnp.abs(b)
        if colf_ref is not None:
            a = a * colf_ref[0, pl.ds(col, 1), :]
            b = b * colf_ref[1, pl.ds(col, 1), :]
        m = op(a, b).T
        s = jnp.max(m, axis=0, keepdims=True) if op is jnp.maximum else jnp.sum(m, axis=0, keepdims=True)
        at = (h, pl.ds(row, 1), slice(None))
        rowout_ref[at] = op(rowout_ref[at], s)


def col_pass(tiles_ref, t, col, row, rowf_ref, colout_ref, op, magnitude):
    parts = [None, None]
    for h in range(2):
        if rowf_ref is not None:
            f = jnp.broadcast_to(rowf_ref[h, pl.ds(row, 1), :], (LANES, LANES)).T
        for w in range(2):
            a = tiles_ref[t, h * LANES : (h + 1) * LANES, w * LANES : (w + 1) * LANES]
            if magnitude:
                a = jnp.abs(a)
            if rowf_ref is not None:
                a = a * f
            a = a.reshape(16, 8, LANES)
            s = jnp.max(a, axis=0) if op is jnp.maximum else jnp.sum(a, axis=0)
            parts[w] = s if parts[w] is None else op(parts[w], s)
    for w in range(2):
        s = parts[w]
        s = jnp.max(s, axis=0, keepdims=True) if op is jnp.maximum else jnp.sum(s, axis=0, keepdims=True)
        at = (w, pl.ds(col, 1), slice(None))
        colout_ref[at] = op(colout_ref[at], s)


def split_to(ref, value, lo=0):
    for w in range(2):
        ref[w, lo : lo + value.shape[0], :] = value[:, w * LANES : (w + 1) * LANES]


def join_from(ref, out):
    for w in range(2):
        out[0 : ref.shape[1], w * LANES : (w + 1) * LANES] = ref[w]


ROWS = pltpu.VMEM((2, RT, LANES), F32)
COLS = pltpu.VMEM((2, CW, LANES), F32)


def tile_call(kernel, ids, tiles, operands, outs, scratch=(), load=False):
    def spec(x):
        return pl.BlockSpec(memory_space=pltpu.SMEM if x.shape[0] == 1 else pltpu.VMEM)

    shapes = [jax.ShapeDtypeStruct(s, F32) for s in outs]
    where = pl.BlockSpec(memory_space=pltpu.VMEM)
    scratch = list(scratch)
    if load:
        where = pl.BlockSpec(memory_space=pl.ANY)
        shapes.append(pltpu.VMEM((NT, TILE, TILE), F32))
        scratch.append(pltpu.SemaphoreType.DMA((STEPS,)))
    else:
        tiles = pltpu.with_memory_space_constraint(tiles, pltpu.VMEM)
    ids_spec = pl.BlockSpec(memory_space=pltpu.SMEM)
    return pl.pallas_call(
        kernel,
        out_shape=tuple(shapes),
        in_specs=[ids_spec, ids_spec, where] + [spec(x) for x in operands],
        out_specs=tuple(pl.BlockSpec(memory_space=pltpu.VMEM) for _ in shapes),
        scratch_shapes=scratch,
        compiler_params=pltpu.CompilerParams(vmem_limit_bytes=VMEM_LIMIT),
    )(*ids, tiles, *operands)


def each_tile(rows_ref, cols_ref, visit, ready=None):
    def group(step, carry):
        if ready is not None:
            ready(step)
        for i in range(GROUP):
            t = step * GROUP + i
            visit(t, cols_ref[t], rows_ref[t])
        return carry

    lax.fori_loop(0, STEPS, group, 0)


def first_stats_kernel(
    rows_ref, cols_ref, source, rhs, dual, rowout, colout, tiles_ref, racc, cacc, sems
):
    def load(step):
        part = pl.ds(step * GROUP, GROUP)
        return pltpu.make_async_copy(source.at[part], tiles_ref.at[part], sems.at[step])

    for step in range(STEPS):
        load(step).start()
    racc[...] = jnp.zeros_like(racc)
    cacc[...] = jnp.zeros_like(cacc)

    def visit(t, col, row):
        row_pass(tiles_ref, t, col, row, None, racc, jnp.maximum, True)
        col_pass(tiles_ref, t, col, row, None, cacc, jnp.maximum, True)

    each_tile(rows_ref, cols_ref, visit, lambda step: load(step).wait())

    join_from(racc, rowout)
    rowout[RT : RT + SHARE] = rhs[...]
    rowout[RT + SHARE :] = dual[...]
    join_from(cacc, colout)


def next_stats_kernel(
    op, first, rows_ref, cols_ref, tiles_ref, r0, r1, r2, r3, loc, mine, other, *rest
):
    if first:
        rowout, colout, rownew, colnew, racc, cacc, rowf, colf = rest
    else:
        rowold, colold, rowout, colout, rownew, colnew, racc, cacc, rowf, colf = rest

    row = tree(jnp.maximum, r0[0:RT], (r1[0:RT], r2[0:RT], r3[0:RT]))
    if first:
        new = 1.0 / jnp.sqrt(row + EPS)
    else:
        old = rowold[...]
        new = old / jnp.sqrt(old * row + EPS)
    rownew[...] = new
    split_to(rowf, new)
    for lo, hi, src in ((0, CT, loc), (CT, CT + HALF, mine), (CT + HALF, CW, other)):
        stat = src[0 : hi - lo]
        if first:
            new = 1.0 / jnp.sqrt(stat + EPS)
        else:
            old = colold[lo:hi]
            new = old / jnp.sqrt(old * stat + EPS)
        colnew[lo:hi] = new
        split_to(colf, new, lo)
    racc[...] = jnp.zeros_like(racc)
    cacc[...] = jnp.zeros_like(cacc)

    def visit(t, col, row):
        row_pass(tiles_ref, t, col, row, colf, racc, op, True)
        col_pass(tiles_ref, t, col, row, rowf, cacc, op, True)

    each_tile(rows_ref, cols_ref, visit)

    join_from(racc, rowout)
    join_from(cacc, colout)


def first_backward_kernel(
    rows_ref, cols_ref, tiles_ref, y_at, r0, r1, r2, r3, colout, rhsout, dualout, cacc, work
):
    for k, ref in enumerate((r0, r1, r2, r3)):
        at = pl.ds(pl.multiple_of((y_at[0, 0] ^ k) * SHARE, SHARE), SHARE)
        rhsout[at, :] = ref[RT : RT + SHARE]
        dualout[at, :] = ref[RT + SHARE :]
    split_to(work, dualout[...])
    cacc[...] = jnp.zeros_like(cacc)

    def visit(t, col, row):
        col_pass(tiles_ref, t, col, row, work, cacc, jnp.add, False)

    each_tile(rows_ref, cols_ref, visit)

    join_from(cacc, colout)


def backward_kernel(
    rows_ref, cols_ref, tiles_ref, scalars, r0, r1, r2, r3, dual, rhs, rowf, colout, dualnew, cacc, work
):
    total = tree(jnp.add, r0[...], (r1[...], r2[...], r3[...]))
    new = dual[...] + scalars[0, 1] * (rhs[...] - rowf[...] * total)
    dualnew[...] = new
    split_to(work, rowf[...] * new)
    cacc[...] = jnp.zeros_like(cacc)

    def visit(t, col, row):
        col_pass(tiles_ref, t, col, row, work, cacc, jnp.add, False)

    each_tile(rows_ref, cols_ref, visit)

    join_from(cacc, colout)


def forward_kernel(
    rows_ref, cols_ref, tiles_ref, scalars, loc, mine, other, primal, cost, upper, colf, rowout, fresh, racc, work
):
    for lo, hi, src in ((0, CT, loc), (CT, CT + HALF, mine), (CT + HALF, CW, other)):
        at = slice(lo, hi)
        x, scale = primal[at], colf[at]
        grad = scale * src[0 : hi - lo]
        new = jnp.clip(x - scalars[0, 0] * (cost[at] - grad), 0.0, upper[at])
        fresh[at] = new
        split_to(work, scale * (2.0 * new - x), lo)
    racc[...] = jnp.zeros_like(racc)

    def visit(t, col, row):
        row_pass(tiles_ref, t, col, row, work, racc, jnp.add, False)

    each_tile(rows_ref, cols_ref, visit)

    join_from(racc, rowout)


def body(
    tile_values,
    tile_rows,
    tile_cols,
    cost_local,
    cost_link,
    bound_local,
    bound_link,
    rhs,
    start_local,
    start_link,
    start_dual,
):
    tiles = tile_values[0, 0]
    scen = lax.axis_index("scen")
    y_at = lax.axis_index("col")
    x_at = scen // 8
    core = scen % 2
    chunk = HALF // 4

    raw_cols = tile_cols[0, 0]
    turned = CT + ((raw_cols - CT) ^ (core * HALF))
    ids = (tile_rows[0, 0], jnp.where(raw_cols < CT, raw_cols, turned))

    def turn(x):
        return jnp.where(core == 0, x, jnp.concatenate([x[HALF:], x[:HALF]], axis=0))

    def whole_columns(local, link):
        return jnp.concatenate([local[0, 0], turn(link[0])], axis=0)

    def halves(x):
        return x[CT : CT + HALF], x[CT + HALF :]

    row_part, col_part, tiles = tile_call(
        first_stats_kernel,
        ids,
        tiles,
        (rhs[0], start_dual[0]),
        ((RT + 2 * SHARE, TILE), (CW, TILE)),
        (ROWS, COLS),
        load=True,
    )
    mine, other = halves(col_part)
    rows_got = [swap_y(row_part, k) for k in (1, 2, 3)]
    link = jnp.maximum(mine, swap_core(other))
    link = tree(jnp.maximum, link, [swap_x(link, k) for k in (1, 2, 3)])
    link = tree(jnp.maximum, link, [swap_z(link, k) for k in (1, 2, 3)])
    grad0, rhs_rows, dual_rows = tile_call(
        first_backward_kernel,
        ids,
        tiles,
        (y_at.reshape(1, 1), row_part, *rows_got),
        ((CW, TILE), (RT, TILE), (RT, TILE)),
        (COLS, ROWS),
    )
    grad_mine, grad_other = halves(grad0)
    grad_half = grad_mine + swap_core(grad_other)

    operands = (row_part, *rows_got, col_part, link, swap_core(link))
    row_part, col_part, row_scale, col_scale = tile_call(
        functools.partial(next_stats_kernel, jnp.maximum, True),
        ids,
        tiles,
        operands,
        ((RT, TILE), (CW, TILE), (RT, TILE), (CW, TILE)),
        (ROWS, COLS, ROWS, COLS),
    )
    mine, other = halves(col_part)
    rows_got = [swap_y(row_part, k) for k in (1, 2, 3)]
    link = jnp.maximum(mine, swap_core(other))
    got = [
        swap_x(
            jnp.concatenate(
                [link, lax.dynamic_slice_in_dim(grad_half, (x_at ^ k) * chunk, chunk, 0)], axis=0
            ),
            k,
        )
        for k in (1, 2, 3)
    ]
    link = tree(jnp.maximum, link, [g[:HALF] for g in got])
    grad_chunk = tree(
        jnp.add,
        lax.dynamic_slice_in_dim(grad_half, x_at * chunk, chunk, 0),
        [g[HALF:] for g in got],
    )
    both = jnp.concatenate([link, grad_chunk], axis=0)
    got = [swap_z(both, k) for k in (1, 2, 3)]
    link = tree(jnp.maximum, link, [g[:HALF] for g in got])
    grad_chunk = tree(jnp.add, grad_chunk, [g[HALF:] for g in got])

    operands = (row_part, *rows_got, col_part, link, swap_core(link), row_scale, col_scale)
    row_part, col_part, row_scale, col_scale = tile_call(
        functools.partial(next_stats_kernel, jnp.add, False),
        ids,
        tiles,
        operands,
        ((RT, TILE), (CW, TILE), (RT, TILE), (CW, TILE)),
        (ROWS, COLS, ROWS, COLS),
    )
    mine, other = halves(col_part)
    rows_got = [swap_y(row_part, k) for k in (1, 2, 3)]
    link = mine + swap_core(other)
    row_total = tree(jnp.add, row_part, rows_got)
    row_scale = row_scale / jnp.sqrt(row_scale * row_total + EPS)
    rhs_scaled = row_scale * rhs_rows
    dual_scaled = dual_rows / row_scale
    rhs_square = jnp.sum((rhs_scaled * rhs_scaled).reshape(RT // 8, 8, TILE), axis=0)
    local_old = col_scale[:CT]
    cost_loc = local_old / jnp.sqrt(local_old * col_part[:CT] + EPS) * cost_local[0, 0]
    both = jnp.concatenate([link, rhs_square, cost_loc * cost_loc], axis=0)
    got = [swap_x(jnp.concatenate([both, grad_chunk], axis=0), k) for k in (1, 2, 3)]
    parts = jnp.stack([grad_chunk] + [g[HALF + 2 * CT :] for g in got])
    grad_half = jnp.take(parts, x_at ^ jnp.arange(4), axis=0).reshape(HALF, TILE)
    both = tree(jnp.add, both, [g[: HALF + 2 * CT] for g in got])
    both = tree(jnp.add, both, [swap_z(both, k) for k in (1, 2, 3)])
    back = swap_core(jnp.concatenate([both, grad_half], axis=0))
    squares = both[HALF:] + back[HALF : HALF + 2 * CT]
    stat = jnp.concatenate([col_part[:CT], both[:HALF], back[:HALF]], axis=0)
    col_scale = col_scale / jnp.sqrt(col_scale * stat + EPS)
    grads = (grad0, grad_half, back[HALF + 2 * CT :])
    cost = col_scale * whole_columns(cost_local, cost_link)
    upper = whole_columns(bound_local, bound_link) / col_scale
    primal = whole_columns(start_local, start_link) / col_scale

    half_squares = [jnp.sum((c * c).reshape(HALF // 8, 8, TILE), axis=0) for c in halves(cost)]
    cost_part = squares[CT:] + (half_squares[0] + half_squares[1])
    cost_total = tree(jnp.add, cost_part, [swap_y(cost_part, k) for k in (1, 2, 3)])
    weight_ratio = jnp.sqrt((jnp.sum(cost_total) + EPS) / (jnp.sum(squares[:CT]) + EPS))
    steps = jnp.stack([STEP / weight_ratio, STEP * weight_ratio])[None]

    for index in range(ITERS):
        row_part, primal = tile_call(
            forward_kernel,
            ids,
            tiles,
            (steps, *grads, primal, cost, upper, col_scale),
            ((RT, TILE), (CW, TILE)),
            (ROWS, COLS),
        )
        if index == ITERS - 1:
            break
        rows_got = [swap_y(row_part, k) for k in (1, 2, 3)]
        col_part, dual_scaled = tile_call(
            backward_kernel,
            ids,
            tiles,
            (steps, row_part, *rows_got, dual_scaled, rhs_scaled, row_scale),
            ((CW, TILE), (RT, TILE)),
            (COLS, ROWS),
        )
        mine, other = halves(col_part)
        link = mine + swap_core(other)
        link = tree(jnp.add, link, [swap_x(link, k) for k in (1, 2, 3)])
        link = tree(jnp.add, link, [swap_z(link, k) for k in (1, 2, 3)])
        grads = (col_part, link, swap_core(link))

    def piece(x, k):
        return lax.dynamic_slice_in_dim(x, (y_at ^ k) * SHARE, SHARE, 0)

    total = tree(jnp.add, piece(row_part, 0), [swap_y(piece(row_part, k), k) for k in (1, 2, 3)])
    scale = piece(row_scale, 0)
    dual = piece(dual_scaled, 0) + steps[0, 1] * (piece(rhs_scaled, 0) - scale * total)
    solved = col_scale * primal
    return (
        solved[:CT][None, None],
        turn(solved[CT:])[None],
        (scale * dual)[None],
    )


def solution(mesh):
    placed = (
        P("scen", "col", None, None, None),
        P("scen", "col", None),
        P("scen", "col", None),
        P("scen", "col", None, None),
        P("col", None, None),
        P("scen", "col", None, None),
        P("col", None, None),
        P("scen", "col", None),
        P("scen", "col", None, None),
        P("col", None, None),
        P("scen", "col", None),
    )
    return jax.shard_map(
        body,
        mesh=mesh,
        in_specs=placed,
        out_specs=(P("scen", "col", None, None), P("col", None, None), P("scen", "col", None)),
        check_vma=False,
    )
```

```python
import functools

import jax
import jax.numpy as jnp
from jax import lax
from jax.experimental import pallas as pl
from jax.experimental.pallas import tpu as pltpu
from jax.sharding import PartitionSpec as P

TILE = 256
RT = 128
CT = 8
LT = 256
ITERS = 3
NT = 64
HALF = LT // 2
SHARE = RT // 4
CW = CT + LT
GROUP = 8
STEPS = NT // GROUP

EPS = 1e-06
STEP = 0.9
F32 = jnp.float32
LANES = 128
VMEM_LIMIT = 24 * 1024 * 1024


def swap_core(x):
    return lax.ppermute(x, "scen", [(i, i ^ 1) for i in range(32)])


def swap_z(x, k):
    return lax.ppermute(x, "scen", [(i, i ^ (k << 1)) for i in range(32)])


def swap_x(x, k):
    return lax.ppermute(x, "scen", [(i, i ^ (k << 3)) for i in range(32)])


def swap_y(x, k):
    return lax.ppermute(x, "col", [(i, i ^ k) for i in range(4)])


def tree(op, own, got):
    return op(op(own, got[0]), op(got[1], got[2]))


def row_pass(tiles_ref, t, col, row, colf_ref, rowout_ref, op, magnitude):
    for h in range(2):
        a = tiles_ref[t, h * LANES : (h + 1) * LANES, 0:LANES]
        b = tiles_ref[t, h * LANES : (h + 1) * LANES, LANES:TILE]
        if magnitude:
            a, b = jnp.abs(a), jnp.abs(b)
        if colf_ref is not None:
            a = a * colf_ref[0, pl.ds(col, 1), :]
            b = b * colf_ref[1, pl.ds(col, 1), :]
        m = op(a, b).T
        s = jnp.max(m, axis=0, keepdims=True) if op is jnp.maximum else jnp.sum(m, axis=0, keepdims=True)
        at = (h, pl.ds(row, 1), slice(None))
        rowout_ref[at] = op(rowout_ref[at], s)


def col_pass(tiles_ref, t, col, row, rowf_ref, colout_ref, op, magnitude):
    parts = [None, None]
    for h in range(2):
        if rowf_ref is not None:
            f = jnp.broadcast_to(rowf_ref[h, pl.ds(row, 1), :], (LANES, LANES)).T
        for w in range(2):
            a = tiles_ref[t, h * LANES : (h + 1) * LANES, w * LANES : (w + 1) * LANES]
            if magnitude:
                a = jnp.abs(a)
            if rowf_ref is not None:
                a = a * f
            a = a.reshape(16, 8, LANES)
            s = jnp.max(a, axis=0) if op is jnp.maximum else jnp.sum(a, axis=0)
            parts[w] = s if parts[w] is None else op(parts[w], s)
    for w in range(2):
        s = parts[w]
        s = jnp.max(s, axis=0, keepdims=True) if op is jnp.maximum else jnp.sum(s, axis=0, keepdims=True)
        at = (w, pl.ds(col, 1), slice(None))
        colout_ref[at] = op(colout_ref[at], s)


def split_to(ref, value, lo=0):
    for w in range(2):
        ref[w, lo : lo + value.shape[0], :] = value[:, w * LANES : (w + 1) * LANES]


def join_from(ref, out, lo, hi):
    for w in range(2):
        out[0 : hi - lo, w * LANES : (w + 1) * LANES] = ref[w, lo:hi, :]


ROWS = pltpu.VMEM((2, RT, LANES), F32)
COLS = pltpu.VMEM((2, CW, LANES), F32)
OWN = CT + HALF
EIGHT = 2 * CT
CHUNK = HALF // 4


def call(kernel, smem, tiles, operands, outs, scratch=()):
    operands = [pltpu.with_memory_space_constraint(tiles, pltpu.VMEM)] + list(operands)
    vmem = pl.BlockSpec(memory_space=pltpu.VMEM)
    return pl.pallas_call(
        kernel,
        out_shape=tuple(jax.ShapeDtypeStruct((n, TILE), F32) for n in outs),
        in_specs=[pl.BlockSpec(memory_space=pltpu.SMEM) for _ in smem] + [vmem for _ in operands],
        out_specs=tuple(vmem for _ in outs),
        scratch_shapes=list(scratch),
        compiler_params=pltpu.CompilerParams(vmem_limit_bytes=VMEM_LIMIT),
    )(*smem, *operands)


def each_tile(rows_ref, cols_ref, place_ref, visit, ready=None):
    turn = place_ref[0] * HALF

    def group(step, carry):
        if ready is not None:
            ready(step)
        for i in range(GROUP):
            t = step * GROUP + i
            col = cols_ref[t]
            col = jnp.where(col < CT, col, CT + ((col - CT) ^ turn))
            visit(t, col, rows_ref[t])
        return carry

    lax.fori_loop(0, STEPS, group, 0)


def put_columns(cacc, colown, colother):
    join_from(cacc, colown, 0, OWN)
    join_from(cacc, colother, OWN, CW)


def first_stats_kernel(
    rows_ref, cols_ref, place, source, rhs, dual, rowout, colown, colother, tiles_ref, racc, cacc, sems
):
    def load(step):
        part = pl.ds(step * GROUP, GROUP)
        return pltpu.make_async_copy(source.at[part], tiles_ref.at[part], sems.at[step])

    for step in range(STEPS):
        load(step).start()
    extra = [
        pltpu.make_async_copy(src, rowout.at[pl.ds(RT + i * SHARE, SHARE)], sems.at[STEPS + i])
        for i, src in enumerate((rhs, dual))
    ]
    for copy in extra:
        copy.start()
    racc[...] = jnp.zeros_like(racc)
    cacc[...] = jnp.zeros_like(cacc)

    def visit(t, col, row):
        row_pass(tiles_ref, t, col, row, None, racc, jnp.maximum, True)
        col_pass(tiles_ref, t, col, row, None, cacc, jnp.maximum, True)

    each_tile(rows_ref, cols_ref, place, visit, lambda step: load(step).wait())
    join_from(racc, rowout, 0, RT)
    put_columns(cacc, colown, colother)
    for copy in extra:
        copy.wait()


def first_stats(ids, source, rhs, dual):
    vmem = pl.BlockSpec(memory_space=pltpu.VMEM)
    shapes = [jax.ShapeDtypeStruct((n, TILE), F32) for n in (RT + 2 * SHARE, OWN, HALF)]
    return pl.pallas_call(
        first_stats_kernel,
        out_shape=(*shapes, pltpu.VMEM((NT, TILE, TILE), F32)),
        in_specs=[pl.BlockSpec(memory_space=pltpu.SMEM)] * 3 + [pl.BlockSpec(memory_space=pl.ANY)] * 3,
        out_specs=(vmem,) * 4,
        scratch_shapes=[ROWS, COLS, pltpu.SemaphoreType.DMA((STEPS + 2,))],
        compiler_params=pltpu.CompilerParams(vmem_limit_bytes=VMEM_LIMIT),
    )(*ids, source, rhs, dual)


def next_stats_kernel(
    op, first, rows_ref, cols_ref, place, tiles_ref, r0, r1, r2, r3, loc, mine, other, *rest
):
    if first:
        rowout, colown, colother, rownew, colnew, racc, cacc, rowf, colf = rest
    else:
        rowold, colold, rowout, colown, colother, rownew, colnew, racc, cacc, rowf, colf = rest
    row = tree(jnp.maximum, r0[0:RT], (r1[0:RT], r2[0:RT], r3[0:RT]))
    if first:
        new = 1.0 / jnp.sqrt(row + EPS)
    else:
        old = rowold[...]
        new = old / jnp.sqrt(old * row + EPS)
    rownew[...] = new
    split_to(rowf, new)
    for lo, hi, src in ((0, CT, loc), (CT, OWN, mine), (OWN, CW, other)):
        stat = src[0 : hi - lo]
        if first:
            new = 1.0 / jnp.sqrt(stat + EPS)
        else:
            old = colold[lo:hi]
            new = old / jnp.sqrt(old * stat + EPS)
        colnew[lo:hi] = new
        split_to(colf, new, lo)
    racc[...] = jnp.zeros_like(racc)
    cacc[...] = jnp.zeros_like(cacc)

    def visit(t, col, row):
        row_pass(tiles_ref, t, col, row, colf, racc, op, True)
        col_pass(tiles_ref, t, col, row, rowf, cacc, op, True)

    each_tile(rows_ref, cols_ref, place, visit)
    join_from(racc, rowout, 0, RT)
    put_columns(cacc, colown, colother)


def first_backward_kernel(
    rows_ref, cols_ref, place, tiles_ref, r0, r1, r2, r3, colown, colother, rhsout, dualout, cacc, work
):
    for k, ref in enumerate((r0, r1, r2, r3)):
        at = pl.ds(pl.multiple_of((place[2] ^ k) * SHARE, SHARE), SHARE)
        rhsout[at, :] = ref[RT : RT + SHARE]
        dualout[at, :] = ref[RT + SHARE :]
    split_to(work, dualout[...])
    cacc[...] = jnp.zeros_like(cacc)

    def visit(t, col, row):
        col_pass(tiles_ref, t, col, row, work, cacc, jnp.add, False)

    each_tile(rows_ref, cols_ref, place, visit)
    put_columns(cacc, colown, colother)


def backward_kernel(
    rows_ref, cols_ref, place, tiles_ref, steps, r0, r1, r2, r3, dual, rhs, rowf, colown, colother, dualnew,
    cacc, work,
):
    total = tree(jnp.add, r0[...], (r1[...], r2[...], r3[...]))
    new = dual[...] + steps[1:2] * (rhs[...] - rowf[...] * total)
    dualnew[...] = new
    split_to(work, rowf[...] * new)
    cacc[...] = jnp.zeros_like(cacc)

    def visit(t, col, row):
        col_pass(tiles_ref, t, col, row, work, cacc, jnp.add, False)

    each_tile(rows_ref, cols_ref, place, visit)
    put_columns(cacc, colown, colother)


def forward_kernel(index, grad_at, rows_ref, cols_ref, place, tiles_ref, *rest):
    if index == 0:
        c0, c1, c2, c3, rhs_square, *rest = rest
    else:
        steps, *rest = rest
    loc, mine, other, primal, cost, upper, colf, *rest = rest
    if index == 0:
        steps, *rest = rest
        total = tree(jnp.add, c0[...], (c1[...], c2[...], c3[...]))
        cost_sum = jnp.sum(total, axis=(0, 1), keepdims=True)
        rhs_sum = jnp.sum(rhs_square[...], axis=(0, 1), keepdims=True)
        ratio = jnp.sqrt((cost_sum + EPS) / (rhs_sum + EPS))
        steps[...] = jnp.zeros_like(steps)
        steps[0:1] = jnp.broadcast_to(STEP / ratio, (1, TILE))
        steps[1:2] = jnp.broadcast_to(STEP * ratio, (1, TILE))
    if index < ITERS - 1:
        rowout, fresh, racc, work = rest
    else:
        local, link, p0, p1, p2, p3, racc, work = rest
    for lo, hi, src, first in ((0, CT, loc, 0), (CT, OWN, mine, grad_at), (OWN, CW, other, grad_at)):
        at = slice(lo, hi)
        x, scale = primal[at], colf[at]
        grad = scale * src[first : first + hi - lo]
        new = jnp.clip(x - steps[0:1] * (cost[at] - grad), 0.0, upper[at])
        if index < ITERS - 1:
            fresh[at] = new
        elif lo == 0:
            local[...] = scale * new
        else:
            half = place[0] if lo == CT else 1 - place[0]
            link[pl.ds(pl.multiple_of(half * HALF, HALF), HALF), :] = scale * new
        split_to(work, scale * (2.0 * new - x), lo)
    racc[...] = jnp.zeros_like(racc)

    def visit(t, col, row):
        row_pass(tiles_ref, t, col, row, work, racc, jnp.add, False)

    each_tile(rows_ref, cols_ref, place, visit)
    if index < ITERS - 1:
        join_from(racc, rowout, 0, RT)
    else:
        for k, out in enumerate((p0, p1, p2, p3)):
            at = pl.ds(pl.multiple_of((place[2] ^ k) * SHARE, SHARE), SHARE)
            for w in range(2):
                out[:, w * LANES : (w + 1) * LANES] = racc[w, at, :]


def core_kernel(op, tiles_ref, colown, got, out):
    out[...] = op(colown[CT:OWN], got[...])


def merge_kernel(op, tiles_ref, own, r1, r2, r3, out):
    out[...] = tree(op, own[...], (r1[...], r2[...], r3[...]))


def core_grad_kernel(place, tiles_ref, colown, got, gradown, gradgot, m0, m1, m2, m3, half):
    link = jnp.maximum(colown[CT:OWN], got[...])
    half[...] = gradown[CT:OWN] + gradgot[...]
    for k, out in enumerate((m0, m1, m2, m3)):
        out[0:HALF] = link
        out[HALF:] = half[pl.ds(pl.multiple_of((place[1] ^ k) * CHUNK, CHUNK), CHUNK), :]


def merge_grad_kernel(parts, tiles_ref, own, r1, r2, r3, *outs):
    link = tree(jnp.maximum, own[0:HALF], (r1[0:HALF], r2[0:HALF], r3[0:HALF]))
    grad = tree(jnp.add, own[HALF:], (r1[HALF:], r2[HALF:], r3[HALF:]))
    if parts == 1:
        outs[0][0:HALF] = link
        outs[0][HALF:] = grad
    else:
        outs[0][...] = link
        outs[1][...] = grad


def rows_kernel(
    tiles_ref, r0, r1, r2, r3, rowold, rhs, dual, colown, got, colold, cost, chunk, rownew, rhs_scaled,
    dual_scaled, out,
):
    total = tree(jnp.add, r0[...], (r1[...], r2[...], r3[...]))
    old = rowold[...]
    new = old / jnp.sqrt(old * total + EPS)
    rownew[...] = new
    scaled = new * rhs[...]
    rhs_scaled[...] = scaled
    dual_scaled[...] = dual[...] / new
    out[0:HALF] = colown[CT:OWN] + got[...]
    out[HALF:OWN] = jnp.sum((scaled * scaled).reshape(RT // 8, 8, TILE), axis=0)
    old = colold[0:CT]
    part = old / jnp.sqrt(old * colown[0:CT] + EPS) * cost[...]
    out[OWN : OWN + CT] = part * part
    out[OWN + CT :] = chunk[...]


def merge_norm_kernel(place, tiles_ref, own, r1, r2, r3, both, half):
    for k, ref in enumerate((own, r1, r2, r3)):
        half[pl.ds(pl.multiple_of((place[1] ^ k) * CHUNK, CHUNK), CHUNK), :] = ref[HALF + EIGHT :]
    at = slice(0, HALF + EIGHT)
    both[...] = tree(jnp.add, own[at], (r1[at], r2[at], r3[at]))


def merge_all_kernel(tiles_ref, own, r1, r2, r3, half, out):
    out[0 : HALF + EIGHT] = tree(jnp.add, own[...], (r1[...], r2[...], r3[...]))
    out[HALF + EIGHT :] = half[...]


def setup_kernel(
    place, tiles_ref, own, back, colown, colold, cost_loc, cost_lnk, bound_loc, bound_lnk, start_loc, start_lnk,
    colnew, cost, upper, primal, rhs_square, cost_square,
):
    squares = own[HALF : HALF + EIGHT] + back[HALF : HALF + EIGHT]
    rhs_square[...] = squares[0:CT]
    sums = []
    for lo, hi, stat, half in (
        (0, CT, colown, None),
        (CT, OWN, own, place[0]),
        (OWN, CW, back, 1 - place[0]),
    ):
        at = slice(lo, hi)
        if half is None:
            c, b, x = cost_loc[...], bound_loc[...], start_loc[...]
        else:
            rows = pl.ds(pl.multiple_of(half * HALF, HALF), HALF)
            c, b, x = cost_lnk[rows, :], bound_lnk[rows, :], start_lnk[rows, :]
        old = colold[at]
        new = old / jnp.sqrt(old * stat[0 : hi - lo] + EPS)
        colnew[at] = new
        c = new * c
        cost[at] = c
        upper[at] = b / new
        primal[at] = x / new
        if half is not None:
            sums.append(jnp.sum((c * c).reshape(HALF // 8, 8, TILE), axis=0))
    cost_square[...] = squares[CT:] + (sums[0] + sums[1])


def end_kernel(place, steps, p0, p1, p2, p3, dual, rhs, rowf, out):
    at = pl.ds(pl.multiple_of(place[2] * SHARE, SHARE), SHARE)
    total = tree(jnp.add, p0[...], (p1[...], p2[...], p3[...]))
    scale = rowf[at, :]
    out[...] = scale * (dual[at, :] + steps[1:2] * (rhs[at, :] - scale * total))


def body(
    tile_values,
    tile_rows,
    tile_cols,
    cost_local,
    cost_link,
    bound_local,
    bound_link,
    rhs,
    start_local,
    start_link,
    start_dual,
):
    scen = lax.axis_index("scen")
    place = jnp.stack([scen % 2, scen // 8, lax.axis_index("col")])
    ids = (tile_rows[0, 0], tile_cols[0, 0], place)

    def over(swap, x):
        got = {k: swap(x, k) for k in (2, 1, 3)}
        return x, got[1], got[2], got[3]

    row_part, colown, colother, tiles = first_stats(ids, tile_values[0, 0], rhs[0], start_dual[0])

    def run(kernel, smem, operands, outs, scratch=()):
        return call(kernel, smem, tiles, operands, outs, scratch)

    rows = over(swap_y, row_part)
    (link,) = run(functools.partial(core_kernel, jnp.maximum), (), (colown, swap_core(colother)), (HALF,))
    gradown, gradother, rhs_rows, dual_rows = run(
        first_backward_kernel, ids, rows, (OWN, HALF, RT, RT), (COLS, ROWS)
    )
    gradgot = swap_core(gradother)
    (link,) = run(functools.partial(merge_kernel, jnp.maximum), (), over(swap_x, link), (HALF,))
    (link,) = run(functools.partial(merge_kernel, jnp.maximum), (), over(swap_z, link), (HALF,))

    row_part, colown, colother, row_scale, col_scale = run(
        functools.partial(next_stats_kernel, jnp.maximum, True),
        ids,
        (*rows, colown, link, swap_core(link)),
        (RT, OWN, HALF, RT, CW),
        (ROWS, COLS, ROWS, COLS),
    )
    rows = over(swap_y, row_part)
    sent = run(
        core_grad_kernel,
        (place,),
        (colown, swap_core(colother), gradown, gradgot),
        (HALF + CHUNK,) * 4,
        (pltpu.VMEM((HALF, TILE), F32),),
    )
    got = {k: swap_x(sent[k], k) for k in (2, 1, 3)}
    (both,) = run(
        functools.partial(merge_grad_kernel, 1), (), (sent[0], got[1], got[2], got[3]), (HALF + CHUNK,)
    )
    link, chunk = run(functools.partial(merge_grad_kernel, 2), (), over(swap_z, both), (HALF, CHUNK))

    row_part, colown, colother, row_scale, col_scale = run(
        functools.partial(next_stats_kernel, jnp.add, False),
        ids,
        (*rows, colown, link, swap_core(link), row_scale, col_scale),
        (RT, OWN, HALF, RT, CW),
        (ROWS, COLS, ROWS, COLS),
    )
    rows = over(swap_y, row_part)
    row_scale, rhs_scaled, dual_scaled, both = run(
        rows_kernel,
        (),
        (*rows, row_scale, rhs_rows, dual_rows, colown, swap_core(colother), col_scale, cost_local[0, 0], chunk),
        (RT, RT, RT, HALF + EIGHT + CHUNK),
    )
    both, half = run(merge_norm_kernel, (place,), over(swap_x, both), (HALF + EIGHT, HALF))
    (mine,) = run(merge_all_kernel, (), (*over(swap_z, both), half), (LT + EIGHT,))
    other = swap_core(mine)
    col_scale, cost, upper, primal, rhs_square, cost_square = run(
        setup_kernel,
        (place,),
        (
            mine,
            other,
            colown,
            col_scale,
            cost_local[0, 0],
            cost_link[0],
            bound_local[0, 0],
            bound_link[0],
            start_local[0, 0],
            start_link[0],
        ),
        (CW, CW, CW, CW, CT, CT),
    )
    norms = (*over(swap_y, cost_square), rhs_square)

    grads, grad_at = (gradown, mine, other), HALF + EIGHT
    for index in range(ITERS):
        given = norms if index == 0 else (steps,)
        outs = (RT, CW) if index < ITERS - 1 else (CT, LT) + (SHARE,) * 4
        result = run(
            functools.partial(forward_kernel, index, grad_at),
            ids,
            (*given, *grads, primal, cost, upper, col_scale),
            ((CT,) if index == 0 else ()) + outs,
            (ROWS, COLS),
        )
        if index == 0:
            steps, *result = result
        if index == ITERS - 1:
            break
        row_part, primal = result
        colown, colother, dual_scaled = run(
            backward_kernel,
            ids,
            (steps, *over(swap_y, row_part), dual_scaled, rhs_scaled, row_scale),
            (OWN, HALF, RT),
            (COLS, ROWS),
        )
        (link,) = run(functools.partial(core_kernel, jnp.add), (), (colown, swap_core(colother)), (HALF,))
        (link,) = run(functools.partial(merge_kernel, jnp.add), (), over(swap_x, link), (HALF,))
        (link,) = run(functools.partial(merge_kernel, jnp.add), (), over(swap_z, link), (HALF,))
        grads, grad_at = (colown, link, swap_core(link)), 0

    local, link, *pieces = result
    got = {k: swap_y(pieces[k], k) for k in (2, 1, 3)}
    vmem = pl.BlockSpec(memory_space=pltpu.VMEM)
    multipliers = pl.pallas_call(
        end_kernel,
        out_shape=jax.ShapeDtypeStruct((SHARE, TILE), F32),
        in_specs=[pl.BlockSpec(memory_space=pltpu.SMEM)] + [vmem] * 8,
        out_specs=vmem,
    )(place, steps, pieces[0], got[1], got[2], got[3], dual_scaled, rhs_scaled, row_scale)
    return local[None, None], link[None], multipliers[None]


def solution(mesh):
    placed = (
        P("scen", "col", None, None, None),
        P("scen", "col", None),
        P("scen", "col", None),
        P("scen", "col", None, None),
        P("col", None, None),
        P("scen", "col", None, None),
        P("col", None, None),
        P("scen", "col", None),
        P("scen", "col", None, None),
        P("col", None, None),
        P("scen", "col", None),
    )
    return jax.shard_map(
        body,
        mesh=mesh,
        in_specs=placed,
        out_specs=(P("scen", "col", None, None), P("col", None, None), P("scen", "col", None)),
        check_vma=False,
    )
```

```python
import functools

import jax
import jax.numpy as jnp
from jax import lax
from jax.experimental import pallas as pl
from jax.experimental.pallas import tpu as pltpu
from jax.sharding import PartitionSpec as P

TILE = 256
RT = 128
CT = 8
LT = 256
ITERS = 3
NT = 64
HALF = LT // 2
SHARE = RT // 4
CW = CT + LT
GROUP = 8
STEPS = NT // GROUP

EPS = 1e-06
STEP = 0.9
F32 = jnp.float32
LANES = 128
VMEM_LIMIT = 24 * 1024 * 1024


def swap_core(x):
    return lax.ppermute(x, "scen", [(i, i ^ 1) for i in range(32)])


def swap_first(x, k):
    return lax.ppermute(x, "scen", [(i, i ^ (k << (1 if i % 2 else 3))) for i in range(32)])


def swap_second(x, k):
    return lax.ppermute(x, "scen", [(i, i ^ (k << (3 if i % 2 else 1))) for i in range(32)])


def swap_y(x, k):
    return lax.ppermute(x, "col", [(i, i ^ k) for i in range(4)])


def tree(op, own, got):
    return op(op(own, got[0]), op(got[1], got[2]))


def row_pass(tiles_ref, t, col, row, colf_ref, rowout_ref, op, magnitude):
    for h in range(2):
        a = tiles_ref[t, h * LANES : (h + 1) * LANES, 0:LANES]
        b = tiles_ref[t, h * LANES : (h + 1) * LANES, LANES:TILE]
        if magnitude:
            a, b = jnp.abs(a), jnp.abs(b)
        if colf_ref is not None:
            a = a * colf_ref[0, pl.ds(col, 1), :]
            b = b * colf_ref[1, pl.ds(col, 1), :]
        m = op(a, b).T
        s = jnp.max(m, axis=0, keepdims=True) if op is jnp.maximum else jnp.sum(m, axis=0, keepdims=True)
        at = (h, pl.ds(row, 1), slice(None))
        rowout_ref[at] = op(rowout_ref[at], s)


def col_pass(tiles_ref, t, col, row, rowf_ref, colout_ref, op, magnitude):
    parts = [None, None]
    for h in range(2):
        if rowf_ref is not None:
            f = jnp.broadcast_to(rowf_ref[h, pl.ds(row, 1), :], (LANES, LANES)).T
        for w in range(2):
            a = tiles_ref[t, h * LANES : (h + 1) * LANES, w * LANES : (w + 1) * LANES]
            if magnitude:
                a = jnp.abs(a)
            if rowf_ref is not None:
                a = a * f
            a = a.reshape(16, 8, LANES)
            s = jnp.max(a, axis=0) if op is jnp.maximum else jnp.sum(a, axis=0)
            parts[w] = s if parts[w] is None else op(parts[w], s)
    for w in range(2):
        s = parts[w]
        s = jnp.max(s, axis=0, keepdims=True) if op is jnp.maximum else jnp.sum(s, axis=0, keepdims=True)
        at = (w, pl.ds(col, 1), slice(None))
        colout_ref[at] = op(colout_ref[at], s)


def split_to(ref, value, lo=0):
    for w in range(2):
        ref[w, lo : lo + value.shape[0], :] = value[:, w * LANES : (w + 1) * LANES]


def join_from(ref, out, lo, hi):
    for w in range(2):
        out[0 : hi - lo, w * LANES : (w + 1) * LANES] = ref[w, lo:hi, :]


ROWS = pltpu.VMEM((2, RT, LANES), F32)
COLS = pltpu.VMEM((2, CW, LANES), F32)
OWN = CT + HALF
EIGHT = 2 * CT
CHUNK = HALF // 4


def call(kernel, smem, tiles, operands, outs, scratch=()):
    operands = [pltpu.with_memory_space_constraint(tiles, pltpu.VMEM)] + list(operands)
    vmem = pl.BlockSpec(memory_space=pltpu.VMEM)
    return pl.pallas_call(
        kernel,
        out_shape=tuple(jax.ShapeDtypeStruct((n, TILE), F32) for n in outs),
        in_specs=[pl.BlockSpec(memory_space=pltpu.SMEM) for _ in smem] + [vmem for _ in operands],
        out_specs=tuple(vmem for _ in outs),
        scratch_shapes=list(scratch),
        compiler_params=pltpu.CompilerParams(vmem_limit_bytes=VMEM_LIMIT),
    )(*smem, *operands)


def each_tile(rows_ref, cols_ref, place_ref, visit, ready=None):
    turn = place_ref[0] * HALF

    def group(step, carry):
        if ready is not None:
            ready(step)
        for i in range(GROUP):
            t = step * GROUP + i
            col = cols_ref[t]
            col = jnp.where(col < CT, col, CT + ((col - CT) ^ turn))
            visit(t, col, rows_ref[t])
        return carry

    lax.fori_loop(0, STEPS, group, 0)


def put_columns(cacc, colown, colother):
    join_from(cacc, colown, 0, OWN)
    join_from(cacc, colother, OWN, CW)


def first_stats_kernel(
    place, rows_hbm, cols_hbm, source, rhs, dual, rowout, colown, colother, tiles_ref, racc, cacc,
    rows_ref, cols_ref, sems,
):
    indices = [
        pltpu.make_async_copy(src, dst, sems.at[STEPS + 2 + i])
        for i, (src, dst) in enumerate(((rows_hbm, rows_ref), (cols_hbm, cols_ref)))
    ]
    for copy in indices:
        copy.start()

    def load(step):
        part = pl.ds(step * GROUP, GROUP)
        return pltpu.make_async_copy(source.at[part], tiles_ref.at[part], sems.at[step])

    for step in range(STEPS):
        load(step).start()
    extra = [
        pltpu.make_async_copy(src, rowout.at[pl.ds(RT + i * SHARE, SHARE)], sems.at[STEPS + i])
        for i, src in enumerate((rhs, dual))
    ]
    for copy in extra:
        copy.start()
    racc[...] = jnp.zeros_like(racc)
    cacc[...] = jnp.zeros_like(cacc)

    for copy in indices:
        copy.wait()

    def visit(t, col, row):
        row_pass(tiles_ref, t, col, row, None, racc, jnp.maximum, True)
        col_pass(tiles_ref, t, col, row, None, cacc, jnp.maximum, True)

    each_tile(rows_ref, cols_ref, place, visit, lambda step: load(step).wait())
    join_from(racc, rowout, 0, RT)
    put_columns(cacc, colown, colother)
    for copy in extra:
        copy.wait()


def first_stats(ids, source, rhs, dual):
    vmem = pl.BlockSpec(memory_space=pltpu.VMEM)
    shapes = [jax.ShapeDtypeStruct((n, TILE), F32) for n in (RT + 2 * SHARE, OWN, HALF)]
    return pl.pallas_call(
        first_stats_kernel,
        out_shape=(*shapes, pltpu.VMEM((NT, TILE, TILE), F32)),
        in_specs=[pl.BlockSpec(memory_space=pltpu.SMEM)] + [pl.BlockSpec(memory_space=pltpu.HBM)] * 5,
        out_specs=(vmem,) * 4,
        scratch_shapes=[
            ROWS,
            COLS,
            pltpu.SMEM((NT,), jnp.int32),
            pltpu.SMEM((NT,), jnp.int32),
            pltpu.SemaphoreType.DMA((STEPS + 4,)),
        ],
        compiler_params=pltpu.CompilerParams(vmem_limit_bytes=VMEM_LIMIT),
    )(ids[2], *(pltpu.with_memory_space_constraint(x, pltpu.HBM) for x in (*ids[:2], source, rhs, dual)))


def next_stats_kernel(
    op, first, rows_ref, cols_ref, place, tiles_ref, rowstat, loc, mine, other, *rest
):
    if first:
        rowout, colown, colother, rownew, colnew, racc, cacc, rowf, colf = rest
    else:
        rowold, colold, rowout, colown, colother, rownew, colnew, racc, cacc, rowf, colf = rest
    row = rowstat[...]
    if first:
        new = 1.0 / jnp.sqrt(row + EPS)
    else:
        old = rowold[...]
        new = old / jnp.sqrt(old * row + EPS)
    rownew[...] = new
    split_to(rowf, new)
    for lo, hi, src in ((0, CT, loc), (CT, OWN, mine), (OWN, CW, other)):
        stat = src[0 : hi - lo]
        if first:
            new = 1.0 / jnp.sqrt(stat + EPS)
        else:
            old = colold[lo:hi]
            new = old / jnp.sqrt(old * stat + EPS)
        colnew[lo:hi] = new
        split_to(colf, new, lo)
    racc[...] = jnp.zeros_like(racc)
    cacc[...] = jnp.zeros_like(cacc)

    def visit(t, col, row):
        row_pass(tiles_ref, t, col, row, colf, racc, op, True)
        col_pass(tiles_ref, t, col, row, rowf, cacc, op, True)

    each_tile(rows_ref, cols_ref, place, visit)
    join_from(racc, rowout, 0, RT)
    put_columns(cacc, colown, colother)


def first_backward_kernel(
    rows_ref, cols_ref, place, tiles_ref, r0, r1, r2, r3, colown, colother, rhsout, dualout, cacc, work
):
    for k, ref in enumerate((r0, r1, r2, r3)):
        at = pl.ds(pl.multiple_of((place[2] ^ k) * SHARE, SHARE), SHARE)
        rhsout[at, :] = ref[RT : RT + SHARE]
        dualout[at, :] = ref[RT + SHARE :]
    split_to(work, dualout[...])
    cacc[...] = jnp.zeros_like(cacc)

    def visit(t, col, row):
        col_pass(tiles_ref, t, col, row, work, cacc, jnp.add, False)

    each_tile(rows_ref, cols_ref, place, visit)
    put_columns(cacc, colown, colother)


def backward_kernel(
    rows_ref, cols_ref, place, tiles_ref, steps, r0, r1, r2, r3, dual, rhs, rowf, colown, colother, dualnew,
    cacc, work,
):
    total = tree(jnp.add, r0[...], (r1[...], r2[...], r3[...]))
    new = dual[...] + steps[1:2] * (rhs[...] - rowf[...] * total)
    dualnew[...] = new
    split_to(work, rowf[...] * new)
    cacc[...] = jnp.zeros_like(cacc)

    def visit(t, col, row):
        col_pass(tiles_ref, t, col, row, work, cacc, jnp.add, False)

    each_tile(rows_ref, cols_ref, place, visit)
    put_columns(cacc, colown, colother)


def forward_kernel(index, grad_at, rows_ref, cols_ref, place, tiles_ref, *rest):
    if index == 0:
        c0, c1, c2, c3, rhs_square, *rest = rest
    else:
        steps, *rest = rest
    loc, mine, other, primal, cost, upper, colf, *rest = rest
    if index == 0:
        steps, *rest = rest
        total = tree(jnp.add, c0[...], (c1[...], c2[...], c3[...]))
        cost_sum = jnp.sum(total, axis=(0, 1), keepdims=True)
        rhs_sum = jnp.sum(rhs_square[...], axis=(0, 1), keepdims=True)
        ratio = jnp.sqrt((cost_sum + EPS) / (rhs_sum + EPS))
        steps[...] = jnp.zeros_like(steps)
        steps[0:1] = jnp.broadcast_to(STEP / ratio, (1, TILE))
        steps[1:2] = jnp.broadcast_to(STEP * ratio, (1, TILE))
    if index < ITERS - 1:
        rowout, fresh, racc, work = rest
    else:
        dual, rhs, rowf, local, link, dualout, rhsout, rowfout, p0, p1, p2, p3, racc, work = rest
        own = pl.ds(pl.multiple_of(place[2] * SHARE, SHARE), SHARE)
        for ref, out in ((dual, dualout), (rhs, rhsout), (rowf, rowfout)):
            out[...] = ref[own, :]
    for lo, hi, src, first in ((0, CT, loc, 0), (CT, OWN, mine, grad_at), (OWN, CW, other, grad_at)):
        at = slice(lo, hi)
        x, scale = primal[at], colf[at]
        grad = scale * src[first : first + hi - lo]
        new = jnp.clip(x - steps[0:1] * (cost[at] - grad), 0.0, upper[at])
        if index < ITERS - 1:
            fresh[at] = new
        elif lo == 0:
            local[...] = scale * new
        else:
            half = place[0] if lo == CT else 1 - place[0]
            link[pl.ds(pl.multiple_of(half * HALF, HALF), HALF), :] = scale * new
        split_to(work, scale * (2.0 * new - x), lo)
    racc[...] = jnp.zeros_like(racc)

    def visit(t, col, row):
        row_pass(tiles_ref, t, col, row, work, racc, jnp.add, False)

    each_tile(rows_ref, cols_ref, place, visit)
    if index < ITERS - 1:
        join_from(racc, rowout, 0, RT)
    else:
        for k, out in enumerate((p0, p1, p2, p3)):
            at = pl.ds(pl.multiple_of((place[2] ^ k) * SHARE, SHARE), SHARE)
            for w in range(2):
                out[:, w * LANES : (w + 1) * LANES] = racc[w, at, :]


def core_kernel(op, tiles_ref, colown, got, out):
    out[...] = op(colown[CT:OWN], got[...])


def merge_kernel(op, tiles_ref, own, r1, r2, r3, out):
    out[...] = tree(op, own[...], (r1[...], r2[...], r3[...]))


def merge_after_kernel(tiles_ref, own, r1, r2, r3, after, out):
    out[...] = tree(jnp.maximum, own[...], (r1[...], r2[...], r3[...]))


def merge_rows_kernel(tiles_ref, own, r1, r2, r3, y0, y1, y2, y3, out, rows):
    out[...] = tree(jnp.maximum, own[...], (r1[...], r2[...], r3[...]))
    rows[...] = tree(jnp.maximum, y0[0:RT], (y1[0:RT], y2[0:RT], y3[0:RT]))


def core_grad_kernel(place, tiles_ref, colown, got, gradown, gradgot, m0, m1, m2, m3, half):
    link = jnp.maximum(colown[CT:OWN], got[...])
    half[...] = gradown[CT:OWN] + gradgot[...]
    for k, out in enumerate((m0, m1, m2, m3)):
        out[0:HALF] = link
        out[HALF:] = half[pl.ds(pl.multiple_of((place[1] ^ k) * CHUNK, CHUNK), CHUNK), :]


def merge_grad_rows_kernel(tiles_ref, own, r1, r2, r3, y0, y1, y2, y3, both, rows):
    both[0:HALF] = tree(jnp.maximum, own[0:HALF], (r1[0:HALF], r2[0:HALF], r3[0:HALF]))
    both[HALF:] = tree(jnp.add, own[HALF:], (r1[HALF:], r2[HALF:], r3[HALF:]))
    rows[...] = tree(jnp.maximum, y0[...], (y1[...], y2[...], y3[...]))


def merge_grad_kernel(tiles_ref, own, r1, r2, r3, link, grad):
    link[...] = tree(jnp.maximum, own[0:HALF], (r1[0:HALF], r2[0:HALF], r3[0:HALF]))
    grad[...] = tree(jnp.add, own[HALF:], (r1[HALF:], r2[HALF:], r3[HALF:]))


def rows_kernel(
    tiles_ref, r0, r1, r2, r3, rowold, rhs, dual, colown, got, colold, cost, chunk, rownew, rhs_scaled,
    dual_scaled, out,
):
    total = tree(jnp.add, r0[...], (r1[...], r2[...], r3[...]))
    old = rowold[...]
    new = old / jnp.sqrt(old * total + EPS)
    rownew[...] = new
    scaled = new * rhs[...]
    rhs_scaled[...] = scaled
    dual_scaled[...] = dual[...] / new
    out[0:HALF] = colown[CT:OWN] + got[...]
    out[HALF:OWN] = jnp.sum((scaled * scaled).reshape(RT // 8, 8, TILE), axis=0)
    old = colold[0:CT]
    part = old / jnp.sqrt(old * colown[0:CT] + EPS) * cost[...]
    out[OWN : OWN + CT] = part * part
    out[OWN + CT :] = chunk[...]


def merge_norm_kernel(place, tiles_ref, own, r1, r2, r3, both, half):
    for k, ref in enumerate((own, r1, r2, r3)):
        half[pl.ds(pl.multiple_of((place[1] ^ k) * CHUNK, CHUNK), CHUNK), :] = ref[HALF + EIGHT :]
    at = slice(0, HALF + EIGHT)
    both[...] = tree(jnp.add, own[at], (r1[at], r2[at], r3[at]))


def merge_all_kernel(tiles_ref, own, r1, r2, r3, half, out):
    out[0 : HALF + EIGHT] = tree(jnp.add, own[...], (r1[...], r2[...], r3[...]))
    out[HALF + EIGHT :] = half[...]


def setup_kernel(
    place, tiles_ref, own, back, colown, colold, cost_loc, cost_lnk, bound_loc, bound_lnk, start_loc, start_lnk,
    colnew, cost, upper, primal, rhs_square, cost_square,
):
    squares = own[HALF : HALF + EIGHT] + back[HALF : HALF + EIGHT]
    rhs_square[...] = squares[0:CT]
    sums = []
    for lo, hi, stat, half in (
        (0, CT, colown, None),
        (CT, OWN, own, place[0]),
        (OWN, CW, back, 1 - place[0]),
    ):
        at = slice(lo, hi)
        if half is None:
            c, b, x = cost_loc[...], bound_loc[...], start_loc[...]
        else:
            rows = pl.ds(pl.multiple_of(half * HALF, HALF), HALF)
            c, b, x = cost_lnk[rows, :], bound_lnk[rows, :], start_lnk[rows, :]
        old = colold[at]
        new = old / jnp.sqrt(old * stat[0 : hi - lo] + EPS)
        colnew[at] = new
        c = new * c
        cost[at] = c
        upper[at] = b / new
        primal[at] = x / new
        if half is not None:
            sums.append(jnp.sum((c * c).reshape(HALF // 8, 8, TILE), axis=0))
    cost_square[...] = squares[CT:] + (sums[0] + sums[1])


def end_kernel(steps, p0, p1, p2, p3, dual, rhs, rowf, out):
    total = tree(jnp.add, p0[...], (p1[...], p2[...], p3[...]))
    scale = rowf[...]
    out[...] = scale * (dual[...] + steps[1:2] * (rhs[...] - scale * total))


def body(
    tile_values,
    tile_rows,
    tile_cols,
    cost_local,
    cost_link,
    bound_local,
    bound_link,
    rhs,
    start_local,
    start_link,
    start_dual,
):
    scen = lax.axis_index("scen")
    core = scen % 2
    place = jnp.stack(
        [core, jnp.where(core == 0, scen // 8, (scen // 2) % 4), lax.axis_index("col")]
    )
    ids = (tile_rows[0, 0], tile_cols[0, 0], place)

    def over(swap, x):
        got = {k: swap(x, k) for k in (2, 1, 3)}
        return x, got[1], got[2], got[3]

    row_part, colown, colother, tiles = first_stats(ids, tile_values[0, 0], rhs[0], start_dual[0])

    def run(kernel, smem, operands, outs, scratch=()):
        return call(kernel, smem, tiles, operands, outs, scratch)

    rows = over(swap_y, row_part)
    (link,) = run(functools.partial(core_kernel, jnp.maximum), (), (colown, swap_core(colother)), (HALF,))
    link, row_stat = run(merge_rows_kernel, (), (*over(swap_first, link), *rows), (HALF, RT))
    gradown, gradother, rhs_rows, dual_rows = run(
        first_backward_kernel, ids, rows, (OWN, HALF, RT, RT), (COLS, ROWS)
    )
    gradgot = swap_core(gradother)
    (link,) = run(merge_after_kernel, (), (*over(swap_second, link), gradother), (HALF,))

    row_part, colown, colother, row_scale, col_scale = run(
        functools.partial(next_stats_kernel, jnp.maximum, True),
        ids,
        (row_stat, colown, link, swap_core(link)),
        (RT, OWN, HALF, RT, CW),
        (ROWS, COLS, ROWS, COLS),
    )
    rows = over(swap_y, row_part)
    sent = run(
        core_grad_kernel,
        (place,),
        (colown, swap_core(colother), gradown, gradgot),
        (HALF + CHUNK,) * 4,
        (pltpu.VMEM((HALF, TILE), F32),),
    )
    got = {k: swap_first(sent[k], k) for k in (2, 1, 3)}
    both, row_stat = run(
        merge_grad_rows_kernel, (), (sent[0], got[1], got[2], got[3], *rows), (HALF + CHUNK, RT)
    )
    link, chunk = run(merge_grad_kernel, (), over(swap_second, both), (HALF, CHUNK))

    row_part, colown, colother, row_scale, col_scale = run(
        functools.partial(next_stats_kernel, jnp.add, False),
        ids,
        (row_stat, colown, link, swap_core(link), row_scale, col_scale),
        (RT, OWN, HALF, RT, CW),
        (ROWS, COLS, ROWS, COLS),
    )
    rows = over(swap_y, row_part)
    row_scale, rhs_scaled, dual_scaled, both = run(
        rows_kernel,
        (),
        (*rows, row_scale, rhs_rows, dual_rows, colown, swap_core(colother), col_scale, cost_local[0, 0], chunk),
        (RT, RT, RT, HALF + EIGHT + CHUNK),
    )
    both, half = run(merge_norm_kernel, (place,), over(swap_first, both), (HALF + EIGHT, HALF))
    (mine,) = run(merge_all_kernel, (), (*over(swap_second, both), half), (LT + EIGHT,))
    other = swap_core(mine)
    col_scale, cost, upper, primal, rhs_square, cost_square = run(
        setup_kernel,
        (place,),
        (
            mine,
            other,
            colown,
            col_scale,
            cost_local[0, 0],
            cost_link[0],
            bound_local[0, 0],
            bound_link[0],
            start_local[0, 0],
            start_link[0],
        ),
        (CW, CW, CW, CW, CT, CT),
    )
    norms = (*over(swap_y, cost_square), rhs_square)

    grads, grad_at = (gradown, mine, other), HALF + EIGHT
    for index in range(ITERS):
        given = norms if index == 0 else (steps,)
        extra = (dual_scaled, rhs_scaled, row_scale) if index == ITERS - 1 else ()
        outs = (RT, CW) if index < ITERS - 1 else (CT, LT) + (SHARE,) * 7
        result = run(
            functools.partial(forward_kernel, index, grad_at),
            ids,
            (*given, *grads, primal, cost, upper, col_scale, *extra),
            ((CT,) if index == 0 else ()) + outs,
            (ROWS, COLS),
        )
        if index == 0:
            steps, *result = result
        if index == ITERS - 1:
            break
        row_part, primal = result
        colown, colother, dual_scaled = run(
            backward_kernel,
            ids,
            (steps, *over(swap_y, row_part), dual_scaled, rhs_scaled, row_scale),
            (OWN, HALF, RT),
            (COLS, ROWS),
        )
        (link,) = run(functools.partial(core_kernel, jnp.add), (), (colown, swap_core(colother)), (HALF,))
        (link,) = run(functools.partial(merge_kernel, jnp.add), (), over(swap_first, link), (HALF,))
        (link,) = run(functools.partial(merge_kernel, jnp.add), (), over(swap_second, link), (HALF,))
        grads, grad_at = (colown, link, swap_core(link)), 0

    local, link, dual, rhs_own, scale, *pieces = result
    got = {k: swap_y(pieces[k], k) for k in (2, 1, 3)}
    vmem = pl.BlockSpec(memory_space=pltpu.VMEM)
    multipliers = pl.pallas_call(
        end_kernel,
        out_shape=jax.ShapeDtypeStruct((SHARE, TILE), F32),
        in_specs=[vmem] * 8,
        out_specs=vmem,
    )(steps, pieces[0], got[1], got[2], got[3], dual, rhs_own, scale)
    return local[None, None], link[None], multipliers[None]


def solution(mesh):
    placed = (
        P("scen", "col", None, None, None),
        P("scen", "col", None),
        P("scen", "col", None),
        P("scen", "col", None, None),
        P("col", None, None),
        P("scen", "col", None, None),
        P("col", None, None),
        P("scen", "col", None),
        P("scen", "col", None, None),
        P("col", None, None),
        P("scen", "col", None),
    )
    return jax.shard_map(
        body,
        mesh=mesh,
        in_specs=placed,
        out_specs=(P("scen", "col", None, None), P("col", None, None), P("scen", "col", None)),
        check_vma=False,
    )
```

```python
import functools

import jax
import jax.numpy as jnp
from jax import lax
from jax.experimental import pallas as pl
from jax.experimental.pallas import tpu as pltpu
from jax.sharding import PartitionSpec as P

TILE = 256
RT = 128
CT = 8
LT = 256
ITERS = 3
NT = 64
HALF = LT // 2
SHARE = RT // 4
CW = CT + LT
GROUP = 8
STEPS = NT // GROUP

EPS = 1e-06
STEP = 0.9
F32 = jnp.float32
LANES = 128
VMEM_LIMIT = 24 * 1024 * 1024


def swap_core(x):
    return lax.ppermute(x, "scen", [(i, i ^ 1) for i in range(32)])


def swap_first(x, k):
    return lax.ppermute(x, "scen", [(i, i ^ (k << (1 if i % 2 else 3))) for i in range(32)])


def swap_second(x, k):
    return lax.ppermute(x, "scen", [(i, i ^ (k << (3 if i % 2 else 1))) for i in range(32)])


def swap_y(x, k):
    return lax.ppermute(x, "col", [(i, i ^ k) for i in range(4)])


def tree(op, own, got):
    return op(op(own, got[0]), op(got[1], got[2]))


def row_pass(tiles_ref, t, col, row, colf_ref, rowout_ref, op, magnitude):
    for h in range(2):
        a = tiles_ref[t, h * LANES : (h + 1) * LANES, 0:LANES]
        b = tiles_ref[t, h * LANES : (h + 1) * LANES, LANES:TILE]
        if magnitude:
            a, b = jnp.abs(a), jnp.abs(b)
        if colf_ref is not None:
            a = a * colf_ref[0, pl.ds(col, 1), :]
            b = b * colf_ref[1, pl.ds(col, 1), :]
        m = op(a, b).T
        s = jnp.max(m, axis=0, keepdims=True) if op is jnp.maximum else jnp.sum(m, axis=0, keepdims=True)
        at = (h, pl.ds(row, 1), slice(None))
        rowout_ref[at] = op(rowout_ref[at], s)


def col_pass(tiles_ref, t, col, row, rowf_ref, colout_ref, op, magnitude):
    parts = [None, None]
    for h in range(2):
        if rowf_ref is not None:
            f = jnp.broadcast_to(rowf_ref[h, pl.ds(row, 1), :], (LANES, LANES)).T
        for w in range(2):
            a = tiles_ref[t, h * LANES : (h + 1) * LANES, w * LANES : (w + 1) * LANES]
            if magnitude:
                a = jnp.abs(a)
            if rowf_ref is not None:
                a = a * f
            a = a.reshape(16, 8, LANES)
            s = jnp.max(a, axis=0) if op is jnp.maximum else jnp.sum(a, axis=0)
            parts[w] = s if parts[w] is None else op(parts[w], s)
    for w in range(2):
        s = parts[w]
        s = jnp.max(s, axis=0, keepdims=True) if op is jnp.maximum else jnp.sum(s, axis=0, keepdims=True)
        at = (w, pl.ds(col, 1), slice(None))
        colout_ref[at] = op(colout_ref[at], s)


def split_to(ref, value, lo=0):
    for w in range(2):
        ref[w, lo : lo + value.shape[0], :] = value[:, w * LANES : (w + 1) * LANES]


def join_from(ref, out, lo, hi):
    for w in range(2):
        out[0 : hi - lo, w * LANES : (w + 1) * LANES] = ref[w, lo:hi, :]


ROWS = pltpu.VMEM((2, RT, LANES), F32)
COLS = pltpu.VMEM((2, CW, LANES), F32)
OWN = CT + HALF
EIGHT = 2 * CT
CHUNK = HALF // 4


def call(kernel, smem, tiles, operands, outs, scratch=()):
    operands = [pltpu.with_memory_space_constraint(tiles, pltpu.VMEM)] + list(operands)
    vmem = pl.BlockSpec(memory_space=pltpu.VMEM)
    return pl.pallas_call(
        kernel,
        out_shape=tuple(jax.ShapeDtypeStruct((n, TILE), F32) for n in outs),
        in_specs=[pl.BlockSpec(memory_space=pltpu.SMEM) for _ in smem] + [vmem for _ in operands],
        out_specs=tuple(vmem for _ in outs),
        scratch_shapes=list(scratch),
        compiler_params=pltpu.CompilerParams(vmem_limit_bytes=VMEM_LIMIT),
    )(*smem, *operands)


def each_tile(rows_ref, cols_ref, place_ref, visit, ready=None):
    turn = place_ref[0] * HALF

    def group(step, carry):
        if ready is not None:
            ready(step)
        for i in range(GROUP):
            t = step * GROUP + i
            col = cols_ref[t]
            col = jnp.where(col < CT, col, CT + ((col - CT) ^ turn))
            visit(t, col, rows_ref[t])
        return carry

    lax.fori_loop(0, STEPS, group, 0)


def put_columns(cacc, colown, colother):
    join_from(cacc, colown, 0, OWN)
    join_from(cacc, colother, OWN, CW)


def first_stats_kernel(
    place, rows_hbm, cols_hbm, source, rhs, dual, rowout, colown, colother, tiles_ref, racc, cacc,
    rows_ref, cols_ref, sems,
):
    indices = [
        pltpu.make_async_copy(src, dst, sems.at[STEPS + 2 + i])
        for i, (src, dst) in enumerate(((rows_hbm, rows_ref), (cols_hbm, cols_ref)))
    ]
    for copy in indices:
        copy.start()

    def load(step):
        part = pl.ds(step * GROUP, GROUP)
        return pltpu.make_async_copy(source.at[part], tiles_ref.at[part], sems.at[step])

    for step in range(STEPS):
        load(step).start()
    extra = [
        pltpu.make_async_copy(src, rowout.at[pl.ds(RT + i * SHARE, SHARE)], sems.at[STEPS + i])
        for i, src in enumerate((rhs, dual))
    ]
    for copy in extra:
        copy.start()
    racc[...] = jnp.zeros_like(racc)
    cacc[...] = jnp.zeros_like(cacc)

    for copy in indices:
        copy.wait()

    def visit(t, col, row):
        row_pass(tiles_ref, t, col, row, None, racc, jnp.maximum, True)
        col_pass(tiles_ref, t, col, row, None, cacc, jnp.maximum, True)

    each_tile(rows_ref, cols_ref, place, visit, lambda step: load(step).wait())
    join_from(racc, rowout, 0, RT)
    put_columns(cacc, colown, colother)
    for copy in extra:
        copy.wait()


def first_stats(ids, source, rhs, dual):
    vmem = pl.BlockSpec(memory_space=pltpu.VMEM)
    shapes = [jax.ShapeDtypeStruct((n, TILE), F32) for n in (RT + 2 * SHARE, OWN, HALF)]
    return pl.pallas_call(
        first_stats_kernel,
        out_shape=(*shapes, pltpu.VMEM((NT, TILE, TILE), F32)),
        in_specs=[pl.BlockSpec(memory_space=pltpu.SMEM)] + [pl.BlockSpec(memory_space=pltpu.HBM)] * 5,
        out_specs=(vmem,) * 4,
        scratch_shapes=[
            ROWS,
            COLS,
            pltpu.SMEM((NT,), jnp.int32),
            pltpu.SMEM((NT,), jnp.int32),
            pltpu.SemaphoreType.DMA((STEPS + 4,)),
        ],
        compiler_params=pltpu.CompilerParams(vmem_limit_bytes=VMEM_LIMIT),
    )(ids[2], *(pltpu.with_memory_space_constraint(x, pltpu.HBM) for x in (*ids[:2], source, rhs, dual)))


def second_stats_kernel(
    rows_ref, cols_ref, place, tiles_ref, r0, r1, r2, r3, loc, mine, other, rowout, colown, colother, rownew,
    colnew, racc, cacc, rowf, colf,
):
    row = tree(jnp.maximum, r0[0:RT], (r1[0:RT], r2[0:RT], r3[0:RT]))
    new = 1.0 / jnp.sqrt(row + EPS)
    rownew[...] = new
    split_to(rowf, new)
    for lo, hi, src in ((0, CT, loc), (CT, OWN, mine), (OWN, CW, other)):
        new = 1.0 / jnp.sqrt(src[0 : hi - lo] + EPS)
        colnew[lo:hi] = new
        split_to(colf, new, lo)
    racc[...] = jnp.zeros_like(racc)
    cacc[...] = jnp.zeros_like(cacc)

    def visit(t, col, row):
        row_pass(tiles_ref, t, col, row, colf, racc, jnp.maximum, True)
        col_pass(tiles_ref, t, col, row, rowf, cacc, jnp.maximum, True)

    each_tile(rows_ref, cols_ref, place, visit)
    join_from(racc, rowout, 0, RT)
    put_columns(cacc, colown, colother)


def third_rows_kernel(
    rows_ref, cols_ref, place, tiles_ref, r0, r1, r2, r3, loc, mine, other, rowold, colold, rowout, rownew,
    colnew, racc, colf,
):
    row = tree(jnp.maximum, r0[...], (r1[...], r2[...], r3[...]))
    old = rowold[...]
    rownew[...] = old / jnp.sqrt(old * row + EPS)
    for lo, hi, src in ((0, CT, loc), (CT, OWN, mine), (OWN, CW, other)):
        old = colold[lo:hi]
        new = old / jnp.sqrt(old * src[0 : hi - lo] + EPS)
        colnew[lo:hi] = new
        split_to(colf, new, lo)
    racc[...] = jnp.zeros_like(racc)

    def visit(t, col, row):
        row_pass(tiles_ref, t, col, row, colf, racc, jnp.add, True)

    each_tile(rows_ref, cols_ref, place, visit)
    join_from(racc, rowout, 0, RT)


def third_columns_kernel(rows_ref, cols_ref, place, tiles_ref, row_scale, colown, colother, cacc, rowf):
    split_to(rowf, row_scale[...])
    cacc[...] = jnp.zeros_like(cacc)

    def visit(t, col, row):
        col_pass(tiles_ref, t, col, row, rowf, cacc, jnp.add, True)

    each_tile(rows_ref, cols_ref, place, visit)
    put_columns(cacc, colown, colother)


def first_backward_kernel(
    rows_ref, cols_ref, place, tiles_ref, r0, r1, r2, r3, after, colown, colother, rhsout, dualout, cacc, work
):
    for k, ref in enumerate((r0, r1, r2, r3)):
        at = pl.ds(pl.multiple_of((place[2] ^ k) * SHARE, SHARE), SHARE)
        rhsout[at, :] = ref[RT : RT + SHARE]
        dualout[at, :] = ref[RT + SHARE :]
    split_to(work, dualout[...])
    cacc[...] = jnp.zeros_like(cacc)

    def visit(t, col, row):
        col_pass(tiles_ref, t, col, row, work, cacc, jnp.add, False)

    each_tile(rows_ref, cols_ref, place, visit)
    put_columns(cacc, colown, colother)


def backward_kernel(
    rows_ref, cols_ref, place, tiles_ref, steps, r0, r1, r2, r3, dual, rhs, rowf, colown, colother, dualnew,
    cacc, work,
):
    total = tree(jnp.add, r0[...], (r1[...], r2[...], r3[...]))
    new = dual[...] + steps[1:2] * (rhs[...] - rowf[...] * total)
    dualnew[...] = new
    split_to(work, rowf[...] * new)
    cacc[...] = jnp.zeros_like(cacc)

    def visit(t, col, row):
        col_pass(tiles_ref, t, col, row, work, cacc, jnp.add, False)

    each_tile(rows_ref, cols_ref, place, visit)
    put_columns(cacc, colown, colother)


def forward_kernel(index, grad_at, rows_ref, cols_ref, place, tiles_ref, *rest):
    if index == 0:
        c0, c1, c2, c3, rhs_square, *rest = rest
    else:
        steps, *rest = rest
    loc, mine, other, primal, cost, upper, colf, *rest = rest
    if index == 0:
        steps, *rest = rest
        total = tree(jnp.add, c0[...], (c1[...], c2[...], c3[...]))
        cost_sum = jnp.sum(total, axis=(0, 1), keepdims=True)
        rhs_sum = jnp.sum(rhs_square[...], axis=(0, 1), keepdims=True)
        ratio = jnp.sqrt((cost_sum + EPS) / (rhs_sum + EPS))
        steps[...] = jnp.zeros_like(steps)
        steps[0:1] = jnp.broadcast_to(STEP / ratio, (1, TILE))
        steps[1:2] = jnp.broadcast_to(STEP * ratio, (1, TILE))
    if index < ITERS - 1:
        rowout, fresh, racc, work = rest
    else:
        dual, rhs, rowf, local, link, dualout, rhsout, rowfout, p0, p1, p2, p3, racc, work = rest
        own = pl.ds(pl.multiple_of(place[2] * SHARE, SHARE), SHARE)
        for ref, out in ((dual, dualout), (rhs, rhsout), (rowf, rowfout)):
            out[...] = ref[own, :]
    for lo, hi, src, first in ((0, CT, loc, 0), (CT, OWN, mine, grad_at), (OWN, CW, other, grad_at)):
        at = slice(lo, hi)
        x, scale = primal[at], colf[at]
        grad = scale * src[first : first + hi - lo]
        new = jnp.clip(x - steps[0:1] * (cost[at] - grad), 0.0, upper[at])
        if index < ITERS - 1:
            fresh[at] = new
        elif lo == 0:
            local[...] = scale * new
        else:
            half = place[0] if lo == CT else 1 - place[0]
            link[pl.ds(pl.multiple_of(half * HALF, HALF), HALF), :] = scale * new
        split_to(work, scale * (2.0 * new - x), lo)
    racc[...] = jnp.zeros_like(racc)

    def visit(t, col, row):
        row_pass(tiles_ref, t, col, row, work, racc, jnp.add, False)

    each_tile(rows_ref, cols_ref, place, visit)
    if index < ITERS - 1:
        join_from(racc, rowout, 0, RT)
    else:
        for k, out in enumerate((p0, p1, p2, p3)):
            at = pl.ds(pl.multiple_of((place[2] ^ k) * SHARE, SHARE), SHARE)
            for w in range(2):
                out[:, w * LANES : (w + 1) * LANES] = racc[w, at, :]


def core_kernel(op, tiles_ref, colown, got, out):
    out[...] = op(colown[CT:OWN], got[...])


def merge_kernel(op, tiles_ref, own, r1, r2, r3, out):
    out[...] = tree(op, own[...], (r1[...], r2[...], r3[...]))


def merge_grad_kernel(place, tiles_ref, own, r1, r2, r3, gradown, gradgot, m0, m1, m2, m3, half):
    link = tree(jnp.maximum, own[...], (r1[...], r2[...], r3[...]))
    half[...] = gradown[CT:OWN] + gradgot[...]
    for k, out in enumerate((m0, m1, m2, m3)):
        out[0:HALF] = link
        out[HALF:] = half[pl.ds(pl.multiple_of((place[1] ^ k) * CHUNK, CHUNK), CHUNK), :]


def merge_chunk_kernel(tiles_ref, own, r1, r2, r3, link, chunk):
    link[...] = tree(jnp.maximum, own[0:HALF], (r1[0:HALF], r2[0:HALF], r3[0:HALF]))
    chunk[...] = tree(jnp.add, own[HALF:], (r1[HALF:], r2[HALF:], r3[HALF:]))


def rows_kernel(
    tiles_ref, r0, r1, r2, r3, rowold, rhs, dual, colown, got, colold, cost, chunk, rownew, rhs_scaled,
    dual_scaled, out,
):
    total = tree(jnp.add, r0[...], (r1[...], r2[...], r3[...]))
    old = rowold[...]
    new = old / jnp.sqrt(old * total + EPS)
    rownew[...] = new
    scaled = new * rhs[...]
    rhs_scaled[...] = scaled
    dual_scaled[...] = dual[...] / new
    out[0:HALF] = colown[CT:OWN] + got[...]
    out[HALF:OWN] = jnp.sum((scaled * scaled).reshape(RT // 8, 8, TILE), axis=0)
    old = colold[0:CT]
    part = old / jnp.sqrt(old * colown[0:CT] + EPS) * cost[...]
    out[OWN : OWN + CT] = part * part
    out[OWN + CT :] = chunk[...]


def merge_all_kernel(place, tiles_ref, own, r1, r2, r3, out):
    at = slice(0, HALF + EIGHT)
    out[at] = tree(jnp.add, own[at], (r1[at], r2[at], r3[at]))
    for k, ref in enumerate((own, r1, r2, r3)):
        start = pl.multiple_of((place[1] ^ k) * CHUNK, CHUNK)
        out[pl.ds(HALF + EIGHT + start, CHUNK), :] = ref[HALF + EIGHT :]


def setup_kernel(
    place, tiles_ref, own, back, colown, colold, cost_loc, cost_lnk, bound_loc, bound_lnk, start_loc, start_lnk,
    colnew, cost, upper, primal, rhs_square, cost_square,
):
    squares = own[HALF : HALF + EIGHT] + back[HALF : HALF + EIGHT]
    rhs_square[...] = squares[0:CT]
    sums = []
    for lo, hi, stat, half in (
        (0, CT, colown, None),
        (CT, OWN, own, place[0]),
        (OWN, CW, back, 1 - place[0]),
    ):
        at = slice(lo, hi)
        if half is None:
            c, b, x = cost_loc[...], bound_loc[...], start_loc[...]
        else:
            rows = pl.ds(pl.multiple_of(half * HALF, HALF), HALF)
            c, b, x = cost_lnk[rows, :], bound_lnk[rows, :], start_lnk[rows, :]
        old = colold[at]
        new = old / jnp.sqrt(old * stat[0 : hi - lo] + EPS)
        colnew[at] = new
        c = new * c
        cost[at] = c
        upper[at] = b / new
        primal[at] = x / new
        if half is not None:
            sums.append(jnp.sum((c * c).reshape(HALF // 8, 8, TILE), axis=0))
    cost_square[...] = squares[CT:] + (sums[0] + sums[1])


def end_kernel(steps, p0, p1, p2, p3, dual, rhs, rowf, out):
    total = tree(jnp.add, p0[...], (p1[...], p2[...], p3[...]))
    scale = rowf[...]
    out[...] = scale * (dual[...] + steps[1:2] * (rhs[...] - scale * total))


def body(
    tile_values,
    tile_rows,
    tile_cols,
    cost_local,
    cost_link,
    bound_local,
    bound_link,
    rhs,
    start_local,
    start_link,
    start_dual,
):
    scen = lax.axis_index("scen")
    core = scen % 2
    x_at, z_at = scen // 8, (scen // 2) % 4
    place = jnp.stack([core, jnp.where(core == 0, z_at, x_at), lax.axis_index("col")])
    ids = (tile_rows[0, 0], tile_cols[0, 0], place)

    def over(swap, x):
        got = {k: swap(x, k) for k in (2, 1, 3)}
        return x, got[1], got[2], got[3]

    row_part, colown, colother, tiles = first_stats(ids, tile_values[0, 0], rhs[0], start_dual[0])

    def run(kernel, smem, operands, outs, scratch=()):
        return call(kernel, smem, tiles, operands, outs, scratch)

    rows = over(swap_y, row_part)
    (link,) = run(functools.partial(core_kernel, jnp.maximum), (), (colown, swap_core(colother)), (HALF,))
    (link,) = run(functools.partial(merge_kernel, jnp.maximum), (), over(swap_first, link), (HALF,))
    (link,) = run(functools.partial(merge_kernel, jnp.maximum), (), over(swap_second, link), (HALF,))

    first_rows = rows
    row_part, colown, colother, row_scale, col_scale = run(
        second_stats_kernel,
        ids,
        (*rows, colown, link, swap_core(link)),
        (RT, OWN, HALF, RT, CW),
        (ROWS, COLS, ROWS, COLS),
    )
    rows = over(swap_y, row_part)
    (link,) = run(functools.partial(core_kernel, jnp.maximum), (), (colown, swap_core(colother)), (HALF,))
    got = over(swap_first, link)
    gradown, gradother, rhs_rows, dual_rows = run(
        first_backward_kernel, ids, (*first_rows, got[3]), (OWN, HALF, RT, RT), (COLS, ROWS)
    )
    sent = run(
        merge_grad_kernel,
        (place,),
        (*got, gradown, swap_core(gradother)),
        (HALF + CHUNK,) * 4,
        (pltpu.VMEM((HALF, TILE), F32),),
    )
    got = {k: swap_second(sent[k], k) for k in (2, 1, 3)}
    link, chunk = run(merge_chunk_kernel, (), (sent[0], got[1], got[2], got[3]), (HALF, CHUNK))

    row_part, row_scale, col_scale = run(
        third_rows_kernel,
        ids,
        (*rows, colown, link, swap_core(link), row_scale, col_scale),
        (RT, RT, CW),
        (ROWS, COLS),
    )
    rows = over(swap_y, row_part)
    colown, colother = run(third_columns_kernel, ids, (row_scale,), (OWN, HALF), (COLS, ROWS))
    row_scale, rhs_scaled, dual_scaled, both = run(
        rows_kernel,
        (),
        (*rows, row_scale, rhs_rows, dual_rows, colown, swap_core(colother), col_scale, cost_local[0, 0], chunk),
        (RT, RT, RT, HALF + EIGHT + CHUNK),
    )
    (both,) = run(
        functools.partial(merge_kernel, jnp.add), (), over(swap_first, both), (HALF + EIGHT + CHUNK,)
    )
    (mine,) = run(merge_all_kernel, (place,), over(swap_second, both), (LT + EIGHT,))
    other = swap_core(mine)
    col_scale, cost, upper, primal, rhs_square, cost_square = run(
        setup_kernel,
        (place,),
        (
            mine,
            other,
            colown,
            col_scale,
            cost_local[0, 0],
            cost_link[0],
            bound_local[0, 0],
            bound_link[0],
            start_local[0, 0],
            start_link[0],
        ),
        (CW, CW, CW, CW, CT, CT),
    )
    norms = (*over(swap_y, cost_square), rhs_square)

    grads, grad_at = (gradown, mine, other), HALF + EIGHT
    for index in range(ITERS):
        given = norms if index == 0 else (steps,)
        extra = (dual_scaled, rhs_scaled, row_scale) if index == ITERS - 1 else ()
        outs = (RT, CW) if index < ITERS - 1 else (CT, LT) + (SHARE,) * 7
        result = run(
            functools.partial(forward_kernel, index, grad_at),
            ids,
            (*given, *grads, primal, cost, upper, col_scale, *extra),
            ((CT,) if index == 0 else ()) + outs,
            (ROWS, COLS),
        )
        if index == 0:
            steps, *result = result
        if index == ITERS - 1:
            break
        row_part, primal = result
        colown, colother, dual_scaled = run(
            backward_kernel,
            ids,
            (steps, *over(swap_y, row_part), dual_scaled, rhs_scaled, row_scale),
            (OWN, HALF, RT),
            (COLS, ROWS),
        )
        (link,) = run(functools.partial(core_kernel, jnp.add), (), (colown, swap_core(colother)), (HALF,))
        (link,) = run(functools.partial(merge_kernel, jnp.add), (), over(swap_first, link), (HALF,))
        (link,) = run(functools.partial(merge_kernel, jnp.add), (), over(swap_second, link), (HALF,))
        grads, grad_at = (colown, link, swap_core(link)), 0

    local, link, dual, rhs_own, scale, *pieces = result
    got = {k: swap_y(pieces[k], k) for k in (2, 1, 3)}
    vmem = pl.BlockSpec(memory_space=pltpu.VMEM)
    multipliers = pl.pallas_call(
        end_kernel,
        out_shape=jax.ShapeDtypeStruct((SHARE, TILE), F32),
        in_specs=[vmem] * 8,
        out_specs=vmem,
        compiler_params=pltpu.CompilerParams(vmem_limit_bytes=1024 * 1024),
    )(steps, pieces[0], got[1], got[2], got[3], dual, rhs_own, scale)
    return local[None, None], link[None], multipliers[None]


def solution(mesh):
    placed = (
        P("scen", "col", None, None, None),
        P("scen", "col", None),
        P("scen", "col", None),
        P("scen", "col", None, None),
        P("col", None, None),
        P("scen", "col", None, None),
        P("col", None, None),
        P("scen", "col", None),
        P("scen", "col", None, None),
        P("col", None, None),
        P("scen", "col", None),
    )
    return jax.shard_map(
        body,
        mesh=mesh,
        in_specs=placed,
        out_specs=(P("scen", "col", None, None), P("col", None, None), P("scen", "col", None)),
        check_vma=False,
    )
```

```python
import functools

import jax
import jax.numpy as jnp
from jax import lax
from jax.experimental import pallas as pl
from jax.experimental.pallas import tpu as pltpu
from jax.sharding import PartitionSpec as P

TILE = 256
RT = 128
CT = 8
LT = 256
ITERS = 3
NT = 64
HALF = LT // 2
SHARE = RT // 4
CW = CT + LT
GROUP = 8
STEPS = NT // GROUP

EPS = 1e-06
STEP = 0.9
F32 = jnp.float32
LANES = 128
VMEM_LIMIT = 24 * 1024 * 1024


def swap_core(x):
    return lax.ppermute(x, "scen", [(i, i ^ 1) for i in range(32)])


def swap_first(x, k):
    return lax.ppermute(x, "scen", [(i, i ^ (k << (1 if i % 2 else 3))) for i in range(32)])


def swap_second(x, k):
    return lax.ppermute(x, "scen", [(i, i ^ (k << (3 if i % 2 else 1))) for i in range(32)])


def swap_y(x, k):
    return lax.ppermute(x, "col", [(i, i ^ k) for i in range(4)])


def tree(op, own, got):
    return op(op(own, got[0]), op(got[1], got[2]))


def row_pass(tiles_ref, t, col, row, colf_ref, rowout_ref, op, magnitude):
    for h in range(2):
        a = tiles_ref[t, h * LANES : (h + 1) * LANES, 0:LANES]
        b = tiles_ref[t, h * LANES : (h + 1) * LANES, LANES:TILE]
        if magnitude:
            a, b = jnp.abs(a), jnp.abs(b)
        if colf_ref is not None:
            a = a * colf_ref[0, pl.ds(col, 1), :]
            b = b * colf_ref[1, pl.ds(col, 1), :]
        m = op(a, b).T
        s = jnp.max(m, axis=0, keepdims=True) if op is jnp.maximum else jnp.sum(m, axis=0, keepdims=True)
        at = (h, pl.ds(row, 1), slice(None))
        rowout_ref[at] = op(rowout_ref[at], s)


def col_pass(tiles_ref, t, col, row, rowf_ref, colout_ref, op, magnitude):
    parts = [None, None]
    for h in range(2):
        if rowf_ref is not None:
            f = jnp.broadcast_to(rowf_ref[h, pl.ds(row, 1), :], (LANES, LANES)).T
        for w in range(2):
            a = tiles_ref[t, h * LANES : (h + 1) * LANES, w * LANES : (w + 1) * LANES]
            if magnitude:
                a = jnp.abs(a)
            if rowf_ref is not None:
                a = a * f
            a = a.reshape(16, 8, LANES)
            s = jnp.max(a, axis=0) if op is jnp.maximum else jnp.sum(a, axis=0)
            parts[w] = s if parts[w] is None else op(parts[w], s)
    for w in range(2):
        s = parts[w]
        s = jnp.max(s, axis=0, keepdims=True) if op is jnp.maximum else jnp.sum(s, axis=0, keepdims=True)
        at = (w, pl.ds(col, 1), slice(None))
        colout_ref[at] = op(colout_ref[at], s)


def split_to(ref, value, lo=0):
    for w in range(2):
        ref[w, lo : lo + value.shape[0], :] = value[:, w * LANES : (w + 1) * LANES]


def join_from(ref, out, lo, hi):
    for w in range(2):
        out[0 : hi - lo, w * LANES : (w + 1) * LANES] = ref[w, lo:hi, :]


ROWS = pltpu.VMEM((2, RT, LANES), F32)
COLS = pltpu.VMEM((2, CW, LANES), F32)
OWN = CT + HALF
EIGHT = 2 * CT
CHUNK = HALF // 4


def call(kernel, smem, tiles, operands, outs, scratch=()):
    operands = [pltpu.with_memory_space_constraint(tiles, pltpu.VMEM)] + list(operands)
    vmem = pl.BlockSpec(memory_space=pltpu.VMEM)
    return pl.pallas_call(
        kernel,
        out_shape=tuple(jax.ShapeDtypeStruct((n, TILE), F32) for n in outs),
        in_specs=[pl.BlockSpec(memory_space=pltpu.SMEM) for _ in smem] + [vmem for _ in operands],
        out_specs=tuple(vmem for _ in outs),
        scratch_shapes=list(scratch),
        compiler_params=pltpu.CompilerParams(vmem_limit_bytes=VMEM_LIMIT),
    )(*smem, *operands)


def each_tile(rows_ref, cols_ref, place_ref, visit, ready=None):
    turn = place_ref[0] * HALF

    def group(step, carry):
        if ready is not None:
            ready(step)
        for i in range(GROUP):
            t = step * GROUP + i
            col = cols_ref[t]
            col = jnp.where(col < CT, col, CT + ((col - CT) ^ turn))
            visit(t, col, rows_ref[t])
        return carry

    lax.fori_loop(0, STEPS, group, 0)


def put_columns(cacc, colown, colother):
    join_from(cacc, colown, 0, OWN)
    join_from(cacc, colother, OWN, CW)


def first_stats_kernel(
    place, rows_hbm, cols_hbm, source, rhs, dual, rowout, colown, colother, tiles_ref, racc, cacc,
    rows_ref, cols_ref, sems,
):
    indices = [
        pltpu.make_async_copy(src, dst, sems.at[STEPS + 2 + i])
        for i, (src, dst) in enumerate(((rows_hbm, rows_ref), (cols_hbm, cols_ref)))
    ]
    for copy in indices:
        copy.start()

    def load(step):
        part = pl.ds(step * GROUP, GROUP)
        return pltpu.make_async_copy(source.at[part], tiles_ref.at[part], sems.at[step])

    for step in range(STEPS):
        load(step).start()
    extra = [
        pltpu.make_async_copy(src, rowout.at[pl.ds(RT + i * SHARE, SHARE)], sems.at[STEPS + i])
        for i, src in enumerate((rhs, dual))
    ]
    for copy in extra:
        copy.start()
    racc[...] = jnp.zeros_like(racc)
    cacc[...] = jnp.zeros_like(cacc)

    for copy in indices:
        copy.wait()

    def visit(t, col, row):
        row_pass(tiles_ref, t, col, row, None, racc, jnp.maximum, True)
        col_pass(tiles_ref, t, col, row, None, cacc, jnp.maximum, True)

    each_tile(rows_ref, cols_ref, place, visit, lambda step: load(step).wait())
    join_from(racc, rowout, 0, RT)
    put_columns(cacc, colown, colother)
    for copy in extra:
        copy.wait()


def first_stats(ids, source, rhs, dual):
    vmem = pl.BlockSpec(memory_space=pltpu.VMEM)
    shapes = [jax.ShapeDtypeStruct((n, TILE), F32) for n in (RT + 2 * SHARE, OWN, HALF)]
    return pl.pallas_call(
        first_stats_kernel,
        out_shape=(*shapes, pltpu.VMEM((NT, TILE, TILE), F32)),
        in_specs=[pl.BlockSpec(memory_space=pltpu.SMEM)] + [pl.BlockSpec(memory_space=pltpu.HBM)] * 5,
        out_specs=(vmem,) * 4,
        scratch_shapes=[
            ROWS,
            COLS,
            pltpu.SMEM((NT,), jnp.int32),
            pltpu.SMEM((NT,), jnp.int32),
            pltpu.SemaphoreType.DMA((STEPS + 4,)),
        ],
        compiler_params=pltpu.CompilerParams(vmem_limit_bytes=VMEM_LIMIT),
    )(ids[2], *(pltpu.with_memory_space_constraint(x, pltpu.HBM) for x in (*ids[:2], source, rhs, dual)))


def second_stats_kernel(
    rows_ref, cols_ref, place, tiles_ref, r0, r1, r3, r2, loc, mine, other, rowout, colown, colother, rownew,
    colnew, racc, cacc, rowf, colf,
):
    row = tree(jnp.maximum, r0[0:RT], (r1[0:RT], r2[0:RT], r3[0:RT]))
    new = 1.0 / jnp.sqrt(row + EPS)
    rownew[...] = new
    split_to(rowf, new)
    for lo, hi, src in ((0, CT, loc), (CT, OWN, mine), (OWN, CW, other)):
        new = 1.0 / jnp.sqrt(src[0 : hi - lo] + EPS)
        colnew[lo:hi] = new
        split_to(colf, new, lo)
    racc[...] = jnp.zeros_like(racc)
    cacc[...] = jnp.zeros_like(cacc)

    def visit(t, col, row):
        row_pass(tiles_ref, t, col, row, colf, racc, jnp.maximum, True)
        col_pass(tiles_ref, t, col, row, rowf, cacc, jnp.maximum, True)

    each_tile(rows_ref, cols_ref, place, visit)
    join_from(racc, rowout, 0, RT)
    put_columns(cacc, colown, colother)


def third_rows_kernel(
    rows_ref, cols_ref, place, tiles_ref, r0, r1, r3, r2, loc, mine, other, rowold, colold, rowout, rownew,
    colnew, racc, colf,
):
    row = tree(jnp.maximum, r0[...], (r1[...], r2[...], r3[...]))
    old = rowold[...]
    rownew[...] = old / jnp.sqrt(old * row + EPS)
    for lo, hi, src in ((0, CT, loc), (CT, OWN, mine), (OWN, CW, other)):
        old = colold[lo:hi]
        new = old / jnp.sqrt(old * src[0 : hi - lo] + EPS)
        colnew[lo:hi] = new
        split_to(colf, new, lo)
    racc[...] = jnp.zeros_like(racc)

    def visit(t, col, row):
        row_pass(tiles_ref, t, col, row, colf, racc, jnp.add, True)

    each_tile(rows_ref, cols_ref, place, visit)
    join_from(racc, rowout, 0, RT)


def third_columns_kernel(rows_ref, cols_ref, place, tiles_ref, row_scale, colown, colother, cacc, rowf):
    split_to(rowf, row_scale[...])
    cacc[...] = jnp.zeros_like(cacc)

    def visit(t, col, row):
        col_pass(tiles_ref, t, col, row, rowf, cacc, jnp.add, True)

    each_tile(rows_ref, cols_ref, place, visit)
    put_columns(cacc, colown, colother)


def first_backward_kernel(
    rows_ref, cols_ref, place, tiles_ref, r0, r1, r3, r2, after, colown, colother, rhsout, dualout, cacc, work
):
    for k, ref in enumerate((r0, r1, r2, r3)):
        at = pl.ds(pl.multiple_of((place[2] ^ k) * SHARE, SHARE), SHARE)
        rhsout[at, :] = ref[RT : RT + SHARE]
        dualout[at, :] = ref[RT + SHARE :]
    split_to(work, dualout[...])
    cacc[...] = jnp.zeros_like(cacc)

    def visit(t, col, row):
        col_pass(tiles_ref, t, col, row, work, cacc, jnp.add, False)

    each_tile(rows_ref, cols_ref, place, visit)
    put_columns(cacc, colown, colother)


def backward_kernel(
    rows_ref, cols_ref, place, tiles_ref, steps, r0, r1, r3, r2, dual, rhs, rowf, colown, colother, dualnew,
    cacc, work,
):
    total = tree(jnp.add, r0[...], (r1[...], r2[...], r3[...]))
    new = dual[...] + steps[1:2] * (rhs[...] - rowf[...] * total)
    dualnew[...] = new
    split_to(work, rowf[...] * new)
    cacc[...] = jnp.zeros_like(cacc)

    def visit(t, col, row):
        col_pass(tiles_ref, t, col, row, work, cacc, jnp.add, False)

    each_tile(rows_ref, cols_ref, place, visit)
    put_columns(cacc, colown, colother)


def forward_kernel(index, grad_at, rows_ref, cols_ref, place, tiles_ref, *rest):
    if index == 0:
        c0, c1, c3, c2, rhs_square, *rest = rest
    else:
        steps, *rest = rest
    loc, mine, other, primal, cost, upper, colf, *rest = rest
    if index == 0:
        steps, *rest = rest
        total = tree(jnp.add, c0[...], (c1[...], c2[...], c3[...]))
        cost_sum = jnp.sum(total, axis=(0, 1), keepdims=True)
        rhs_sum = jnp.sum(rhs_square[...], axis=(0, 1), keepdims=True)
        ratio = jnp.sqrt((cost_sum + EPS) / (rhs_sum + EPS))
        steps[...] = jnp.zeros_like(steps)
        steps[0:1] = jnp.broadcast_to(STEP / ratio, (1, TILE))
        steps[1:2] = jnp.broadcast_to(STEP * ratio, (1, TILE))
    if index < ITERS - 1:
        rowout, fresh, racc, work = rest
    else:
        dual, rhs, rowf, local, link, dualout, rhsout, rowfout, p0, p1, p2, p3, racc, work = rest
        own = pl.ds(pl.multiple_of(place[2] * SHARE, SHARE), SHARE)
        for ref, out in ((dual, dualout), (rhs, rhsout), (rowf, rowfout)):
            out[...] = ref[own, :]
    for lo, hi, src, first in ((0, CT, loc, 0), (CT, OWN, mine, grad_at), (OWN, CW, other, grad_at)):
        at = slice(lo, hi)
        x, scale = primal[at], colf[at]
        grad = scale * src[first : first + hi - lo]
        new = jnp.clip(x - steps[0:1] * (cost[at] - grad), 0.0, upper[at])
        if index < ITERS - 1:
            fresh[at] = new
        elif lo == 0:
            local[...] = scale * new
        else:
            half = place[0] if lo == CT else 1 - place[0]
            link[pl.ds(pl.multiple_of(half * HALF, HALF), HALF), :] = scale * new
        split_to(work, scale * (2.0 * new - x), lo)
    racc[...] = jnp.zeros_like(racc)

    def visit(t, col, row):
        row_pass(tiles_ref, t, col, row, work, racc, jnp.add, False)

    each_tile(rows_ref, cols_ref, place, visit)
    if index < ITERS - 1:
        join_from(racc, rowout, 0, RT)
    else:
        for k, out in enumerate((p0, p1, p2, p3)):
            at = pl.ds(pl.multiple_of((place[2] ^ k) * SHARE, SHARE), SHARE)
            for w in range(2):
                out[:, w * LANES : (w + 1) * LANES] = racc[w, at, :]


def core_kernel(op, tiles_ref, colown, got, out):
    out[...] = op(colown[CT:OWN], got[...])


def merge_kernel(op, tiles_ref, own, r1, r3, r2, out):
    out[...] = tree(op, own[...], (r1[...], r2[...], r3[...]))


def merge_grad_kernel(place, tiles_ref, own, r1, r3, r2, gradown, gradgot, m0, m1, m2, m3, half):
    link = tree(jnp.maximum, own[...], (r1[...], r2[...], r3[...]))
    half[...] = gradown[CT:OWN] + gradgot[...]
    for k, out in enumerate((m0, m1, m2, m3)):
        out[0:HALF] = link
        out[HALF:] = half[pl.ds(pl.multiple_of((place[1] ^ k) * CHUNK, CHUNK), CHUNK), :]


def merge_chunk_kernel(tiles_ref, own, r2, r1, r3, link, chunk):
    link[...] = tree(jnp.maximum, own[0:HALF], (r1[0:HALF], r2[0:HALF], r3[0:HALF]))
    chunk[...] = tree(jnp.add, own[HALF:], (r1[HALF:], r2[HALF:], r3[HALF:]))


def rows_kernel(
    tiles_ref, r0, r1, r3, r2, rowold, rhs, dual, colown, got, colold, cost, chunk, rownew, rhs_scaled,
    dual_scaled, out,
):
    total = tree(jnp.add, r0[...], (r1[...], r2[...], r3[...]))
    old = rowold[...]
    new = old / jnp.sqrt(old * total + EPS)
    rownew[...] = new
    scaled = new * rhs[...]
    rhs_scaled[...] = scaled
    dual_scaled[...] = dual[...] / new
    out[0:HALF] = colown[CT:OWN] + got[...]
    out[HALF:OWN] = jnp.sum((scaled * scaled).reshape(RT // 8, 8, TILE), axis=0)
    old = colold[0:CT]
    part = old / jnp.sqrt(old * colown[0:CT] + EPS) * cost[...]
    out[OWN : OWN + CT] = part * part
    out[OWN + CT :] = chunk[...]


def merge_all_kernel(place, tiles_ref, own, r1, r3, r2, out):
    at = slice(0, HALF + EIGHT)
    out[at] = tree(jnp.add, own[at], (r1[at], r2[at], r3[at]))
    for k, ref in enumerate((own, r1, r2, r3)):
        start = pl.multiple_of((place[1] ^ k) * CHUNK, CHUNK)
        out[pl.ds(HALF + EIGHT + start, CHUNK), :] = ref[HALF + EIGHT :]


def setup_kernel(
    place, tiles_ref, own, back, colown, colold, cost_loc, cost_lnk, bound_loc, bound_lnk, start_loc, start_lnk,
    colnew, cost, upper, primal, rhs_square, cost_square,
):
    squares = own[HALF : HALF + EIGHT] + back[HALF : HALF + EIGHT]
    rhs_square[...] = squares[0:CT]
    sums = []
    for lo, hi, stat, half in (
        (0, CT, colown, None),
        (CT, OWN, own, place[0]),
        (OWN, CW, back, 1 - place[0]),
    ):
        at = slice(lo, hi)
        if half is None:
            c, b, x = cost_loc[...], bound_loc[...], start_loc[...]
        else:
            rows = pl.ds(pl.multiple_of(half * HALF, HALF), HALF)
            c, b, x = cost_lnk[rows, :], bound_lnk[rows, :], start_lnk[rows, :]
        old = colold[at]
        new = old / jnp.sqrt(old * stat[0 : hi - lo] + EPS)
        colnew[at] = new
        c = new * c
        cost[at] = c
        upper[at] = b / new
        primal[at] = x / new
        if half is not None:
            sums.append(jnp.sum((c * c).reshape(HALF // 8, 8, TILE), axis=0))
    cost_square[...] = squares[CT:] + (sums[0] + sums[1])


def end_kernel(steps, p0, p2, p1, p3, dual, rhs, rowf, out):
    total = tree(jnp.add, p0[...], (p1[...], p2[...], p3[...]))
    scale = rowf[...]
    out[...] = scale * (dual[...] + steps[1:2] * (rhs[...] - scale * total))


def body(
    tile_values,
    tile_rows,
    tile_cols,
    cost_local,
    cost_link,
    bound_local,
    bound_link,
    rhs,
    start_local,
    start_link,
    start_dual,
):
    scen = lax.axis_index("scen")
    core = scen % 2
    x_at, z_at = scen // 8, (scen // 2) % 4
    place = jnp.stack([core, jnp.where(core == 0, z_at, x_at), lax.axis_index("col")])
    ids = (tile_rows[0, 0], tile_cols[0, 0], place)

    def over(swap, x):
        got = {k: swap(x, k) for k in (2, 1, 3)}
        return x, got[1], got[3], got[2]

    row_part, colown, colother, tiles = first_stats(ids, tile_values[0, 0], rhs[0], start_dual[0])

    def run(kernel, smem, operands, outs, scratch=()):
        return call(kernel, smem, tiles, operands, outs, scratch)

    rows = over(swap_y, row_part)
    (link,) = run(functools.partial(core_kernel, jnp.maximum), (), (colown, swap_core(colother)), (HALF,))
    (link,) = run(functools.partial(merge_kernel, jnp.maximum), (), over(swap_first, link), (HALF,))
    (link,) = run(functools.partial(merge_kernel, jnp.maximum), (), over(swap_second, link), (HALF,))

    first_rows = rows
    row_part, colown, colother, row_scale, col_scale = run(
        second_stats_kernel,
        ids,
        (*rows, colown, link, swap_core(link)),
        (RT, OWN, HALF, RT, CW),
        (ROWS, COLS, ROWS, COLS),
    )
    rows = over(swap_y, row_part)
    (link,) = run(functools.partial(core_kernel, jnp.maximum), (), (colown, swap_core(colother)), (HALF,))
    got = over(swap_first, link)
    gradown, gradother, rhs_rows, dual_rows = run(
        first_backward_kernel, ids, (*first_rows, got[2]), (OWN, HALF, RT, RT), (COLS, ROWS)
    )
    sent = run(
        merge_grad_kernel,
        (place,),
        (*got, gradown, swap_core(gradother)),
        (HALF + CHUNK,) * 4,
        (pltpu.VMEM((HALF, TILE), F32),),
    )
    got = {k: swap_second(sent[k], k) for k in (2, 1, 3)}
    link, chunk = run(merge_chunk_kernel, (), (sent[0], got[2], got[1], got[3]), (HALF, CHUNK))

    row_part, row_scale, col_scale = run(
        third_rows_kernel,
        ids,
        (*rows, colown, link, swap_core(link), row_scale, col_scale),
        (RT, RT, CW),
        (ROWS, COLS),
    )
    rows = over(swap_y, row_part)
    colown, colother = run(third_columns_kernel, ids, (row_scale,), (OWN, HALF), (COLS, ROWS))
    row_scale, rhs_scaled, dual_scaled, both = run(
        rows_kernel,
        (),
        (*rows, row_scale, rhs_rows, dual_rows, colown, swap_core(colother), col_scale, cost_local[0, 0], chunk),
        (RT, RT, RT, HALF + EIGHT + CHUNK),
    )
    (both,) = run(
        functools.partial(merge_kernel, jnp.add), (), over(swap_first, both), (HALF + EIGHT + CHUNK,)
    )
    (mine,) = run(merge_all_kernel, (place,), over(swap_second, both), (LT + EIGHT,))
    other = swap_core(mine)
    col_scale, cost, upper, primal, rhs_square, cost_square = run(
        setup_kernel,
        (place,),
        (
            mine,
            other,
            colown,
            col_scale,
            cost_local[0, 0],
            cost_link[0],
            bound_local[0, 0],
            bound_link[0],
            start_local[0, 0],
            start_link[0],
        ),
        (CW, CW, CW, CW, CT, CT),
    )
    norms = (*over(swap_y, cost_square), rhs_square)

    grads, grad_at = (gradown, mine, other), HALF + EIGHT
    for index in range(ITERS):
        given = norms if index == 0 else (steps,)
        extra = (dual_scaled, rhs_scaled, row_scale) if index == ITERS - 1 else ()
        outs = (RT, CW) if index < ITERS - 1 else (CT, LT) + (SHARE,) * 7
        result = run(
            functools.partial(forward_kernel, index, grad_at),
            ids,
            (*given, *grads, primal, cost, upper, col_scale, *extra),
            ((CT,) if index == 0 else ()) + outs,
            (ROWS, COLS),
        )
        if index == 0:
            steps, *result = result
        if index == ITERS - 1:
            break
        row_part, primal = result
        colown, colother, dual_scaled = run(
            backward_kernel,
            ids,
            (steps, *over(swap_y, row_part), dual_scaled, rhs_scaled, row_scale),
            (OWN, HALF, RT),
            (COLS, ROWS),
        )
        (link,) = run(functools.partial(core_kernel, jnp.add), (), (colown, swap_core(colother)), (HALF,))
        (link,) = run(functools.partial(merge_kernel, jnp.add), (), over(swap_first, link), (HALF,))
        (link,) = run(functools.partial(merge_kernel, jnp.add), (), over(swap_second, link), (HALF,))
        grads, grad_at = (colown, link, swap_core(link)), 0

    local, link, dual, rhs_own, scale, *pieces = result
    got = {k: swap_y(pieces[k], k) for k in (2, 1, 3)}
    vmem = pl.BlockSpec(memory_space=pltpu.VMEM)
    multipliers = pl.pallas_call(
        end_kernel,
        out_shape=jax.ShapeDtypeStruct((SHARE, TILE), F32),
        in_specs=[vmem] * 8,
        out_specs=vmem,
        compiler_params=pltpu.CompilerParams(vmem_limit_bytes=1024 * 1024),
    )(steps, pieces[0], got[2], got[1], got[3], dual, rhs_own, scale)
    return local[None, None], link[None], multipliers[None]


def solution(mesh):
    placed = (
        P("scen", "col", None, None, None),
        P("scen", "col", None),
        P("scen", "col", None),
        P("scen", "col", None, None),
        P("col", None, None),
        P("scen", "col", None, None),
        P("col", None, None),
        P("scen", "col", None),
        P("scen", "col", None, None),
        P("col", None, None),
        P("scen", "col", None),
    )
    return jax.shard_map(
        body,
        mesh=mesh,
        in_specs=placed,
        out_specs=(P("scen", "col", None, None), P("col", None, None), P("scen", "col", None)),
        check_vma=False,
    )
```

```python
import functools

import jax
import jax.numpy as jnp
from jax import lax
from jax.experimental import pallas as pl
from jax.experimental.pallas import tpu as pltpu
from jax.sharding import PartitionSpec as P

TILE = 256
RT = 128
CT = 8
LT = 256
ITERS = 3
NT = 64
HALF = LT // 2
SHARE = RT // 4
CW = CT + LT
GROUP = 8
STEPS = NT // GROUP

EPS = 1e-06
STEP = 0.9
F32 = jnp.float32
LANES = 128
VMEM_LIMIT = 24 * 1024 * 1024


def swap_core(x):
    return lax.ppermute(x, "scen", [(i, i ^ 1) for i in range(32)])


def swap_first(x, k):
    return lax.ppermute(x, "scen", [(i, i ^ (k << (1 if i % 2 else 3))) for i in range(32)])


def swap_second(x, k):
    return lax.ppermute(x, "scen", [(i, i ^ (k << (3 if i % 2 else 1))) for i in range(32)])


def swap_y(x, k):
    return lax.ppermute(x, "col", [(i, i ^ k) for i in range(4)])


def tree(op, own, got):
    return op(op(own, got[0]), op(got[1], got[2]))


def row_pass(tiles_ref, t, col, row, colf_ref, rowout_ref, op, magnitude):
    for h in range(2):
        a = tiles_ref[t, h * LANES : (h + 1) * LANES, 0:LANES]
        b = tiles_ref[t, h * LANES : (h + 1) * LANES, LANES:TILE]
        if magnitude:
            a, b = jnp.abs(a), jnp.abs(b)
        if colf_ref is not None:
            a = a * colf_ref[0, pl.ds(col, 1), :]
            b = b * colf_ref[1, pl.ds(col, 1), :]
        m = op(a, b).T
        s = jnp.max(m, axis=0, keepdims=True) if op is jnp.maximum else jnp.sum(m, axis=0, keepdims=True)
        at = (h, pl.ds(row, 1), slice(None))
        rowout_ref[at] = op(rowout_ref[at], s)


def col_pass(tiles_ref, t, col, row, rowf_ref, colout_ref, op, magnitude):
    parts = [None, None]
    for h in range(2):
        if rowf_ref is not None:
            f = jnp.broadcast_to(rowf_ref[h, pl.ds(row, 1), :], (LANES, LANES)).T
        for w in range(2):
            a = tiles_ref[t, h * LANES : (h + 1) * LANES, w * LANES : (w + 1) * LANES]
            if magnitude:
                a = jnp.abs(a)
            if rowf_ref is not None:
                a = a * f
            a = a.reshape(16, 8, LANES)
            s = jnp.max(a, axis=0) if op is jnp.maximum else jnp.sum(a, axis=0)
            parts[w] = s if parts[w] is None else op(parts[w], s)
    for w in range(2):
        s = parts[w]
        s = jnp.max(s, axis=0, keepdims=True) if op is jnp.maximum else jnp.sum(s, axis=0, keepdims=True)
        at = (w, pl.ds(col, 1), slice(None))
        colout_ref[at] = op(colout_ref[at], s)


def split_to(ref, value, lo=0):
    for w in range(2):
        ref[w, lo : lo + value.shape[0], :] = value[:, w * LANES : (w + 1) * LANES]


def join_from(ref, out, lo, hi):
    for w in range(2):
        out[0 : hi - lo, w * LANES : (w + 1) * LANES] = ref[w, lo:hi, :]


ROWS = pltpu.VMEM((2, RT, LANES), F32)
COLS = pltpu.VMEM((2, CW, LANES), F32)
OWN = CT + HALF
EIGHT = 2 * CT
CHUNK = HALF // 4


def call(kernel, smem, tiles, operands, outs, scratch=()):
    operands = [pltpu.with_memory_space_constraint(tiles, pltpu.VMEM)] + list(operands)
    vmem = pl.BlockSpec(memory_space=pltpu.VMEM)
    return pl.pallas_call(
        kernel,
        out_shape=tuple(jax.ShapeDtypeStruct((n, TILE), F32) for n in outs),
        in_specs=[pl.BlockSpec(memory_space=pltpu.SMEM) for _ in smem] + [vmem for _ in operands],
        out_specs=tuple(vmem for _ in outs),
        scratch_shapes=list(scratch),
        compiler_params=pltpu.CompilerParams(vmem_limit_bytes=VMEM_LIMIT),
    )(*smem, *operands)


def each_tile(rows_ref, cols_ref, place_ref, visit, ready=None):
    turn = place_ref[0] * HALF

    def group(step, carry):
        if ready is not None:
            ready(step)
        for i in range(GROUP):
            t = step * GROUP + i
            col = cols_ref[t]
            col = jnp.where(col < CT, col, CT + ((col - CT) ^ turn))
            visit(t, col, rows_ref[t])
        return carry

    lax.fori_loop(0, STEPS, group, 0)


def put_columns(cacc, colown, colother):
    join_from(cacc, colown, 0, OWN)
    join_from(cacc, colother, OWN, CW)


def first_stats_kernel(
    place, rows_hbm, cols_hbm, source, rhs, dual, rowout, colown, colother, tiles_ref, racc, cacc,
    rows_ref, cols_ref, sems,
):
    indices = [
        pltpu.make_async_copy(src, dst, sems.at[STEPS + 2 + i])
        for i, (src, dst) in enumerate(((rows_hbm, rows_ref), (cols_hbm, cols_ref)))
    ]
    for copy in indices:
        copy.start()

    def load(step):
        part = pl.ds(step * GROUP, GROUP)
        return pltpu.make_async_copy(source.at[part], tiles_ref.at[part], sems.at[step])

    for step in range(STEPS):
        load(step).start()
    extra = [
        pltpu.make_async_copy(src, rowout.at[pl.ds(RT + i * SHARE, SHARE)], sems.at[STEPS + i])
        for i, src in enumerate((rhs, dual))
    ]
    for copy in extra:
        copy.start()
    racc[...] = jnp.zeros_like(racc)
    cacc[...] = jnp.zeros_like(cacc)

    for copy in indices:
        copy.wait()

    def visit(t, col, row):
        row_pass(tiles_ref, t, col, row, None, racc, jnp.maximum, True)
        col_pass(tiles_ref, t, col, row, None, cacc, jnp.maximum, True)

    each_tile(rows_ref, cols_ref, place, visit, lambda step: load(step).wait())
    join_from(racc, rowout, 0, RT)
    put_columns(cacc, colown, colother)
    for copy in extra:
        copy.wait()


def first_stats(ids, source, rhs, dual):
    vmem = pl.BlockSpec(memory_space=pltpu.VMEM)
    shapes = [jax.ShapeDtypeStruct((n, TILE), F32) for n in (RT + 2 * SHARE, OWN, HALF)]
    return pl.pallas_call(
        first_stats_kernel,
        out_shape=(*shapes, pltpu.VMEM((NT, TILE, TILE), F32)),
        in_specs=[pl.BlockSpec(memory_space=pltpu.SMEM)] + [pl.BlockSpec(memory_space=pltpu.HBM)] * 5,
        out_specs=(vmem,) * 4,
        scratch_shapes=[
            ROWS,
            COLS,
            pltpu.SMEM((NT,), jnp.int32),
            pltpu.SMEM((NT,), jnp.int32),
            pltpu.SemaphoreType.DMA((STEPS + 4,)),
        ],
        compiler_params=pltpu.CompilerParams(vmem_limit_bytes=VMEM_LIMIT),
    )(ids[2], *(pltpu.with_memory_space_constraint(x, pltpu.HBM) for x in (*ids[:2], source, rhs, dual)))


def second_stats_kernel(
    rows_ref, cols_ref, place, tiles_ref, r0, r1, r3, r2, loc, mine, other, rowout, colown, colother, rownew,
    colnew, racc, cacc, rowf, colf,
):
    row = tree(jnp.maximum, r0[0:RT], (r1[0:RT], r2[0:RT], r3[0:RT]))
    new = 1.0 / jnp.sqrt(row + EPS)
    rownew[...] = new
    split_to(rowf, new)
    for lo, hi, src in ((0, CT, loc), (CT, OWN, mine), (OWN, CW, other)):
        new = 1.0 / jnp.sqrt(src[0 : hi - lo] + EPS)
        colnew[lo:hi] = new
        split_to(colf, new, lo)
    racc[...] = jnp.zeros_like(racc)
    cacc[...] = jnp.zeros_like(cacc)

    def visit(t, col, row):
        row_pass(tiles_ref, t, col, row, colf, racc, jnp.maximum, True)
        col_pass(tiles_ref, t, col, row, rowf, cacc, jnp.maximum, True)

    each_tile(rows_ref, cols_ref, place, visit)
    join_from(racc, rowout, 0, RT)
    put_columns(cacc, colown, colother)


def third_rows_kernel(
    rows_ref, cols_ref, place, tiles_ref, r0, r1, r3, r2, loc, mine, other, rowold, colold, rowout, rownew,
    colnew, racc, colf,
):
    row = tree(jnp.maximum, r0[...], (r1[...], r2[...], r3[...]))
    old = rowold[...]
    rownew[...] = old / jnp.sqrt(old * row + EPS)
    for lo, hi, src in ((0, CT, loc), (CT, OWN, mine), (OWN, CW, other)):
        old = colold[lo:hi]
        new = old / jnp.sqrt(old * src[0 : hi - lo] + EPS)
        colnew[lo:hi] = new
        split_to(colf, new, lo)
    racc[...] = jnp.zeros_like(racc)

    def visit(t, col, row):
        row_pass(tiles_ref, t, col, row, colf, racc, jnp.add, True)

    each_tile(rows_ref, cols_ref, place, visit)
    join_from(racc, rowout, 0, RT)


def third_columns_kernel(rows_ref, cols_ref, place, tiles_ref, row_scale, colown, colother, cacc, rowf):
    split_to(rowf, row_scale[...])
    cacc[...] = jnp.zeros_like(cacc)

    def visit(t, col, row):
        col_pass(tiles_ref, t, col, row, rowf, cacc, jnp.add, True)

    each_tile(rows_ref, cols_ref, place, visit)
    put_columns(cacc, colown, colother)


def first_backward_kernel(
    rows_ref, cols_ref, place, tiles_ref, r0, r1, r3, r2, after, colown, colother, rhsout, dualout, cacc, work
):
    for k, ref in enumerate((r0, r1, r2, r3)):
        at = pl.ds(pl.multiple_of((place[2] ^ k) * SHARE, SHARE), SHARE)
        rhsout[at, :] = ref[RT : RT + SHARE]
        dualout[at, :] = ref[RT + SHARE :]
    split_to(work, dualout[...])
    cacc[...] = jnp.zeros_like(cacc)

    def visit(t, col, row):
        col_pass(tiles_ref, t, col, row, work, cacc, jnp.add, False)

    each_tile(rows_ref, cols_ref, place, visit)
    put_columns(cacc, colown, colother)


def backward_kernel(
    rows_ref, cols_ref, place, tiles_ref, steps, r0, r1, r3, r2, dual, rhs, rowf, colown, colother, dualnew,
    cacc, work,
):
    total = tree(jnp.add, r0[...], (r1[...], r2[...], r3[...]))
    new = dual[...] + steps[1:2] * (rhs[...] - rowf[...] * total)
    dualnew[...] = new
    split_to(work, rowf[...] * new)
    cacc[...] = jnp.zeros_like(cacc)

    def visit(t, col, row):
        col_pass(tiles_ref, t, col, row, work, cacc, jnp.add, False)

    each_tile(rows_ref, cols_ref, place, visit)
    put_columns(cacc, colown, colother)


def forward_kernel(index, grad_at, rows_ref, cols_ref, place, tiles_ref, *rest):
    if index == 0:
        c0, c1, c3, c2, rhs_square, *rest = rest
    else:
        steps, *rest = rest
    loc, mine, other, primal, cost, upper, colf, *rest = rest
    if index == 0:
        steps, *rest = rest
        total = tree(jnp.add, c0[...], (c1[...], c2[...], c3[...]))
        cost_sum = jnp.sum(total, axis=(0, 1), keepdims=True)
        rhs_sum = jnp.sum(rhs_square[...], axis=(0, 1), keepdims=True)
        ratio = jnp.sqrt((cost_sum + EPS) / (rhs_sum + EPS))
        steps[...] = jnp.zeros_like(steps)
        steps[0:1] = jnp.broadcast_to(STEP / ratio, (1, TILE))
        steps[1:2] = jnp.broadcast_to(STEP * ratio, (1, TILE))
    if index < ITERS - 1:
        rowout, fresh, racc, work = rest
    else:
        dual, rhs, rowf, local, link, dualout, rhsout, rowfout, p0, p1, p2, p3, racc, work = rest
        own = pl.ds(pl.multiple_of(place[2] * SHARE, SHARE), SHARE)
        for ref, out in ((dual, dualout), (rhs, rhsout), (rowf, rowfout)):
            out[...] = ref[own, :]
    for lo, hi, src, first in ((0, CT, loc, 0), (CT, OWN, mine, grad_at), (OWN, CW, other, grad_at)):
        at = slice(lo, hi)
        x, scale = primal[at], colf[at]
        grad = scale * src[first : first + hi - lo]
        new = jnp.clip(x - steps[0:1] * (cost[at] - grad), 0.0, upper[at])
        if index < ITERS - 1:
            fresh[at] = new
        elif lo == 0:
            local[...] = scale * new
        else:
            half = place[0] if lo == CT else 1 - place[0]
            link[pl.ds(pl.multiple_of(half * HALF, HALF), HALF), :] = scale * new
        split_to(work, scale * (2.0 * new - x), lo)
    racc[...] = jnp.zeros_like(racc)

    def visit(t, col, row):
        row_pass(tiles_ref, t, col, row, work, racc, jnp.add, False)

    each_tile(rows_ref, cols_ref, place, visit)
    if index < ITERS - 1:
        join_from(racc, rowout, 0, RT)
    else:
        for k, out in enumerate((p0, p1, p2, p3)):
            at = pl.ds(pl.multiple_of((place[2] ^ k) * SHARE, SHARE), SHARE)
            for w in range(2):
                out[:, w * LANES : (w + 1) * LANES] = racc[w, at, :]


def core_kernel(op, tiles_ref, colown, got, out):
    out[...] = op(colown[CT:OWN], got[...])


def merge_kernel(op, tiles_ref, own, r1, r3, r2, out):
    out[...] = tree(op, own[...], (r1[...], r2[...], r3[...]))


def merge_after_kernel(tiles_ref, own, r1, r3, r2, after, out):
    out[...] = tree(jnp.maximum, own[...], (r1[...], r2[...], r3[...]))


def merge_grad_kernel(place, tiles_ref, own, r1, r3, r2, gradown, gradgot, after, m0, m1, m2, m3, half):
    link = tree(jnp.maximum, own[...], (r1[...], r2[...], r3[...]))
    half[...] = gradown[CT:OWN] + gradgot[...]
    for k, out in enumerate((m0, m1, m2, m3)):
        out[0:HALF] = link
        out[HALF:] = half[pl.ds(pl.multiple_of((place[1] ^ k) * CHUNK, CHUNK), CHUNK), :]


def merge_chunk_kernel(tiles_ref, own, r2, r1, r3, link, chunk):
    link[...] = tree(jnp.maximum, own[0:HALF], (r1[0:HALF], r2[0:HALF], r3[0:HALF]))
    chunk[...] = tree(jnp.add, own[HALF:], (r1[HALF:], r2[HALF:], r3[HALF:]))


def rows_kernel(
    tiles_ref, r0, r1, r3, r2, rowold, rhs, dual, colown, got, colold, cost, chunk, rownew, rhs_scaled,
    dual_scaled, out,
):
    total = tree(jnp.add, r0[...], (r1[...], r2[...], r3[...]))
    old = rowold[...]
    new = old / jnp.sqrt(old * total + EPS)
    rownew[...] = new
    scaled = new * rhs[...]
    rhs_scaled[...] = scaled
    dual_scaled[...] = dual[...] / new
    out[0:HALF] = colown[CT:OWN] + got[...]
    out[HALF:OWN] = jnp.sum((scaled * scaled).reshape(RT // 8, 8, TILE), axis=0)
    old = colold[0:CT]
    part = old / jnp.sqrt(old * colown[0:CT] + EPS) * cost[...]
    out[OWN : OWN + CT] = part * part
    out[OWN + CT :] = chunk[...]


def merge_all_kernel(place, tiles_ref, own, r1, r3, r2, out):
    at = slice(0, HALF + EIGHT)
    out[at] = tree(jnp.add, own[at], (r1[at], r2[at], r3[at]))
    for k, ref in enumerate((own, r1, r2, r3)):
        start = pl.multiple_of((place[1] ^ k) * CHUNK, CHUNK)
        out[pl.ds(HALF + EIGHT + start, CHUNK), :] = ref[HALF + EIGHT :]


def setup_kernel(
    place, tiles_ref, own, back, colown, colold, cost_loc, cost_lnk, bound_loc, bound_lnk, start_loc, start_lnk,
    colnew, cost, upper, primal, rhs_square, cost_square,
):
    squares = own[HALF : HALF + EIGHT] + back[HALF : HALF + EIGHT]
    rhs_square[...] = squares[0:CT]
    sums = []
    for lo, hi, stat, half in (
        (0, CT, colown, None),
        (CT, OWN, own, place[0]),
        (OWN, CW, back, 1 - place[0]),
    ):
        at = slice(lo, hi)
        if half is None:
            c, b, x = cost_loc[...], bound_loc[...], start_loc[...]
        else:
            rows = pl.ds(pl.multiple_of(half * HALF, HALF), HALF)
            c, b, x = cost_lnk[rows, :], bound_lnk[rows, :], start_lnk[rows, :]
        old = colold[at]
        new = old / jnp.sqrt(old * stat[0 : hi - lo] + EPS)
        colnew[at] = new
        c = new * c
        cost[at] = c
        upper[at] = b / new
        primal[at] = x / new
        if half is not None:
            sums.append(jnp.sum((c * c).reshape(HALF // 8, 8, TILE), axis=0))
    cost_square[...] = squares[CT:] + (sums[0] + sums[1])


def end_kernel(steps, p0, p2, p1, p3, dual, rhs, rowf, out):
    total = tree(jnp.add, p0[...], (p1[...], p2[...], p3[...]))
    scale = rowf[...]
    out[...] = scale * (dual[...] + steps[1:2] * (rhs[...] - scale * total))


def body(
    tile_values,
    tile_rows,
    tile_cols,
    cost_local,
    cost_link,
    bound_local,
    bound_link,
    rhs,
    start_local,
    start_link,
    start_dual,
):
    scen = lax.axis_index("scen")
    core = scen % 2
    x_at, z_at = scen // 8, (scen // 2) % 4
    place = jnp.stack([core, jnp.where(core == 0, z_at, x_at), lax.axis_index("col")])
    ids = (tile_rows[0, 0], tile_cols[0, 0], place)

    def over(swap, x):
        got = {k: swap(x, k) for k in (2, 1, 3)}
        return x, got[1], got[3], got[2]

    row_part, colown, colother, tiles = first_stats(ids, tile_values[0, 0], rhs[0], start_dual[0])

    def run(kernel, smem, operands, outs, scratch=()):
        return call(kernel, smem, tiles, operands, outs, scratch)

    rows = over(swap_y, row_part)
    (link,) = run(functools.partial(core_kernel, jnp.maximum), (), (colown, swap_core(colother)), (HALF,))
    (link,) = run(merge_after_kernel, (), (*over(swap_first, link), rows[3]), (HALF,))
    (link,) = run(functools.partial(merge_kernel, jnp.maximum), (), over(swap_second, link), (HALF,))

    first_rows = rows
    row_part, colown, colother, row_scale, col_scale = run(
        second_stats_kernel,
        ids,
        (*rows, colown, link, swap_core(link)),
        (RT, OWN, HALF, RT, CW),
        (ROWS, COLS, ROWS, COLS),
    )
    rows = over(swap_y, row_part)
    (link,) = run(functools.partial(core_kernel, jnp.maximum), (), (colown, swap_core(colother)), (HALF,))
    got = over(swap_first, link)
    gradown, gradother, rhs_rows, dual_rows = run(
        first_backward_kernel, ids, (*first_rows, got[2]), (OWN, HALF, RT, RT), (COLS, ROWS)
    )
    sent = run(
        merge_grad_kernel,
        (place,),
        (*got, gradown, swap_core(gradother), rows[3]),
        (HALF + CHUNK,) * 4,
        (pltpu.VMEM((HALF, TILE), F32),),
    )
    got = {k: swap_second(sent[k], k) for k in (2, 1, 3)}
    link, chunk = run(merge_chunk_kernel, (), (sent[0], got[2], got[1], got[3]), (HALF, CHUNK))

    row_part, row_scale, col_scale = run(
        third_rows_kernel,
        ids,
        (*rows, colown, link, swap_core(link), row_scale, col_scale),
        (RT, RT, CW),
        (ROWS, COLS),
    )
    rows = over(swap_y, row_part)
    colown, colother = run(third_columns_kernel, ids, (row_scale,), (OWN, HALF), (COLS, ROWS))
    row_scale, rhs_scaled, dual_scaled, both = run(
        rows_kernel,
        (),
        (*rows, row_scale, rhs_rows, dual_rows, colown, swap_core(colother), col_scale, cost_local[0, 0], chunk),
        (RT, RT, RT, HALF + EIGHT + CHUNK),
    )
    (both,) = run(
        functools.partial(merge_kernel, jnp.add), (), over(swap_first, both), (HALF + EIGHT + CHUNK,)
    )
    (mine,) = run(merge_all_kernel, (place,), over(swap_second, both), (LT + EIGHT,))
    other = swap_core(mine)
    col_scale, cost, upper, primal, rhs_square, cost_square = run(
        setup_kernel,
        (place,),
        (
            mine,
            other,
            colown,
            col_scale,
            cost_local[0, 0],
            cost_link[0],
            bound_local[0, 0],
            bound_link[0],
            start_local[0, 0],
            start_link[0],
        ),
        (CW, CW, CW, CW, CT, CT),
    )
    norms = (*over(swap_y, cost_square), rhs_square)

    grads, grad_at = (gradown, mine, other), HALF + EIGHT
    for index in range(ITERS):
        given = norms if index == 0 else (steps,)
        extra = (dual_scaled, rhs_scaled, row_scale) if index == ITERS - 1 else ()
        outs = (RT, CW) if index < ITERS - 1 else (CT, LT) + (SHARE,) * 7
        result = run(
            functools.partial(forward_kernel, index, grad_at),
            ids,
            (*given, *grads, primal, cost, upper, col_scale, *extra),
            ((CT,) if index == 0 else ()) + outs,
            (ROWS, COLS),
        )
        if index == 0:
            steps, *result = result
        if index == ITERS - 1:
            break
        row_part, primal = result
        colown, colother, dual_scaled = run(
            backward_kernel,
            ids,
            (steps, *over(swap_y, row_part), dual_scaled, rhs_scaled, row_scale),
            (OWN, HALF, RT),
            (COLS, ROWS),
        )
        (link,) = run(functools.partial(core_kernel, jnp.add), (), (colown, swap_core(colother)), (HALF,))
        (link,) = run(functools.partial(merge_kernel, jnp.add), (), over(swap_first, link), (HALF,))
        (link,) = run(functools.partial(merge_kernel, jnp.add), (), over(swap_second, link), (HALF,))
        grads, grad_at = (colown, link, swap_core(link)), 0

    local, link, dual, rhs_own, scale, *pieces = result
    got = {k: swap_y(pieces[k], k) for k in (2, 1, 3)}
    vmem = pl.BlockSpec(memory_space=pltpu.VMEM)
    multipliers = pl.pallas_call(
        end_kernel,
        out_shape=jax.ShapeDtypeStruct((SHARE, TILE), F32),
        in_specs=[vmem] * 8,
        out_specs=vmem,
        compiler_params=pltpu.CompilerParams(vmem_limit_bytes=1024 * 1024),
    )(steps, pieces[0], got[2], got[1], got[3], dual, rhs_own, scale)
    return local[None, None], link[None], multipliers[None]


def solution(mesh):
    placed = (
        P("scen", "col", None, None, None),
        P("scen", "col", None),
        P("scen", "col", None),
        P("scen", "col", None, None),
        P("col", None, None),
        P("scen", "col", None, None),
        P("col", None, None),
        P("scen", "col", None),
        P("scen", "col", None, None),
        P("col", None, None),
        P("scen", "col", None),
    )
    return jax.shard_map(
        body,
        mesh=mesh,
        in_specs=placed,
        out_specs=(P("scen", "col", None, None), P("col", None, None), P("scen", "col", None)),
        check_vma=False,
    )
```

```python
import functools

import jax
import jax.numpy as jnp
from jax import lax
from jax.experimental import pallas as pl
from jax.experimental.pallas import tpu as pltpu
from jax.sharding import PartitionSpec as P

TILE = 256
RT = 128
CT = 8
LT = 256
ITERS = 3
NT = 64
HALF = LT // 2
SHARE = RT // 4
CW = CT + LT
GROUP = 8
STEPS = NT // GROUP

EPS = 1e-06
STEP = 0.9
F32 = jnp.float32
LANES = 128
VMEM_LIMIT = 24 * 1024 * 1024


def swap_core(x):
    return lax.ppermute(x, "scen", [(i, i ^ 1) for i in range(32)])


def swap_first(x, k):
    return lax.ppermute(x, "scen", [(i, i ^ (k << (1 if i % 2 else 3))) for i in range(32)])


def swap_second(x, k):
    return lax.ppermute(x, "scen", [(i, i ^ (k << (3 if i % 2 else 1))) for i in range(32)])


def swap_y(x, k):
    return lax.ppermute(x, "col", [(i, i ^ k) for i in range(4)])


def tree(op, own, got):
    return op(op(own, got[0]), op(got[1], got[2]))


def row_pass(tiles_ref, t, col, row, colf_ref, rowout_ref, op, magnitude):
    for h in range(2):
        a = tiles_ref[t, h * LANES : (h + 1) * LANES, 0:LANES]
        b = tiles_ref[t, h * LANES : (h + 1) * LANES, LANES:TILE]
        if magnitude:
            a, b = jnp.abs(a), jnp.abs(b)
        if colf_ref is not None:
            a = a * colf_ref[0, pl.ds(col, 1), :]
            b = b * colf_ref[1, pl.ds(col, 1), :]
        m = op(a, b).T
        s = jnp.max(m, axis=0, keepdims=True) if op is jnp.maximum else jnp.sum(m, axis=0, keepdims=True)
        at = (h, pl.ds(row, 1), slice(None))
        rowout_ref[at] = op(rowout_ref[at], s)


def col_pass(tiles_ref, t, col, row, rowf_ref, colout_ref, op, magnitude):
    parts = [None, None]
    for h in range(2):
        if rowf_ref is not None:
            f = jnp.broadcast_to(rowf_ref[h, pl.ds(row, 1), :], (LANES, LANES)).T
        for w in range(2):
            a = tiles_ref[t, h * LANES : (h + 1) * LANES, w * LANES : (w + 1) * LANES]
            if magnitude:
                a = jnp.abs(a)
            if rowf_ref is not None:
                a = a * f
            a = a.reshape(16, 8, LANES)
            s = jnp.max(a, axis=0) if op is jnp.maximum else jnp.sum(a, axis=0)
            parts[w] = s if parts[w] is None else op(parts[w], s)
    for w in range(2):
        s = parts[w]
        s = jnp.max(s, axis=0, keepdims=True) if op is jnp.maximum else jnp.sum(s, axis=0, keepdims=True)
        at = (w, pl.ds(col, 1), slice(None))
        colout_ref[at] = op(colout_ref[at], s)


def split_to(ref, value, lo=0):
    for w in range(2):
        ref[w, lo : lo + value.shape[0], :] = value[:, w * LANES : (w + 1) * LANES]


def join_from(ref, out, lo, hi):
    for w in range(2):
        out[0 : hi - lo, w * LANES : (w + 1) * LANES] = ref[w, lo:hi, :]


ROWS = pltpu.VMEM((2, RT, LANES), F32)
COLS = pltpu.VMEM((2, CW, LANES), F32)
OWN = CT + HALF
PLACE = 2 * NT
EIGHT = 2 * CT
CHUNK = HALF // 4


def call(kernel, smem, tiles, operands, outs, scratch=()):
    operands = [pltpu.with_memory_space_constraint(tiles, pltpu.VMEM)] + list(operands)
    smem = [pltpu.with_memory_space_constraint(x, pltpu.SMEM) for x in smem]
    vmem = pl.BlockSpec(memory_space=pltpu.VMEM)
    return pl.pallas_call(
        kernel,
        out_shape=tuple(jax.ShapeDtypeStruct((n, TILE), F32) for n in outs),
        in_specs=[pl.BlockSpec(memory_space=pltpu.SMEM) for _ in smem] + [vmem for _ in operands],
        out_specs=tuple(vmem for _ in outs),
        scratch_shapes=list(scratch),
        compiler_params=pltpu.CompilerParams(vmem_limit_bytes=VMEM_LIMIT),
    )(*smem, *operands)


def each_tile(index_ref, visit, ready=None):
    def group(step, carry):
        if ready is not None:
            ready(step)
        for i in range(GROUP):
            t = step * GROUP + i
            visit(t, index_ref[NT + t], index_ref[t])
        return carry

    lax.fori_loop(0, STEPS, group, 0)


def put_columns(cacc, colown, colother):
    join_from(cacc, colown, 0, OWN)
    join_from(cacc, colother, OWN, CW)


def first_stats_kernel(
    place, rows_hbm, cols_hbm, source, rhs, dual, rowout, colown, colother, tiles_ref, index_ref, racc, cacc,
    rows_ref, cols_ref, sems,
):
    indices = [
        pltpu.make_async_copy(src, dst, sems.at[STEPS + 2 + i])
        for i, (src, dst) in enumerate(((rows_hbm, rows_ref), (cols_hbm, cols_ref)))
    ]
    for copy in indices:
        copy.start()
    for i in range(3):
        index_ref[PLACE + i] = place[i]

    def load(step):
        part = pl.ds(step * GROUP, GROUP)
        return pltpu.make_async_copy(source.at[part], tiles_ref.at[part], sems.at[step])

    for step in range(STEPS):
        load(step).start()
    extra = [
        pltpu.make_async_copy(src, rowout.at[pl.ds(RT + i * SHARE, SHARE)], sems.at[STEPS + i])
        for i, src in enumerate((rhs, dual))
    ]
    for copy in extra:
        copy.start()
    racc[...] = jnp.zeros_like(racc)
    cacc[...] = jnp.zeros_like(cacc)

    for copy in indices:
        copy.wait()
    turn = place[0] * HALF

    def enter(t, carry):
        col = cols_ref[t]
        index_ref[t] = rows_ref[t]
        index_ref[NT + t] = jnp.where(col < CT, col, CT + ((col - CT) ^ turn))
        return carry

    lax.fori_loop(0, NT, enter, 0)

    def visit(t, col, row):
        row_pass(tiles_ref, t, col, row, None, racc, jnp.maximum, True)
        col_pass(tiles_ref, t, col, row, None, cacc, jnp.maximum, True)

    each_tile(index_ref, visit, lambda step: load(step).wait())
    join_from(racc, rowout, 0, RT)
    put_columns(cacc, colown, colother)
    for copy in extra:
        copy.wait()


def first_stats(ids, source, rhs, dual):
    vmem = pl.BlockSpec(memory_space=pltpu.VMEM)
    shapes = [jax.ShapeDtypeStruct((n, TILE), F32) for n in (RT + 2 * SHARE, OWN, HALF)]
    return pl.pallas_call(
        first_stats_kernel,
        out_shape=(*shapes, pltpu.VMEM((NT, TILE, TILE), F32), pltpu.SMEM((PLACE + 8,), jnp.int32)),
        in_specs=[pl.BlockSpec(memory_space=pltpu.SMEM)] + [pl.BlockSpec(memory_space=pltpu.HBM)] * 5,
        out_specs=(vmem,) * 4 + (pl.BlockSpec(memory_space=pltpu.SMEM),),
        scratch_shapes=[
            ROWS,
            COLS,
            pltpu.SMEM((NT,), jnp.int32),
            pltpu.SMEM((NT,), jnp.int32),
            pltpu.SemaphoreType.DMA((STEPS + 4,)),
        ],
        compiler_params=pltpu.CompilerParams(vmem_limit_bytes=VMEM_LIMIT),
    )(ids[2], *(pltpu.with_memory_space_constraint(x, pltpu.HBM) for x in (*ids[:2], source, rhs, dual)))


def second_stats_kernel(
    index_ref, tiles_ref, r0, r1, r3, r2, loc, mine, other, rowout, colown, colother, rownew,
    colnew, racc, cacc, rowf, colf,
):
    row = tree(jnp.maximum, r0[0:RT], (r1[0:RT], r2[0:RT], r3[0:RT]))
    new = 1.0 / jnp.sqrt(row + EPS)
    rownew[...] = new
    split_to(rowf, new)
    for lo, hi, src in ((0, CT, loc), (CT, OWN, mine), (OWN, CW, other)):
        new = 1.0 / jnp.sqrt(src[0 : hi - lo] + EPS)
        colnew[lo:hi] = new
        split_to(colf, new, lo)
    racc[...] = jnp.zeros_like(racc)
    cacc[...] = jnp.zeros_like(cacc)

    def visit(t, col, row):
        row_pass(tiles_ref, t, col, row, colf, racc, jnp.maximum, True)
        col_pass(tiles_ref, t, col, row, rowf, cacc, jnp.maximum, True)

    each_tile(index_ref, visit)
    join_from(racc, rowout, 0, RT)
    put_columns(cacc, colown, colother)


def third_rows_kernel(
    index_ref, tiles_ref, r0, r1, r3, r2, loc, mine, other, rowold, colold, rowout, rownew,
    colnew, racc, colf,
):
    row = tree(jnp.maximum, r0[...], (r1[...], r2[...], r3[...]))
    old = rowold[...]
    rownew[...] = old / jnp.sqrt(old * row + EPS)
    for lo, hi, src in ((0, CT, loc), (CT, OWN, mine), (OWN, CW, other)):
        old = colold[lo:hi]
        new = old / jnp.sqrt(old * src[0 : hi - lo] + EPS)
        colnew[lo:hi] = new
        split_to(colf, new, lo)
    racc[...] = jnp.zeros_like(racc)

    def visit(t, col, row):
        row_pass(tiles_ref, t, col, row, colf, racc, jnp.add, True)

    each_tile(index_ref, visit)
    join_from(racc, rowout, 0, RT)


def third_columns_kernel(index_ref, tiles_ref, row_scale, colown, colother, cacc, rowf):
    split_to(rowf, row_scale[...])
    cacc[...] = jnp.zeros_like(cacc)

    def visit(t, col, row):
        col_pass(tiles_ref, t, col, row, rowf, cacc, jnp.add, True)

    each_tile(index_ref, visit)
    put_columns(cacc, colown, colother)


def first_backward_kernel(
    index_ref, tiles_ref, r0, r1, r3, r2, after, colown, colother, rhsout, dualout, cacc, work
):
    for k, ref in enumerate((r0, r1, r2, r3)):
        at = pl.ds(pl.multiple_of((index_ref[PLACE + 2] ^ k) * SHARE, SHARE), SHARE)
        rhsout[at, :] = ref[RT : RT + SHARE]
        dualout[at, :] = ref[RT + SHARE :]
    split_to(work, dualout[...])
    cacc[...] = jnp.zeros_like(cacc)

    def visit(t, col, row):
        col_pass(tiles_ref, t, col, row, work, cacc, jnp.add, False)

    each_tile(index_ref, visit)
    put_columns(cacc, colown, colother)


def backward_kernel(
    index_ref, tiles_ref, steps, r0, r1, r3, r2, dual, rhs, rowf, colown, colother, dualnew,
    cacc, work,
):
    total = tree(jnp.add, r0[...], (r1[...], r2[...], r3[...]))
    new = dual[...] + steps[1:2] * (rhs[...] - rowf[...] * total)
    dualnew[...] = new
    split_to(work, rowf[...] * new)
    cacc[...] = jnp.zeros_like(cacc)

    def visit(t, col, row):
        col_pass(tiles_ref, t, col, row, work, cacc, jnp.add, False)

    each_tile(index_ref, visit)
    put_columns(cacc, colown, colother)


def forward_kernel(index, grad_at, index_ref, tiles_ref, *rest):
    if index == 0:
        c0, c1, c3, c2, rhs_square, *rest = rest
    else:
        steps, *rest = rest
    loc, mine, other, primal, cost, upper, colf, *rest = rest
    if index == 0:
        steps, *rest = rest
        total = tree(jnp.add, c0[...], (c1[...], c2[...], c3[...]))
        cost_sum = jnp.sum(total, axis=(0, 1), keepdims=True)
        rhs_sum = jnp.sum(rhs_square[...], axis=(0, 1), keepdims=True)
        ratio = jnp.sqrt((cost_sum + EPS) / (rhs_sum + EPS))
        steps[...] = jnp.zeros_like(steps)
        steps[0:1] = jnp.broadcast_to(STEP / ratio, (1, TILE))
        steps[1:2] = jnp.broadcast_to(STEP * ratio, (1, TILE))
    if index < ITERS - 1:
        rowout, fresh, racc, work = rest
    else:
        dual, rhs, rowf, local, link, dualout, rhsout, rowfout, p0, p1, p2, p3, racc, work = rest
        own = pl.ds(pl.multiple_of(index_ref[PLACE + 2] * SHARE, SHARE), SHARE)
        for ref, out in ((dual, dualout), (rhs, rhsout), (rowf, rowfout)):
            out[...] = ref[own, :]
    for lo, hi, src, first in ((0, CT, loc, 0), (CT, OWN, mine, grad_at), (OWN, CW, other, grad_at)):
        at = slice(lo, hi)
        x, scale = primal[at], colf[at]
        grad = scale * src[first : first + hi - lo]
        new = jnp.clip(x - steps[0:1] * (cost[at] - grad), 0.0, upper[at])
        if index < ITERS - 1:
            fresh[at] = new
        elif lo == 0:
            local[...] = scale * new
        else:
            half = index_ref[PLACE + 0] if lo == CT else 1 - index_ref[PLACE + 0]
            link[pl.ds(pl.multiple_of(half * HALF, HALF), HALF), :] = scale * new
        split_to(work, scale * (2.0 * new - x), lo)
    racc[...] = jnp.zeros_like(racc)

    def visit(t, col, row):
        row_pass(tiles_ref, t, col, row, work, racc, jnp.add, False)

    each_tile(index_ref, visit)
    if index < ITERS - 1:
        join_from(racc, rowout, 0, RT)
    else:
        for k, out in enumerate((p0, p1, p2, p3)):
            at = pl.ds(pl.multiple_of((index_ref[PLACE + 2] ^ k) * SHARE, SHARE), SHARE)
            for w in range(2):
                out[:, w * LANES : (w + 1) * LANES] = racc[w, at, :]


def core_kernel(op, tiles_ref, colown, got, out):
    out[...] = op(colown[CT:OWN], got[...])


def merge_kernel(op, tiles_ref, own, r1, r3, r2, out):
    out[...] = tree(op, own[...], (r1[...], r2[...], r3[...]))


def merge_after_kernel(tiles_ref, own, r1, r3, r2, after, out):
    out[...] = tree(jnp.maximum, own[...], (r1[...], r2[...], r3[...]))


def merge_grad_kernel(index_ref, tiles_ref, own, r1, r3, r2, gradown, gradgot, after, m0, m1, m2, m3, half):
    link = tree(jnp.maximum, own[...], (r1[...], r2[...], r3[...]))
    half[...] = gradown[CT:OWN] + gradgot[...]
    for k, out in enumerate((m0, m1, m2, m3)):
        out[0:HALF] = link
        out[HALF:] = half[pl.ds(pl.multiple_of((index_ref[PLACE + 1] ^ k) * CHUNK, CHUNK), CHUNK), :]


def merge_chunk_kernel(tiles_ref, own, r2, r1, r3, link, chunk):
    link[...] = tree(jnp.maximum, own[0:HALF], (r1[0:HALF], r2[0:HALF], r3[0:HALF]))
    chunk[...] = tree(jnp.add, own[HALF:], (r1[HALF:], r2[HALF:], r3[HALF:]))


def rows_kernel(
    tiles_ref, r0, r1, r3, r2, rowold, rhs, dual, colown, got, colold, cost, chunk, rownew, rhs_scaled,
    dual_scaled, out,
):
    total = tree(jnp.add, r0[...], (r1[...], r2[...], r3[...]))
    old = rowold[...]
    new = old / jnp.sqrt(old * total + EPS)
    rownew[...] = new
    scaled = new * rhs[...]
    rhs_scaled[...] = scaled
    dual_scaled[...] = dual[...] / new
    out[0:HALF] = colown[CT:OWN] + got[...]
    out[HALF:OWN] = jnp.sum((scaled * scaled).reshape(RT // 8, 8, TILE), axis=0)
    old = colold[0:CT]
    part = old / jnp.sqrt(old * colown[0:CT] + EPS) * cost[...]
    out[OWN : OWN + CT] = part * part
    out[OWN + CT :] = chunk[...]


def merge_all_kernel(index_ref, tiles_ref, own, r1, r3, r2, out):
    at = slice(0, HALF + EIGHT)
    out[at] = tree(jnp.add, own[at], (r1[at], r2[at], r3[at]))
    for k, ref in enumerate((own, r1, r2, r3)):
        start = pl.multiple_of((index_ref[PLACE + 1] ^ k) * CHUNK, CHUNK)
        out[pl.ds(HALF + EIGHT + start, CHUNK), :] = ref[HALF + EIGHT :]


def setup_kernel(
    index_ref, tiles_ref, own, back, colown, colold, cost_loc, cost_lnk, bound_loc, bound_lnk, start_loc, start_lnk,
    colnew, cost, upper, primal, rhs_square, cost_square,
):
    squares = own[HALF : HALF + EIGHT] + back[HALF : HALF + EIGHT]
    rhs_square[...] = squares[0:CT]
    sums = []
    for lo, hi, stat, half in (
        (0, CT, colown, None),
        (CT, OWN, own, index_ref[PLACE + 0]),
        (OWN, CW, back, 1 - index_ref[PLACE + 0]),
    ):
        at = slice(lo, hi)
        if half is None:
            c, b, x = cost_loc[...], bound_loc[...], start_loc[...]
        else:
            rows = pl.ds(pl.multiple_of(half * HALF, HALF), HALF)
            c, b, x = cost_lnk[rows, :], bound_lnk[rows, :], start_lnk[rows, :]
        old = colold[at]
        new = old / jnp.sqrt(old * stat[0 : hi - lo] + EPS)
        colnew[at] = new
        c = new * c
        cost[at] = c
        upper[at] = b / new
        primal[at] = x / new
        if half is not None:
            sums.append(jnp.sum((c * c).reshape(HALF // 8, 8, TILE), axis=0))
    cost_square[...] = squares[CT:] + (sums[0] + sums[1])


def end_kernel(steps, p0, p2, p1, p3, dual, rhs, rowf, out):
    total = tree(jnp.add, p0[...], (p1[...], p2[...], p3[...]))
    scale = rowf[...]
    out[...] = scale * (dual[...] + steps[1:2] * (rhs[...] - scale * total))


def body(
    tile_values,
    tile_rows,
    tile_cols,
    cost_local,
    cost_link,
    bound_local,
    bound_link,
    rhs,
    start_local,
    start_link,
    start_dual,
):
    scen = lax.axis_index("scen")
    core = scen % 2
    x_at, z_at = scen // 8, (scen // 2) % 4
    place = jnp.stack([core, jnp.where(core == 0, z_at, x_at), lax.axis_index("col")])
    ids = (tile_rows[0, 0], tile_cols[0, 0], place)

    def over(swap, x):
        got = {k: swap(x, k) for k in (2, 1, 3)}
        return x, got[1], got[3], got[2]

    row_part, colown, colother, tiles, index = first_stats(ids, tile_values[0, 0], rhs[0], start_dual[0])

    def run(kernel, smem, operands, outs, scratch=()):
        return call(kernel, smem, tiles, operands, outs, scratch)

    rows = over(swap_y, row_part)
    (link,) = run(functools.partial(core_kernel, jnp.maximum), (), (colown, swap_core(colother)), (HALF,))
    (link,) = run(merge_after_kernel, (), (*over(swap_first, link), rows[3]), (HALF,))
    (link,) = run(functools.partial(merge_kernel, jnp.maximum), (), over(swap_second, link), (HALF,))

    first_rows = rows
    row_part, colown, colother, row_scale, col_scale = run(
        second_stats_kernel,
        (index,),
        (*rows, colown, link, swap_core(link)),
        (RT, OWN, HALF, RT, CW),
        (ROWS, COLS, ROWS, COLS),
    )
    rows = over(swap_y, row_part)
    (link,) = run(functools.partial(core_kernel, jnp.maximum), (), (colown, swap_core(colother)), (HALF,))
    got = over(swap_first, link)
    gradown, gradother, rhs_rows, dual_rows = run(
        first_backward_kernel, (index,), (*first_rows, got[2]), (OWN, HALF, RT, RT), (COLS, ROWS)
    )
    sent = run(
        merge_grad_kernel,
        (index,),
        (*got, gradown, swap_core(gradother), rows[3]),
        (HALF + CHUNK,) * 4,
        (pltpu.VMEM((HALF, TILE), F32),),
    )
    got = {k: swap_second(sent[k], k) for k in (2, 1, 3)}
    link, chunk = run(merge_chunk_kernel, (), (sent[0], got[2], got[1], got[3]), (HALF, CHUNK))

    row_part, row_scale, col_scale = run(
        third_rows_kernel,
        (index,),
        (*rows, colown, link, swap_core(link), row_scale, col_scale),
        (RT, RT, CW),
        (ROWS, COLS),
    )
    rows = over(swap_y, row_part)
    colown, colother = run(third_columns_kernel, (index,), (row_scale,), (OWN, HALF), (COLS, ROWS))
    row_scale, rhs_scaled, dual_scaled, both = run(
        rows_kernel,
        (),
        (*rows, row_scale, rhs_rows, dual_rows, colown, swap_core(colother), col_scale, cost_local[0, 0], chunk),
        (RT, RT, RT, HALF + EIGHT + CHUNK),
    )
    (both,) = run(
        functools.partial(merge_kernel, jnp.add), (), over(swap_first, both), (HALF + EIGHT + CHUNK,)
    )
    (mine,) = run(merge_all_kernel, (index,), over(swap_second, both), (LT + EIGHT,))
    other = swap_core(mine)
    col_scale, cost, upper, primal, rhs_square, cost_square = run(
        setup_kernel,
        (index,),
        (
            mine,
            other,
            colown,
            col_scale,
            cost_local[0, 0],
            cost_link[0],
            bound_local[0, 0],
            bound_link[0],
            start_local[0, 0],
            start_link[0],
        ),
        (CW, CW, CW, CW, CT, CT),
    )
    norms = (*over(swap_y, cost_square), rhs_square)

    grads, grad_at = (gradown, mine, other), HALF + EIGHT
    for step in range(ITERS):
        given = norms if step == 0 else (steps,)
        extra = (dual_scaled, rhs_scaled, row_scale) if step == ITERS - 1 else ()
        outs = (RT, CW) if step < ITERS - 1 else (CT, LT) + (SHARE,) * 7
        result = run(
            functools.partial(forward_kernel, step, grad_at),
            (index,),
            (*given, *grads, primal, cost, upper, col_scale, *extra),
            ((CT,) if step == 0 else ()) + outs,
            (ROWS, COLS),
        )
        if step == 0:
            steps, *result = result
        if step == ITERS - 1:
            break
        row_part, primal = result
        colown, colother, dual_scaled = run(
            backward_kernel,
            (index,),
            (steps, *over(swap_y, row_part), dual_scaled, rhs_scaled, row_scale),
            (OWN, HALF, RT),
            (COLS, ROWS),
        )
        (link,) = run(functools.partial(core_kernel, jnp.add), (), (colown, swap_core(colother)), (HALF,))
        (link,) = run(functools.partial(merge_kernel, jnp.add), (), over(swap_first, link), (HALF,))
        (link,) = run(functools.partial(merge_kernel, jnp.add), (), over(swap_second, link), (HALF,))
        grads, grad_at = (colown, link, swap_core(link)), 0

    local, link, dual, rhs_own, scale, *pieces = result
    got = {k: swap_y(pieces[k], k) for k in (2, 1, 3)}
    vmem = pl.BlockSpec(memory_space=pltpu.VMEM)
    multipliers = pl.pallas_call(
        end_kernel,
        out_shape=jax.ShapeDtypeStruct((SHARE, TILE), F32),
        in_specs=[vmem] * 8,
        out_specs=vmem,
        compiler_params=pltpu.CompilerParams(vmem_limit_bytes=1024 * 1024),
    )(steps, pieces[0], got[2], got[1], got[3], dual, rhs_own, scale)
    return local[None, None], link[None], multipliers[None]


def solution(mesh):
    placed = (
        P("scen", "col", None, None, None),
        P("scen", "col", None),
        P("scen", "col", None),
        P("scen", "col", None, None),
        P("col", None, None),
        P("scen", "col", None, None),
        P("col", None, None),
        P("scen", "col", None),
        P("scen", "col", None, None),
        P("col", None, None),
        P("scen", "col", None),
    )
    return jax.shard_map(
        body,
        mesh=mesh,
        in_specs=placed,
        out_specs=(P("scen", "col", None, None), P("col", None, None), P("scen", "col", None)),
        check_vma=False,
    )
```

```python
import functools

import jax
import jax.numpy as jnp
from jax import lax
from jax.experimental import pallas as pl
from jax.experimental.pallas import tpu as pltpu
from jax.sharding import PartitionSpec as P

TILE = 256
RT = 128
CT = 8
LT = 256
ITERS = 3
NT = 64
HALF = LT // 2
SHARE = RT // 4
CW = CT + LT
GROUP = 8
STEPS = NT // GROUP
PIECE = GROUP // 2
LOADS = NT // PIECE

EPS = 1e-06
STEP = 0.9
F32 = jnp.float32
LANES = 128
VMEM_LIMIT = 24 * 1024 * 1024


def swap_core(x):
    return lax.ppermute(x, "scen", [(i, i ^ 1) for i in range(32)])


def swap_first(x, k):
    return lax.ppermute(x, "scen", [(i, i ^ (k << (1 if i % 2 else 3))) for i in range(32)])


def swap_second(x, k):
    return lax.ppermute(x, "scen", [(i, i ^ (k << (3 if i % 2 else 1))) for i in range(32)])


def swap_y(x, k):
    return lax.ppermute(x, "col", [(i, i ^ k) for i in range(4)])


def tree(op, own, got):
    return op(op(own, got[0]), op(got[1], got[2]))


def row_pass(tiles_ref, t, col, row, colf_ref, rowout_ref, op, magnitude):
    for h in range(2):
        a = tiles_ref[t, h * LANES : (h + 1) * LANES, 0:LANES]
        b = tiles_ref[t, h * LANES : (h + 1) * LANES, LANES:TILE]
        if magnitude:
            a, b = jnp.abs(a), jnp.abs(b)
        if colf_ref is not None:
            a = a * colf_ref[0, pl.ds(col, 1), :]
            b = b * colf_ref[1, pl.ds(col, 1), :]
        m = op(a, b).T
        s = jnp.max(m, axis=0, keepdims=True) if op is jnp.maximum else jnp.sum(m, axis=0, keepdims=True)
        at = (h, pl.ds(row, 1), slice(None))
        rowout_ref[at] = op(rowout_ref[at], s)


def col_pass(tiles_ref, t, col, row, rowf_ref, colout_ref, op, magnitude):
    parts = [None, None]
    for h in range(2):
        if rowf_ref is not None:
            f = jnp.broadcast_to(rowf_ref[h, pl.ds(row, 1), :], (LANES, LANES)).T
        for w in range(2):
            a = tiles_ref[t, h * LANES : (h + 1) * LANES, w * LANES : (w + 1) * LANES]
            if magnitude:
                a = jnp.abs(a)
            if rowf_ref is not None:
                a = a * f
            a = a.reshape(16, 8, LANES)
            s = jnp.max(a, axis=0) if op is jnp.maximum else jnp.sum(a, axis=0)
            parts[w] = s if parts[w] is None else op(parts[w], s)
    for w in range(2):
        s = parts[w]
        s = jnp.max(s, axis=0, keepdims=True) if op is jnp.maximum else jnp.sum(s, axis=0, keepdims=True)
        at = (w, pl.ds(col, 1), slice(None))
        colout_ref[at] = op(colout_ref[at], s)


def both_pass(tiles_ref, t, col, row, rowf_ref, colf_ref, rowout_ref, colout_ref):
    parts = [None, None]
    for h in range(2):
        at = slice(h * LANES, (h + 1) * LANES)
        blocks = [jnp.abs(tiles_ref[t, at, w * LANES : (w + 1) * LANES]) for w in range(2)]
        factor = None if rowf_ref is None else jnp.broadcast_to(rowf_ref[h, pl.ds(row, 1), :], (LANES, LANES)).T
        scaled = blocks if colf_ref is None else [a * colf_ref[w, pl.ds(col, 1), :] for w, a in enumerate(blocks)]
        s = jnp.max(jnp.maximum(scaled[0], scaled[1]).T, axis=0, keepdims=True)
        at = (h, pl.ds(row, 1), slice(None))
        rowout_ref[at] = jnp.maximum(rowout_ref[at], s)
        for w, a in enumerate(blocks):
            a = a if factor is None else a * factor
            s = jnp.max(a.reshape(16, 8, LANES), axis=0)
            parts[w] = s if parts[w] is None else jnp.maximum(parts[w], s)
    for w in range(2):
        at = (w, pl.ds(col, 1), slice(None))
        colout_ref[at] = jnp.maximum(colout_ref[at], jnp.max(parts[w], axis=0, keepdims=True))


def split_to(ref, value, lo=0):
    for w in range(2):
        ref[w, lo : lo + value.shape[0], :] = value[:, w * LANES : (w + 1) * LANES]


def join_from(ref, out, lo, hi):
    for w in range(2):
        out[0 : hi - lo, w * LANES : (w + 1) * LANES] = ref[w, lo:hi, :]


ROWS = pltpu.VMEM((2, RT, LANES), F32)
COLS = pltpu.VMEM((2, CW, LANES), F32)
OWN = CT + HALF
PLACE = 2 * NT
EIGHT = 2 * CT
CHUNK = HALF // 4


def call(kernel, smem, tiles, operands, outs, scratch=(), to_hbm=0):
    operands = [pltpu.with_memory_space_constraint(tiles, pltpu.VMEM)] + list(operands)
    smem = [pltpu.with_memory_space_constraint(x, pltpu.SMEM) for x in smem]
    vmem = pl.BlockSpec(memory_space=pltpu.VMEM)
    return pl.pallas_call(
        kernel,
        out_shape=tuple(jax.ShapeDtypeStruct((n, TILE), F32) for n in outs),
        in_specs=[pl.BlockSpec(memory_space=pltpu.SMEM) for _ in smem] + [vmem for _ in operands],
        out_specs=tuple(pl.BlockSpec(memory_space=pltpu.HBM) if i < to_hbm else vmem for i in range(len(outs))),
        scratch_shapes=list(scratch),
        compiler_params=pltpu.CompilerParams(vmem_limit_bytes=VMEM_LIMIT),
    )(*smem, *operands)


def each_tile(index_ref, visit, ready=None):
    def group(step, carry):
        for i in range(GROUP):
            if ready is not None and i % PIECE == 0:
                ready(step * (GROUP // PIECE) + i // PIECE)
            t = step * GROUP + i
            visit(t, index_ref[NT + t], index_ref[t])
        return carry

    lax.fori_loop(0, STEPS, group, 0)


def put_columns(cacc, colown, colother):
    join_from(cacc, colown, 0, OWN)
    join_from(cacc, colother, OWN, CW)


def first_stats_kernel(
    place, rows_hbm, cols_hbm, source, rhs, dual, rowout, colown, colother, tiles_ref, index_ref, racc, cacc,
    rows_ref, cols_ref, sems,
):
    indices = [
        pltpu.make_async_copy(src, dst, sems.at[LOADS + 2 + i])
        for i, (src, dst) in enumerate(((rows_hbm, rows_ref), (cols_hbm, cols_ref)))
    ]
    for copy in indices:
        copy.start()
    for i in range(3):
        index_ref[PLACE + i] = place[i]

    def load(step):
        part = pl.ds(step * PIECE, PIECE)
        return pltpu.make_async_copy(source.at[part], tiles_ref.at[part], sems.at[step])

    for step in range(LOADS):
        load(step).start()
    extra = [
        pltpu.make_async_copy(src, rowout.at[pl.ds(RT + i * SHARE, SHARE)], sems.at[LOADS + i])
        for i, src in enumerate((rhs, dual))
    ]
    for copy in extra:
        copy.start()
    racc[...] = jnp.zeros_like(racc)
    cacc[...] = jnp.zeros_like(cacc)

    for copy in indices:
        copy.wait()
    turn = place[0] * HALF

    def enter(t, carry):
        col = cols_ref[t]
        index_ref[t] = rows_ref[t]
        index_ref[NT + t] = jnp.where(col < CT, col, CT + ((col - CT) ^ turn))
        return carry

    lax.fori_loop(0, NT, enter, 0)

    def visit(t, col, row):
        both_pass(tiles_ref, t, col, row, None, None, racc, cacc)

    each_tile(index_ref, visit, lambda step: load(step).wait())
    join_from(racc, rowout, 0, RT)
    put_columns(cacc, colown, colother)
    for copy in extra:
        copy.wait()


def first_stats(ids, source, rhs, dual):
    vmem = pl.BlockSpec(memory_space=pltpu.VMEM)
    shapes = [jax.ShapeDtypeStruct((n, TILE), F32) for n in (RT + 2 * SHARE, OWN, HALF)]
    return pl.pallas_call(
        first_stats_kernel,
        out_shape=(*shapes, pltpu.VMEM((NT, TILE, TILE), F32), pltpu.SMEM((PLACE + 8,), jnp.int32)),
        in_specs=[pl.BlockSpec(memory_space=pltpu.SMEM)] + [pl.BlockSpec(memory_space=pltpu.HBM)] * 5,
        out_specs=(vmem,) * 4 + (pl.BlockSpec(memory_space=pltpu.SMEM),),
        scratch_shapes=[
            ROWS,
            COLS,
            pltpu.SMEM((NT,), jnp.int32),
            pltpu.SMEM((NT,), jnp.int32),
            pltpu.SemaphoreType.DMA((LOADS + 4,)),
        ],
        compiler_params=pltpu.CompilerParams(vmem_limit_bytes=VMEM_LIMIT),
    )(ids[2], *(pltpu.with_memory_space_constraint(x, pltpu.HBM) for x in (*ids[:2], source, rhs, dual)))


def second_stats_kernel(
    index_ref, tiles_ref, r0, r1, r3, r2, loc, mine, other, rowout, colown, colother, rownew,
    colnew, racc, cacc, rowf, colf,
):
    row = tree(jnp.maximum, r0[0:RT], (r1[0:RT], r2[0:RT], r3[0:RT]))
    new = 1.0 / jnp.sqrt(row + EPS)
    rownew[...] = new
    split_to(rowf, new)
    for lo, hi, src in ((0, CT, loc), (CT, OWN, mine), (OWN, CW, other)):
        new = 1.0 / jnp.sqrt(src[0 : hi - lo] + EPS)
        colnew[lo:hi] = new
        split_to(colf, new, lo)
    racc[...] = jnp.zeros_like(racc)
    cacc[...] = jnp.zeros_like(cacc)

    def visit(t, col, row):
        both_pass(tiles_ref, t, col, row, rowf, colf, racc, cacc)

    each_tile(index_ref, visit)
    join_from(racc, rowout, 0, RT)
    put_columns(cacc, colown, colother)


def third_rows_kernel(
    index_ref, tiles_ref, r0, r1, r3, r2, loc, mine, other, rowold, colold, rowout, rownew,
    colnew, racc, colf,
):
    row = tree(jnp.maximum, r0[...], (r1[...], r2[...], r3[...]))
    old = rowold[...]
    rownew[...] = old / jnp.sqrt(old * row + EPS)
    for lo, hi, src in ((0, CT, loc), (CT, OWN, mine), (OWN, CW, other)):
        old = colold[lo:hi]
        new = old / jnp.sqrt(old * src[0 : hi - lo] + EPS)
        colnew[lo:hi] = new
        split_to(colf, new, lo)
    racc[...] = jnp.zeros_like(racc)

    def visit(t, col, row):
        row_pass(tiles_ref, t, col, row, colf, racc, jnp.add, True)

    each_tile(index_ref, visit)
    join_from(racc, rowout, 0, RT)


def third_columns_kernel(index_ref, tiles_ref, row_scale, colown, colother, cacc, rowf):
    split_to(rowf, row_scale[...])
    cacc[...] = jnp.zeros_like(cacc)

    def visit(t, col, row):
        col_pass(tiles_ref, t, col, row, rowf, cacc, jnp.add, True)

    each_tile(index_ref, visit)
    put_columns(cacc, colown, colother)


def first_backward_kernel(
    index_ref, tiles_ref, r0, r1, r3, r2, after, colown, colother, rhsout, dualout, cacc, work
):
    for k, ref in enumerate((r0, r1, r2, r3)):
        at = pl.ds(pl.multiple_of((index_ref[PLACE + 2] ^ k) * SHARE, SHARE), SHARE)
        rhsout[at, :] = ref[RT : RT + SHARE]
        dualout[at, :] = ref[RT + SHARE :]
    split_to(work, dualout[...])
    cacc[...] = jnp.zeros_like(cacc)

    def visit(t, col, row):
        col_pass(tiles_ref, t, col, row, work, cacc, jnp.add, False)

    each_tile(index_ref, visit)
    put_columns(cacc, colown, colother)


def backward_kernel(
    index_ref, tiles_ref, steps, r0, r1, r3, r2, dual, rhs, rowf, colown, colother, dualnew,
    cacc, work,
):
    total = tree(jnp.add, r0[...], (r1[...], r2[...], r3[...]))
    new = dual[...] + steps[1:2] * (rhs[...] - rowf[...] * total)
    dualnew[...] = new
    split_to(work, rowf[...] * new)
    cacc[...] = jnp.zeros_like(cacc)

    def visit(t, col, row):
        col_pass(tiles_ref, t, col, row, work, cacc, jnp.add, False)

    each_tile(index_ref, visit)
    put_columns(cacc, colown, colother)


def forward_kernel(index, grad_at, index_ref, tiles_ref, *rest):
    if index == 0:
        c0, c1, c3, c2, rhs_square, *rest = rest
    else:
        steps, *rest = rest
    loc, mine, other, primal, cost, upper, colf, *rest = rest
    if index == 0:
        steps, *rest = rest
        total = tree(jnp.add, c0[...], (c1[...], c2[...], c3[...]))
        cost_sum = jnp.sum(total, axis=(0, 1), keepdims=True)
        rhs_sum = jnp.sum(rhs_square[...], axis=(0, 1), keepdims=True)
        ratio = jnp.sqrt((cost_sum + EPS) / (rhs_sum + EPS))
        steps[...] = jnp.zeros_like(steps)
        steps[0:1] = jnp.broadcast_to(STEP / ratio, (1, TILE))
        steps[1:2] = jnp.broadcast_to(STEP * ratio, (1, TILE))
    if index < ITERS - 1:
        rowout, fresh, racc, work = rest
    else:
        dual, rhs, rowf, local_hbm, link_hbm, dualout, rhsout, rowfout, p0, p1, p2, p3, *rest = rest
        racc, work, local, link, sems = rest
        own = pl.ds(pl.multiple_of(index_ref[PLACE + 2] * SHARE, SHARE), SHARE)
        for ref, out in ((dual, dualout), (rhs, rhsout), (rowf, rowfout)):
            out[...] = ref[own, :]
    for lo, hi, src, first in ((0, CT, loc, 0), (CT, OWN, mine, grad_at), (OWN, CW, other, grad_at)):
        at = slice(lo, hi)
        x, scale = primal[at], colf[at]
        grad = scale * src[first : first + hi - lo]
        new = jnp.clip(x - steps[0:1] * (cost[at] - grad), 0.0, upper[at])
        if index < ITERS - 1:
            fresh[at] = new
        elif lo == 0:
            local[...] = scale * new
        else:
            half = index_ref[PLACE + 0] if lo == CT else 1 - index_ref[PLACE + 0]
            link[pl.ds(pl.multiple_of(half * HALF, HALF), HALF), :] = scale * new
        split_to(work, scale * (2.0 * new - x), lo)
    leaving = []
    if index == ITERS - 1:
        leaving = [
            pltpu.make_async_copy(src, dst, sems.at[i])
            for i, (src, dst) in enumerate(((local, local_hbm), (link, link_hbm)))
        ]
    for copy in leaving:
        copy.start()
    racc[...] = jnp.zeros_like(racc)

    def visit(t, col, row):
        row_pass(tiles_ref, t, col, row, work, racc, jnp.add, False)

    each_tile(index_ref, visit)
    if index < ITERS - 1:
        join_from(racc, rowout, 0, RT)
    else:
        for k, out in enumerate((p0, p1, p2, p3)):
            at = pl.ds(pl.multiple_of((index_ref[PLACE + 2] ^ k) * SHARE, SHARE), SHARE)
            for w in range(2):
                out[:, w * LANES : (w + 1) * LANES] = racc[w, at, :]
    for copy in leaving:
        copy.wait()


def core_kernel(op, tiles_ref, colown, got, out):
    out[...] = op(colown[CT:OWN], got[...])


def merge_kernel(op, tiles_ref, own, r1, r3, r2, out):
    out[...] = tree(op, own[...], (r1[...], r2[...], r3[...]))


def merge_after_kernel(tiles_ref, own, r1, r3, r2, after, out):
    out[...] = tree(jnp.maximum, own[...], (r1[...], r2[...], r3[...]))


def merge_grad_kernel(index_ref, tiles_ref, own, r1, r3, r2, gradown, gradgot, after, m0, m1, m2, m3, half):
    link = tree(jnp.maximum, own[...], (r1[...], r2[...], r3[...]))
    half[...] = gradown[CT:OWN] + gradgot[...]
    for k, out in enumerate((m0, m1, m2, m3)):
        out[0:HALF] = link
        out[HALF:] = half[pl.ds(pl.multiple_of((index_ref[PLACE + 1] ^ k) * CHUNK, CHUNK), CHUNK), :]


def merge_chunk_kernel(tiles_ref, own, r2, r1, r3, link, chunk):
    link[...] = tree(jnp.maximum, own[0:HALF], (r1[0:HALF], r2[0:HALF], r3[0:HALF]))
    chunk[...] = tree(jnp.add, own[HALF:], (r1[HALF:], r2[HALF:], r3[HALF:]))


def rows_kernel(
    tiles_ref, r0, r1, r3, r2, rowold, rhs, dual, colown, got, colold, cost, chunk, rownew, rhs_scaled,
    dual_scaled, out,
):
    total = tree(jnp.add, r0[...], (r1[...], r2[...], r3[...]))
    old = rowold[...]
    new = old / jnp.sqrt(old * total + EPS)
    rownew[...] = new
    scaled = new * rhs[...]
    rhs_scaled[...] = scaled
    dual_scaled[...] = dual[...] / new
    out[0:HALF] = colown[CT:OWN] + got[...]
    out[HALF:OWN] = jnp.sum((scaled * scaled).reshape(RT // 8, 8, TILE), axis=0)
    old = colold[0:CT]
    part = old / jnp.sqrt(old * colown[0:CT] + EPS) * cost[...]
    out[OWN : OWN + CT] = part * part
    out[OWN + CT :] = chunk[...]


def merge_all_kernel(index_ref, tiles_ref, own, r1, r3, r2, out):
    at = slice(0, HALF + EIGHT)
    out[at] = tree(jnp.add, own[at], (r1[at], r2[at], r3[at]))
    for k, ref in enumerate((own, r1, r2, r3)):
        start = pl.multiple_of((index_ref[PLACE + 1] ^ k) * CHUNK, CHUNK)
        out[pl.ds(HALF + EIGHT + start, CHUNK), :] = ref[HALF + EIGHT :]


def setup_kernel(
    index_ref, tiles_ref, own, back, colown, colold, cost_loc, cost_lnk, bound_loc, bound_lnk, start_loc, start_lnk,
    colnew, cost, upper, primal, rhs_square, cost_square,
):
    squares = own[HALF : HALF + EIGHT] + back[HALF : HALF + EIGHT]
    rhs_square[...] = squares[0:CT]
    sums = []
    for lo, hi, stat, half in (
        (0, CT, colown, None),
        (CT, OWN, own, index_ref[PLACE + 0]),
        (OWN, CW, back, 1 - index_ref[PLACE + 0]),
    ):
        at = slice(lo, hi)
        if half is None:
            c, b, x = cost_loc[...], bound_loc[...], start_loc[...]
        else:
            rows = pl.ds(pl.multiple_of(half * HALF, HALF), HALF)
            c, b, x = cost_lnk[rows, :], bound_lnk[rows, :], start_lnk[rows, :]
        old = colold[at]
        new = old / jnp.sqrt(old * stat[0 : hi - lo] + EPS)
        colnew[at] = new
        c = new * c
        cost[at] = c
        upper[at] = b / new
        primal[at] = x / new
        if half is not None:
            sums.append(jnp.sum((c * c).reshape(HALF // 8, 8, TILE), axis=0))
    cost_square[...] = squares[CT:] + (sums[0] + sums[1])


def end_kernel(steps, p0, p2, p1, p3, dual, rhs, rowf, out):
    total = tree(jnp.add, p0[...], (p1[...], p2[...], p3[...]))
    scale = rowf[...]
    out[...] = scale * (dual[...] + steps[1:2] * (rhs[...] - scale * total))


def body(
    tile_values,
    tile_rows,
    tile_cols,
    cost_local,
    cost_link,
    bound_local,
    bound_link,
    rhs,
    start_local,
    start_link,
    start_dual,
):
    scen = lax.axis_index("scen")
    core = scen % 2
    x_at, z_at = scen // 8, (scen // 2) % 4
    place = jnp.stack([core, jnp.where(core == 0, z_at, x_at), lax.axis_index("col")])
    ids = (tile_rows[0, 0], tile_cols[0, 0], place)

    def over(swap, x):
        got = {k: swap(x, k) for k in (2, 1, 3)}
        return x, got[1], got[3], got[2]

    row_part, colown, colother, tiles, index = first_stats(ids, tile_values[0, 0], rhs[0], start_dual[0])

    def run(kernel, smem, operands, outs, scratch=(), to_hbm=0):
        return call(kernel, smem, tiles, operands, outs, scratch, to_hbm)

    rows = over(swap_y, row_part)
    (link,) = run(functools.partial(core_kernel, jnp.maximum), (), (colown, swap_core(colother)), (HALF,))
    (link,) = run(merge_after_kernel, (), (*over(swap_first, link), rows[3]), (HALF,))
    (link,) = run(functools.partial(merge_kernel, jnp.maximum), (), over(swap_second, link), (HALF,))

    first_rows = rows
    row_part, colown, colother, row_scale, col_scale = run(
        second_stats_kernel,
        (index,),
        (*rows, colown, link, swap_core(link)),
        (RT, OWN, HALF, RT, CW),
        (ROWS, COLS, ROWS, COLS),
    )
    rows = over(swap_y, row_part)
    (link,) = run(functools.partial(core_kernel, jnp.maximum), (), (colown, swap_core(colother)), (HALF,))
    got = over(swap_first, link)
    gradown, gradother, rhs_rows, dual_rows = run(
        first_backward_kernel, (index,), (*first_rows, got[2]), (OWN, HALF, RT, RT), (COLS, ROWS)
    )
    sent = run(
        merge_grad_kernel,
        (index,),
        (*got, gradown, swap_core(gradother), rows[3]),
        (HALF + CHUNK,) * 4,
        (pltpu.VMEM((HALF, TILE), F32),),
    )
    got = {k: swap_second(sent[k], k) for k in (2, 1, 3)}
    link, chunk = run(merge_chunk_kernel, (), (sent[0], got[2], got[1], got[3]), (HALF, CHUNK))

    row_part, row_scale, col_scale = run(
        third_rows_kernel,
        (index,),
        (*rows, colown, link, swap_core(link), row_scale, col_scale),
        (RT, RT, CW),
        (ROWS, COLS),
    )
    rows = over(swap_y, row_part)
    colown, colother = run(third_columns_kernel, (index,), (row_scale,), (OWN, HALF), (COLS, ROWS))
    row_scale, rhs_scaled, dual_scaled, both = run(
        rows_kernel,
        (),
        (*rows, row_scale, rhs_rows, dual_rows, colown, swap_core(colother), col_scale, cost_local[0, 0], chunk),
        (RT, RT, RT, HALF + EIGHT + CHUNK),
    )
    (both,) = run(
        functools.partial(merge_kernel, jnp.add), (), over(swap_first, both), (HALF + EIGHT + CHUNK,)
    )
    (mine,) = run(merge_all_kernel, (index,), over(swap_second, both), (LT + EIGHT,))
    other = swap_core(mine)
    col_scale, cost, upper, primal, rhs_square, cost_square = run(
        setup_kernel,
        (index,),
        (
            mine,
            other,
            colown,
            col_scale,
            cost_local[0, 0],
            cost_link[0],
            bound_local[0, 0],
            bound_link[0],
            start_local[0, 0],
            start_link[0],
        ),
        (CW, CW, CW, CW, CT, CT),
    )
    norms = (*over(swap_y, cost_square), rhs_square)

    grads, grad_at = (gradown, mine, other), HALF + EIGHT
    leaving = (pltpu.VMEM((CT, TILE), F32), pltpu.VMEM((LT, TILE), F32), pltpu.SemaphoreType.DMA((2,)))
    for step in range(ITERS):
        given = norms if step == 0 else (steps,)
        extra = (dual_scaled, rhs_scaled, row_scale) if step == ITERS - 1 else ()
        outs = (RT, CW) if step < ITERS - 1 else (CT, LT) + (SHARE,) * 7
        result = run(
            functools.partial(forward_kernel, step, grad_at),
            (index,),
            (*given, *grads, primal, cost, upper, col_scale, *extra),
            ((CT,) if step == 0 else ()) + outs,
            (ROWS, COLS) + (leaving if step == ITERS - 1 else ()),
            2 if step == ITERS - 1 else 0,
        )
        if step == 0:
            steps, *result = result
        if step == ITERS - 1:
            break
        row_part, primal = result
        colown, colother, dual_scaled = run(
            backward_kernel,
            (index,),
            (steps, *over(swap_y, row_part), dual_scaled, rhs_scaled, row_scale),
            (OWN, HALF, RT),
            (COLS, ROWS),
        )
        (link,) = run(functools.partial(core_kernel, jnp.add), (), (colown, swap_core(colother)), (HALF,))
        (link,) = run(functools.partial(merge_kernel, jnp.add), (), over(swap_first, link), (HALF,))
        (link,) = run(functools.partial(merge_kernel, jnp.add), (), over(swap_second, link), (HALF,))
        grads, grad_at = (colown, link, swap_core(link)), 0

    local, link, dual, rhs_own, scale, *pieces = result
    got = {k: swap_y(pieces[k], k) for k in (2, 1, 3)}
    vmem = pl.BlockSpec(memory_space=pltpu.VMEM)
    multipliers = pl.pallas_call(
        end_kernel,
        out_shape=jax.ShapeDtypeStruct((SHARE, TILE), F32),
        in_specs=[vmem] * 8,
        out_specs=vmem,
        compiler_params=pltpu.CompilerParams(vmem_limit_bytes=1024 * 1024),
    )(steps, pieces[0], got[2], got[1], got[3], dual, rhs_own, scale)
    return local[None, None], link[None], multipliers[None]


def solution(mesh):
    placed = (
        P("scen", "col", None, None, None),
        P("scen", "col", None),
        P("scen", "col", None),
        P("scen", "col", None, None),
        P("col", None, None),
        P("scen", "col", None, None),
        P("col", None, None),
        P("scen", "col", None),
        P("scen", "col", None, None),
        P("col", None, None),
        P("scen", "col", None),
    )
    return jax.shard_map(
        body,
        mesh=mesh,
        in_specs=placed,
        out_specs=(P("scen", "col", None, None), P("col", None, None), P("scen", "col", None)),
        check_vma=False,
    )
```

```python
import functools

import jax
import jax.numpy as jnp
from jax import lax
from jax.experimental import pallas as pl
from jax.experimental.pallas import tpu as pltpu
from jax.sharding import PartitionSpec as P

TILE = 256
RT = 128
CT = 8
LT = 256
ITERS = 3
NT = 64
HALF = LT // 2
SHARE = RT // 4
CW = CT + LT
GROUP = 8
STEPS = NT // GROUP
PIECE = GROUP // 2
LOADS = NT // PIECE

EPS = 1e-06
STEP = 0.9
F32 = jnp.float32
LANES = 128
VMEM_LIMIT = 24 * 1024 * 1024


def swap_core(x):
    return lax.ppermute(x, "scen", [(i, i ^ 1) for i in range(32)])


def swap_first(x, k):
    return lax.ppermute(x, "scen", [(i, i ^ (k << (1 if i % 2 else 3))) for i in range(32)])


def swap_second(x, k):
    return lax.ppermute(x, "scen", [(i, i ^ (k << (3 if i % 2 else 1))) for i in range(32)])


def swap_y(x, k):
    return lax.ppermute(x, "col", [(i, i ^ k) for i in range(4)])


def tree(op, own, got):
    return op(op(own, got[0]), op(got[1], got[2]))


def row_pass(tiles_ref, t, col, row, colf_ref, rowout_ref, op, magnitude):
    for h in range(2):
        a = tiles_ref[t, h * LANES : (h + 1) * LANES, 0:LANES]
        b = tiles_ref[t, h * LANES : (h + 1) * LANES, LANES:TILE]
        if magnitude:
            a, b = jnp.abs(a), jnp.abs(b)
        if colf_ref is not None:
            a = a * colf_ref[0, pl.ds(col, 1), :]
            b = b * colf_ref[1, pl.ds(col, 1), :]
        m = op(a, b).T
        s = jnp.max(m, axis=0, keepdims=True) if op is jnp.maximum else jnp.sum(m, axis=0, keepdims=True)
        at = (h, pl.ds(row, 1), slice(None))
        rowout_ref[at] = op(rowout_ref[at], s)


def col_pass(tiles_ref, t, col, row, rowf_ref, colout_ref, op, magnitude):
    parts = [None, None]
    for h in range(2):
        if rowf_ref is not None:
            f = jnp.broadcast_to(rowf_ref[h, pl.ds(row, 1), :], (LANES, LANES)).T
        for w in range(2):
            a = tiles_ref[t, h * LANES : (h + 1) * LANES, w * LANES : (w + 1) * LANES]
            if magnitude:
                a = jnp.abs(a)
            if rowf_ref is not None:
                a = a * f
            a = a.reshape(16, 8, LANES)
            s = jnp.max(a, axis=0) if op is jnp.maximum else jnp.sum(a, axis=0)
            parts[w] = s if parts[w] is None else op(parts[w], s)
    for w in range(2):
        s = parts[w]
        s = jnp.max(s, axis=0, keepdims=True) if op is jnp.maximum else jnp.sum(s, axis=0, keepdims=True)
        at = (w, pl.ds(col, 1), slice(None))
        colout_ref[at] = op(colout_ref[at], s)


def both_pass(tiles_ref, t, col, row, rowf_ref, colf_ref, rowout_ref, colout_ref):
    parts = [None, None]
    for h in range(2):
        at = slice(h * LANES, (h + 1) * LANES)
        blocks = [jnp.abs(tiles_ref[t, at, w * LANES : (w + 1) * LANES]) for w in range(2)]
        factor = None if rowf_ref is None else jnp.broadcast_to(rowf_ref[h, pl.ds(row, 1), :], (LANES, LANES)).T
        scaled = blocks if colf_ref is None else [a * colf_ref[w, pl.ds(col, 1), :] for w, a in enumerate(blocks)]
        s = jnp.max(jnp.maximum(scaled[0], scaled[1]).T, axis=0, keepdims=True)
        at = (h, pl.ds(row, 1), slice(None))
        rowout_ref[at] = jnp.maximum(rowout_ref[at], s)
        for w, a in enumerate(blocks):
            a = a if factor is None else a * factor
            s = jnp.max(a.reshape(16, 8, LANES), axis=0)
            parts[w] = s if parts[w] is None else jnp.maximum(parts[w], s)
    for w in range(2):
        at = (w, pl.ds(col, 1), slice(None))
        colout_ref[at] = jnp.maximum(colout_ref[at], jnp.max(parts[w], axis=0, keepdims=True))


def split_to(ref, value, lo=0):
    for w in range(2):
        ref[w, lo : lo + value.shape[0], :] = value[:, w * LANES : (w + 1) * LANES]


def join_from(ref, out, lo, hi):
    for w in range(2):
        out[0 : hi - lo, w * LANES : (w + 1) * LANES] = ref[w, lo:hi, :]


ROWS = pltpu.VMEM((2, RT, LANES), F32)
COLS = pltpu.VMEM((2, CW, LANES), F32)
OWN = CT + HALF
PLACE = 2 * NT
EIGHT = 2 * CT
CHUNK = HALF // 4


def call(kernel, smem, tiles, operands, outs, scratch=(), to_hbm=0):
    operands = [pltpu.with_memory_space_constraint(tiles, pltpu.VMEM)] + list(operands)
    smem = [pltpu.with_memory_space_constraint(x, pltpu.SMEM) for x in smem]
    vmem = pl.BlockSpec(memory_space=pltpu.VMEM)
    return pl.pallas_call(
        kernel,
        out_shape=tuple(jax.ShapeDtypeStruct((n, TILE), F32) for n in outs),
        in_specs=[pl.BlockSpec(memory_space=pltpu.SMEM) for _ in smem] + [vmem for _ in operands],
        out_specs=tuple(pl.BlockSpec(memory_space=pltpu.HBM) if i < to_hbm else vmem for i in range(len(outs))),
        scratch_shapes=list(scratch),
        compiler_params=pltpu.CompilerParams(vmem_limit_bytes=VMEM_LIMIT),
    )(*smem, *operands)


def each_tile(index_ref, visit, ready=None):
    def group(step, carry):
        for i in range(GROUP):
            if ready is not None and i % PIECE == 0:
                ready(step * (GROUP // PIECE) + i // PIECE)
            t = step * GROUP + i
            visit(t, index_ref[NT + t], index_ref[t])
        return carry

    lax.fori_loop(0, STEPS, group, 0)


def put_columns(cacc, colown, colother):
    join_from(cacc, colown, 0, OWN)
    join_from(cacc, colother, OWN, CW)


def first_stats_kernel(
    place, rows_hbm, cols_hbm, source, rhs, dual, rowout, colown, colother, tiles_ref, index_ref, racc, cacc,
    rows_ref, cols_ref, sems,
):
    indices = [
        pltpu.make_async_copy(src, dst, sems.at[LOADS + 2 + i])
        for i, (src, dst) in enumerate(((rows_hbm, rows_ref), (cols_hbm, cols_ref)))
    ]
    for copy in indices:
        copy.start()
    for i in range(3):
        index_ref[PLACE + i] = place[i]

    def load(step):
        part = pl.ds(step * PIECE, PIECE)
        return pltpu.make_async_copy(source.at[part], tiles_ref.at[part], sems.at[step])

    for step in range(LOADS):
        load(step).start()
    extra = [
        pltpu.make_async_copy(src, rowout.at[pl.ds(RT + i * SHARE, SHARE)], sems.at[LOADS + i])
        for i, src in enumerate((rhs, dual))
    ]
    for copy in extra:
        copy.start()
    racc[...] = jnp.zeros_like(racc)
    cacc[...] = jnp.zeros_like(cacc)

    for copy in indices:
        copy.wait()
    turn = place[0] * HALF

    def enter(t, carry):
        col = cols_ref[t]
        index_ref[t] = rows_ref[t]
        index_ref[NT + t] = jnp.where(col < CT, col, CT + ((col - CT) ^ turn))
        return carry

    lax.fori_loop(0, NT, enter, 0)

    def visit(t, col, row):
        both_pass(tiles_ref, t, col, row, None, None, racc, cacc)

    each_tile(index_ref, visit, lambda step: load(step).wait())
    join_from(racc, rowout, 0, RT)
    put_columns(cacc, colown, colother)
    for copy in extra:
        copy.wait()


def first_stats(ids, source, rhs, dual):
    vmem = pl.BlockSpec(memory_space=pltpu.VMEM)
    shapes = [jax.ShapeDtypeStruct((n, TILE), F32) for n in (RT + 2 * SHARE, OWN, HALF)]
    return pl.pallas_call(
        first_stats_kernel,
        out_shape=(*shapes, pltpu.VMEM((NT, TILE, TILE), F32), pltpu.SMEM((PLACE + 8,), jnp.int32)),
        in_specs=[pl.BlockSpec(memory_space=pltpu.SMEM)] + [pl.BlockSpec(memory_space=pltpu.HBM)] * 5,
        out_specs=(vmem,) * 4 + (pl.BlockSpec(memory_space=pltpu.SMEM),),
        scratch_shapes=[
            ROWS,
            COLS,
            pltpu.SMEM((NT,), jnp.int32),
            pltpu.SMEM((NT,), jnp.int32),
            pltpu.SemaphoreType.DMA((LOADS + 4,)),
        ],
        compiler_params=pltpu.CompilerParams(vmem_limit_bytes=VMEM_LIMIT),
    )(ids[2], *(pltpu.with_memory_space_constraint(x, pltpu.HBM) for x in (*ids[:2], source, rhs, dual)))


def second_stats_kernel(
    index_ref, tiles_ref, near, far, loc, mine, other, rowout, colown, colother, rownew,
    colnew, racc, cacc, rowf, colf,
):
    row = jnp.maximum(near[0:RT], far[0:RT])
    new = 1.0 / jnp.sqrt(row + EPS)
    rownew[...] = new
    split_to(rowf, new)
    for lo, hi, src in ((0, CT, loc), (CT, OWN, mine), (OWN, CW, other)):
        new = 1.0 / jnp.sqrt(src[0 : hi - lo] + EPS)
        colnew[lo:hi] = new
        split_to(colf, new, lo)
    racc[...] = jnp.zeros_like(racc)
    cacc[...] = jnp.zeros_like(cacc)

    def visit(t, col, row):
        both_pass(tiles_ref, t, col, row, rowf, colf, racc, cacc)

    each_tile(index_ref, visit)
    join_from(racc, rowout, 0, RT)
    put_columns(cacc, colown, colother)


def third_rows_kernel(
    index_ref, tiles_ref, near, far, loc, mine, other, rowold, colold, rowout, rownew,
    colnew, racc, colf,
):
    row = jnp.maximum(near[...], far[...])
    old = rowold[...]
    rownew[...] = old / jnp.sqrt(old * row + EPS)
    for lo, hi, src in ((0, CT, loc), (CT, OWN, mine), (OWN, CW, other)):
        old = colold[lo:hi]
        new = old / jnp.sqrt(old * src[0 : hi - lo] + EPS)
        colnew[lo:hi] = new
        split_to(colf, new, lo)
    racc[...] = jnp.zeros_like(racc)

    def visit(t, col, row):
        row_pass(tiles_ref, t, col, row, colf, racc, jnp.add, True)

    each_tile(index_ref, visit)
    join_from(racc, rowout, 0, RT)


def third_columns_kernel(index_ref, tiles_ref, row_scale, colown, colother, cacc, rowf):
    split_to(rowf, row_scale[...])
    cacc[...] = jnp.zeros_like(cacc)

    def visit(t, col, row):
        col_pass(tiles_ref, t, col, row, rowf, cacc, jnp.add, True)

    each_tile(index_ref, visit)
    put_columns(cacc, colown, colother)


def first_backward_kernel(
    index_ref, tiles_ref, near, far, after, colown, colother, rhsout, dualout, cacc, work
):
    for k, ref, start in ((0, near, RT), (1, near, RT + 2 * SHARE), (3, far, RT), (2, far, RT + 2 * SHARE)):
        at = pl.ds(pl.multiple_of((index_ref[PLACE + 2] ^ k) * SHARE, SHARE), SHARE)
        rhsout[at, :] = ref[start : start + SHARE]
        dualout[at, :] = ref[start + SHARE : start + 2 * SHARE]
    split_to(work, dualout[...])
    cacc[...] = jnp.zeros_like(cacc)

    def visit(t, col, row):
        col_pass(tiles_ref, t, col, row, work, cacc, jnp.add, False)

    each_tile(index_ref, visit)
    put_columns(cacc, colown, colother)


def backward_kernel(
    index_ref, tiles_ref, steps, r0, r1, r3, r2, dual, rhs, rowf, colown, colother, dualnew,
    cacc, work,
):
    total = tree(jnp.add, r0[...], (r1[...], r2[...], r3[...]))
    new = dual[...] + steps[1:2] * (rhs[...] - rowf[...] * total)
    dualnew[...] = new
    split_to(work, rowf[...] * new)
    cacc[...] = jnp.zeros_like(cacc)

    def visit(t, col, row):
        col_pass(tiles_ref, t, col, row, work, cacc, jnp.add, False)

    each_tile(index_ref, visit)
    put_columns(cacc, colown, colother)


def forward_kernel(index, grad_at, index_ref, tiles_ref, *rest):
    if index == 0:
        c0, c1, c3, c2, rhs_square, *rest = rest
    else:
        steps, *rest = rest
    loc, mine, other, primal, cost, upper, colf, *rest = rest
    if index == 0:
        steps, *rest = rest
        total = tree(jnp.add, c0[...], (c1[...], c2[...], c3[...]))
        cost_sum = jnp.sum(total, axis=(0, 1), keepdims=True)
        rhs_sum = jnp.sum(rhs_square[...], axis=(0, 1), keepdims=True)
        ratio = jnp.sqrt((cost_sum + EPS) / (rhs_sum + EPS))
        steps[...] = jnp.zeros_like(steps)
        steps[0:1] = jnp.broadcast_to(STEP / ratio, (1, TILE))
        steps[1:2] = jnp.broadcast_to(STEP * ratio, (1, TILE))
    if index < ITERS - 1:
        rowout, fresh, racc, work = rest
    else:
        dual, rhs, rowf, local_hbm, link_hbm, dualout, rhsout, rowfout, p0, p1, p2, p3, *rest = rest
        racc, work, local, link, sems = rest
        own = pl.ds(pl.multiple_of(index_ref[PLACE + 2] * SHARE, SHARE), SHARE)
        for ref, out in ((dual, dualout), (rhs, rhsout), (rowf, rowfout)):
            out[...] = ref[own, :]
    for lo, hi, src, first in ((0, CT, loc, 0), (CT, OWN, mine, grad_at), (OWN, CW, other, grad_at)):
        at = slice(lo, hi)
        x, scale = primal[at], colf[at]
        grad = scale * src[first : first + hi - lo]
        new = jnp.clip(x - steps[0:1] * (cost[at] - grad), 0.0, upper[at])
        if index < ITERS - 1:
            fresh[at] = new
        elif lo == 0:
            local[...] = scale * new
        else:
            half = index_ref[PLACE + 0] if lo == CT else 1 - index_ref[PLACE + 0]
            link[pl.ds(pl.multiple_of(half * HALF, HALF), HALF), :] = scale * new
        split_to(work, scale * (2.0 * new - x), lo)
    leaving = []
    if index == ITERS - 1:
        leaving = [
            pltpu.make_async_copy(src, dst, sems.at[i])
            for i, (src, dst) in enumerate(((local, local_hbm), (link, link_hbm)))
        ]
    for copy in leaving:
        copy.start()
    racc[...] = jnp.zeros_like(racc)

    def visit(t, col, row):
        row_pass(tiles_ref, t, col, row, work, racc, jnp.add, False)

    each_tile(index_ref, visit)
    if index < ITERS - 1:
        join_from(racc, rowout, 0, RT)
    else:
        for k, out in enumerate((p0, p1, p2, p3)):
            at = pl.ds(pl.multiple_of((index_ref[PLACE + 2] ^ k) * SHARE, SHARE), SHARE)
            for w in range(2):
                out[:, w * LANES : (w + 1) * LANES] = racc[w, at, :]
    for copy in leaving:
        copy.wait()


def core_kernel(op, tiles_ref, colown, got, out):
    out[...] = op(colown[CT:OWN], got[...])


def merge_kernel(op, tiles_ref, own, r1, r3, r2, out):
    out[...] = tree(op, own[...], (r1[...], r2[...], r3[...]))


def merge_rows_kernel(tiles_ref, own, r1, r3, r2, mine, got, out, near):
    out[...] = tree(jnp.maximum, own[...], (r1[...], r2[...], r3[...]))
    near[0:RT] = jnp.maximum(mine[0:RT], got[0:RT])
    near[RT : RT + 2 * SHARE] = mine[RT:]
    near[RT + 2 * SHARE :] = got[RT:]


def merge_grad_kernel(
    index_ref, tiles_ref, own, r1, r3, r2, gradown, gradgot, mine, got, m0, m1, m2, m3, near, half
):
    near[...] = jnp.maximum(mine[...], got[...])
    link = tree(jnp.maximum, own[...], (r1[...], r2[...], r3[...]))
    half[...] = gradown[CT:OWN] + gradgot[...]
    for k, out in enumerate((m0, m1, m2, m3)):
        out[0:HALF] = link
        out[HALF:] = half[pl.ds(pl.multiple_of((index_ref[PLACE + 1] ^ k) * CHUNK, CHUNK), CHUNK), :]


def merge_chunk_kernel(tiles_ref, own, r2, r1, r3, link, chunk):
    link[...] = tree(jnp.maximum, own[0:HALF], (r1[0:HALF], r2[0:HALF], r3[0:HALF]))
    chunk[...] = tree(jnp.add, own[HALF:], (r1[HALF:], r2[HALF:], r3[HALF:]))


def rows_kernel(
    tiles_ref, r0, r1, r3, r2, rowold, rhs, dual, colown, got, colold, cost, chunk, rownew, rhs_scaled,
    dual_scaled, out,
):
    total = tree(jnp.add, r0[...], (r1[...], r2[...], r3[...]))
    old = rowold[...]
    new = old / jnp.sqrt(old * total + EPS)
    rownew[...] = new
    scaled = new * rhs[...]
    rhs_scaled[...] = scaled
    dual_scaled[...] = dual[...] / new
    out[0:HALF] = colown[CT:OWN] + got[...]
    out[HALF:OWN] = jnp.sum((scaled * scaled).reshape(RT // 8, 8, TILE), axis=0)
    old = colold[0:CT]
    part = old / jnp.sqrt(old * colown[0:CT] + EPS) * cost[...]
    out[OWN : OWN + CT] = part * part
    out[OWN + CT :] = chunk[...]


def merge_all_kernel(index_ref, tiles_ref, own, r1, r3, r2, out):
    at = slice(0, HALF + EIGHT)
    out[at] = tree(jnp.add, own[at], (r1[at], r2[at], r3[at]))
    for k, ref in enumerate((own, r1, r2, r3)):
        start = pl.multiple_of((index_ref[PLACE + 1] ^ k) * CHUNK, CHUNK)
        out[pl.ds(HALF + EIGHT + start, CHUNK), :] = ref[HALF + EIGHT :]


def setup_kernel(
    index_ref, tiles_ref, own, back, colown, colold, cost_loc, cost_lnk, bound_loc, bound_lnk, start_loc, start_lnk,
    colnew, cost, upper, primal, rhs_square, cost_square,
):
    squares = own[HALF : HALF + EIGHT] + back[HALF : HALF + EIGHT]
    rhs_square[...] = squares[0:CT]
    sums = []
    for lo, hi, stat, half in (
        (0, CT, colown, None),
        (CT, OWN, own, index_ref[PLACE + 0]),
        (OWN, CW, back, 1 - index_ref[PLACE + 0]),
    ):
        at = slice(lo, hi)
        if half is None:
            c, b, x = cost_loc[...], bound_loc[...], start_loc[...]
        else:
            rows = pl.ds(pl.multiple_of(half * HALF, HALF), HALF)
            c, b, x = cost_lnk[rows, :], bound_lnk[rows, :], start_lnk[rows, :]
        old = colold[at]
        new = old / jnp.sqrt(old * stat[0 : hi - lo] + EPS)
        colnew[at] = new
        c = new * c
        cost[at] = c
        upper[at] = b / new
        primal[at] = x / new
        if half is not None:
            sums.append(jnp.sum((c * c).reshape(HALF // 8, 8, TILE), axis=0))
    cost_square[...] = squares[CT:] + (sums[0] + sums[1])


def end_kernel(steps, p0, p2, p1, p3, dual, rhs, rowf, out):
    total = tree(jnp.add, p0[...], (p1[...], p2[...], p3[...]))
    scale = rowf[...]
    out[...] = scale * (dual[...] + steps[1:2] * (rhs[...] - scale * total))


def body(
    tile_values,
    tile_rows,
    tile_cols,
    cost_local,
    cost_link,
    bound_local,
    bound_link,
    rhs,
    start_local,
    start_link,
    start_dual,
):
    scen = lax.axis_index("scen")
    core = scen % 2
    x_at, z_at = scen // 8, (scen // 2) % 4
    place = jnp.stack([core, jnp.where(core == 0, z_at, x_at), lax.axis_index("col")])
    ids = (tile_rows[0, 0], tile_cols[0, 0], place)

    def over(swap, x):
        got = {k: swap(x, k) for k in (2, 1, 3)}
        return x, got[1], got[3], got[2]

    row_part, colown, colother, tiles, index = first_stats(ids, tile_values[0, 0], rhs[0], start_dual[0])

    def run(kernel, smem, operands, outs, scratch=(), to_hbm=0):
        return call(kernel, smem, tiles, operands, outs, scratch, to_hbm)

    (link,) = run(functools.partial(core_kernel, jnp.maximum), (), (colown, swap_core(colother)), (HALF,))
    link, near = run(
        merge_rows_kernel, (), (*over(swap_first, link), row_part, swap_y(row_part, 1)), (HALF, RT + 4 * SHARE)
    )
    far = swap_y(near, 3)
    (link,) = run(functools.partial(merge_kernel, jnp.maximum), (), over(swap_second, link), (HALF,))

    gathered = (near, far)
    row_part, colown, colother, row_scale, col_scale = run(
        second_stats_kernel,
        (index,),
        (near, far, colown, link, swap_core(link)),
        (RT, OWN, HALF, RT, CW),
        (ROWS, COLS, ROWS, COLS),
    )
    (link,) = run(functools.partial(core_kernel, jnp.maximum), (), (colown, swap_core(colother)), (HALF,))
    got = over(swap_first, link)
    gradown, gradother, rhs_rows, dual_rows = run(
        first_backward_kernel, (index,), (*gathered, got[2]), (OWN, HALF, RT, RT), (COLS, ROWS)
    )
    *sent, near = run(
        merge_grad_kernel,
        (index,),
        (*got, gradown, swap_core(gradother), row_part, swap_y(row_part, 1)),
        (HALF + CHUNK,) * 4 + (RT,),
        (pltpu.VMEM((HALF, TILE), F32),),
    )
    far = swap_y(near, 3)
    got = {k: swap_second(sent[k], k) for k in (2, 1, 3)}
    link, chunk = run(merge_chunk_kernel, (), (sent[0], got[2], got[1], got[3]), (HALF, CHUNK))

    row_part, row_scale, col_scale = run(
        third_rows_kernel,
        (index,),
        (near, far, colown, link, swap_core(link), row_scale, col_scale),
        (RT, RT, CW),
        (ROWS, COLS),
    )
    rows = over(swap_y, row_part)
    colown, colother = run(third_columns_kernel, (index,), (row_scale,), (OWN, HALF), (COLS, ROWS))
    row_scale, rhs_scaled, dual_scaled, both = run(
        rows_kernel,
        (),
        (*rows, row_scale, rhs_rows, dual_rows, colown, swap_core(colother), col_scale, cost_local[0, 0], chunk),
        (RT, RT, RT, HALF + EIGHT + CHUNK),
    )
    (both,) = run(
        functools.partial(merge_kernel, jnp.add), (), over(swap_first, both), (HALF + EIGHT + CHUNK,)
    )
    (mine,) = run(merge_all_kernel, (index,), over(swap_second, both), (LT + EIGHT,))
    other = swap_core(mine)
    col_scale, cost, upper, primal, rhs_square, cost_square = run(
        setup_kernel,
        (index,),
        (
            mine,
            other,
            colown,
            col_scale,
            cost_local[0, 0],
            cost_link[0],
            bound_local[0, 0],
            bound_link[0],
            start_local[0, 0],
            start_link[0],
        ),
        (CW, CW, CW, CW, CT, CT),
    )
    norms = (*over(swap_y, cost_square), rhs_square)

    grads, grad_at = (gradown, mine, other), HALF + EIGHT
    leaving = (pltpu.VMEM((CT, TILE), F32), pltpu.VMEM((LT, TILE), F32), pltpu.SemaphoreType.DMA((2,)))
    for step in range(ITERS):
        given = norms if step == 0 else (steps,)
        extra = (dual_scaled, rhs_scaled, row_scale) if step == ITERS - 1 else ()
        outs = (RT, CW) if step < ITERS - 1 else (CT, LT) + (SHARE,) * 7
        result = run(
            functools.partial(forward_kernel, step, grad_at),
            (index,),
            (*given, *grads, primal, cost, upper, col_scale, *extra),
            ((CT,) if step == 0 else ()) + outs,
            (ROWS, COLS) + (leaving if step == ITERS - 1 else ()),
            2 if step == ITERS - 1 else 0,
        )
        if step == 0:
            steps, *result = result
        if step == ITERS - 1:
            break
        row_part, primal = result
        colown, colother, dual_scaled = run(
            backward_kernel,
            (index,),
            (steps, *over(swap_y, row_part), dual_scaled, rhs_scaled, row_scale),
            (OWN, HALF, RT),
            (COLS, ROWS),
        )
        (link,) = run(functools.partial(core_kernel, jnp.add), (), (colown, swap_core(colother)), (HALF,))
        (link,) = run(functools.partial(merge_kernel, jnp.add), (), over(swap_first, link), (HALF,))
        (link,) = run(functools.partial(merge_kernel, jnp.add), (), over(swap_second, link), (HALF,))
        grads, grad_at = (colown, link, swap_core(link)), 0

    local, link, dual, rhs_own, scale, *pieces = result
    got = {k: swap_y(pieces[k], k) for k in (2, 1, 3)}
    vmem = pl.BlockSpec(memory_space=pltpu.VMEM)
    multipliers = pl.pallas_call(
        end_kernel,
        out_shape=jax.ShapeDtypeStruct((SHARE, TILE), F32),
        in_specs=[vmem] * 8,
        out_specs=vmem,
        compiler_params=pltpu.CompilerParams(vmem_limit_bytes=1024 * 1024),
    )(steps, pieces[0], got[2], got[1], got[3], dual, rhs_own, scale)
    return local[None, None], link[None], multipliers[None]


def solution(mesh):
    placed = (
        P("scen", "col", None, None, None),
        P("scen", "col", None),
        P("scen", "col", None),
        P("scen", "col", None, None),
        P("col", None, None),
        P("scen", "col", None, None),
        P("col", None, None),
        P("scen", "col", None),
        P("scen", "col", None, None),
        P("col", None, None),
        P("scen", "col", None),
    )
    return jax.shard_map(
        body,
        mesh=mesh,
        in_specs=placed,
        out_specs=(P("scen", "col", None, None), P("col", None, None), P("scen", "col", None)),
        check_vma=False,
    )
```

```python
import functools

import jax
import jax.numpy as jnp
from jax import lax
from jax.experimental import pallas as pl
from jax.experimental.pallas import tpu as pltpu
from jax.sharding import PartitionSpec as P

TILE = 256
RT = 128
CT = 8
LT = 256
ITERS = 3
NT = 64
HALF = LT // 2
SHARE = RT // 4
CW = CT + LT
GROUP = 8
STEPS = NT // GROUP
PIECE = GROUP // 2
LOADS = NT // PIECE

EPS = 1e-06
STEP = 0.9
F32 = jnp.float32
LANES = 128
VMEM_LIMIT = 24 * 1024 * 1024


def swap_core(x):
    return lax.ppermute(x, "scen", [(i, i ^ 1) for i in range(32)])


def swap_first(x, k):
    return lax.ppermute(x, "scen", [(i, i ^ (k << (1 if i % 2 else 3))) for i in range(32)])


def swap_second(x, k):
    return lax.ppermute(x, "scen", [(i, i ^ (k << (3 if i % 2 else 1))) for i in range(32)])


def swap_y(x, k):
    return lax.ppermute(x, "col", [(i, i ^ k) for i in range(4)])


def tree(op, own, got):
    return op(op(own, got[0]), op(got[1], got[2]))


def row_pass(tiles_ref, t, col, row, colf_ref, rowout_ref, op, magnitude):
    for h in range(2):
        a = tiles_ref[t, h * LANES : (h + 1) * LANES, 0:LANES]
        b = tiles_ref[t, h * LANES : (h + 1) * LANES, LANES:TILE]
        if magnitude:
            a, b = jnp.abs(a), jnp.abs(b)
        if colf_ref is not None:
            a = a * colf_ref[0, pl.ds(col, 1), :]
            b = b * colf_ref[1, pl.ds(col, 1), :]
        m = op(a, b).T
        s = jnp.max(m, axis=0, keepdims=True) if op is jnp.maximum else jnp.sum(m, axis=0, keepdims=True)
        at = (h, pl.ds(row, 1), slice(None))
        rowout_ref[at] = op(rowout_ref[at], s)


def col_pass(tiles_ref, t, col, row, rowf_ref, colout_ref, op, magnitude):
    parts = [None, None]
    for h in range(2):
        if rowf_ref is not None:
            f = jnp.broadcast_to(rowf_ref[h, pl.ds(row, 1), :], (LANES, LANES)).T
        for w in range(2):
            a = tiles_ref[t, h * LANES : (h + 1) * LANES, w * LANES : (w + 1) * LANES]
            if magnitude:
                a = jnp.abs(a)
            if rowf_ref is not None:
                a = a * f
            a = a.reshape(16, 8, LANES)
            s = jnp.max(a, axis=0) if op is jnp.maximum else jnp.sum(a, axis=0)
            parts[w] = s if parts[w] is None else op(parts[w], s)
    for w in range(2):
        s = parts[w]
        s = jnp.max(s, axis=0, keepdims=True) if op is jnp.maximum else jnp.sum(s, axis=0, keepdims=True)
        at = (w, pl.ds(col, 1), slice(None))
        colout_ref[at] = op(colout_ref[at], s)


def both_pass(tiles_ref, t, col, row, rowf_ref, colf_ref, rowout_ref, colout_ref):
    parts = [None, None]
    for h in range(2):
        at = slice(h * LANES, (h + 1) * LANES)
        blocks = [jnp.abs(tiles_ref[t, at, w * LANES : (w + 1) * LANES]) for w in range(2)]
        factor = None if rowf_ref is None else jnp.broadcast_to(rowf_ref[h, pl.ds(row, 1), :], (LANES, LANES)).T
        scaled = blocks if colf_ref is None else [a * colf_ref[w, pl.ds(col, 1), :] for w, a in enumerate(blocks)]
        s = jnp.max(jnp.maximum(scaled[0], scaled[1]).T, axis=0, keepdims=True)
        at = (h, pl.ds(row, 1), slice(None))
        rowout_ref[at] = jnp.maximum(rowout_ref[at], s)
        for w, a in enumerate(blocks):
            a = a if factor is None else a * factor
            s = jnp.max(a.reshape(16, 8, LANES), axis=0)
            parts[w] = s if parts[w] is None else jnp.maximum(parts[w], s)
    for w in range(2):
        at = (w, pl.ds(col, 1), slice(None))
        colout_ref[at] = jnp.maximum(colout_ref[at], jnp.max(parts[w], axis=0, keepdims=True))


def split_to(ref, value, lo=0):
    for w in range(2):
        ref[w, lo : lo + value.shape[0], :] = value[:, w * LANES : (w + 1) * LANES]


def join_from(ref, out, lo, hi):
    for w in range(2):
        out[0 : hi - lo, w * LANES : (w + 1) * LANES] = ref[w, lo:hi, :]


ROWS = pltpu.VMEM((2, RT, LANES), F32)
COLS = pltpu.VMEM((2, CW, LANES), F32)
OWN = CT + HALF
PLACE = 2 * NT
EIGHT = 2 * CT
CHUNK = HALF // 4


def call(kernel, smem, tiles, operands, outs, scratch=(), to_hbm=0):
    operands = [pltpu.with_memory_space_constraint(tiles, pltpu.VMEM)] + list(operands)
    smem = [pltpu.with_memory_space_constraint(x, pltpu.SMEM) for x in smem]
    vmem = pl.BlockSpec(memory_space=pltpu.VMEM)
    return pl.pallas_call(
        kernel,
        out_shape=tuple(jax.ShapeDtypeStruct((n, TILE), F32) for n in outs),
        in_specs=[pl.BlockSpec(memory_space=pltpu.SMEM) for _ in smem] + [vmem for _ in operands],
        out_specs=tuple(pl.BlockSpec(memory_space=pltpu.HBM) if i < to_hbm else vmem for i in range(len(outs))),
        scratch_shapes=list(scratch),
        compiler_params=pltpu.CompilerParams(vmem_limit_bytes=VMEM_LIMIT),
    )(*smem, *operands)


def each_tile(index_ref, visit, ready=None):
    def group(step, carry):
        for i in range(GROUP):
            if ready is not None and i % PIECE == 0:
                ready(step * (GROUP // PIECE) + i // PIECE)
            t = step * GROUP + i
            visit(t, index_ref[NT + t], index_ref[t])
        return carry

    lax.fori_loop(0, STEPS, group, 0)


def put_columns(cacc, colown, colother):
    join_from(cacc, colown, 0, OWN)
    join_from(cacc, colother, OWN, CW)


def first_stats_kernel(
    place, rows_hbm, cols_hbm, source, rhs, dual, rowout, colown, colother, tiles_ref, index_ref, racc, cacc,
    rows_ref, cols_ref, sems,
):
    indices = [
        pltpu.make_async_copy(src, dst, sems.at[LOADS + 2 + i])
        for i, (src, dst) in enumerate(((rows_hbm, rows_ref), (cols_hbm, cols_ref)))
    ]
    for copy in indices:
        copy.start()
    for i in range(3):
        index_ref[PLACE + i] = place[i]

    def load(step):
        part = pl.ds(step * PIECE, PIECE)
        return pltpu.make_async_copy(source.at[part], tiles_ref.at[part], sems.at[step])

    for step in range(LOADS):
        load(step).start()
    extra = [
        pltpu.make_async_copy(src, rowout.at[pl.ds(RT + i * SHARE, SHARE)], sems.at[LOADS + i])
        for i, src in enumerate((rhs, dual))
    ]
    for copy in extra:
        copy.start()
    racc[...] = jnp.zeros_like(racc)
    cacc[...] = jnp.zeros_like(cacc)

    for copy in indices:
        copy.wait()
    turn = place[0] * HALF

    def enter(t, carry):
        col = cols_ref[t]
        index_ref[t] = rows_ref[t]
        index_ref[NT + t] = jnp.where(col < CT, col, CT + ((col - CT) ^ turn))
        return carry

    lax.fori_loop(0, NT, enter, 0)

    def visit(t, col, row):
        both_pass(tiles_ref, t, col, row, None, None, racc, cacc)

    each_tile(index_ref, visit, lambda step: load(step).wait())
    join_from(racc, rowout, 0, RT)
    put_columns(cacc, colown, colother)
    for copy in extra:
        copy.wait()


def first_stats(ids, source, rhs, dual):
    vmem = pl.BlockSpec(memory_space=pltpu.VMEM)
    shapes = [jax.ShapeDtypeStruct((n, TILE), F32) for n in (RT + 2 * SHARE, OWN, HALF)]
    return pl.pallas_call(
        first_stats_kernel,
        out_shape=(*shapes, pltpu.VMEM((NT, TILE, TILE), F32), pltpu.SMEM((PLACE + 8,), jnp.int32)),
        in_specs=[pl.BlockSpec(memory_space=pltpu.SMEM)] + [pl.BlockSpec(memory_space=pltpu.HBM)] * 5,
        out_specs=(vmem,) * 4 + (pl.BlockSpec(memory_space=pltpu.SMEM),),
        scratch_shapes=[
            ROWS,
            COLS,
            pltpu.SMEM((NT,), jnp.int32),
            pltpu.SMEM((NT,), jnp.int32),
            pltpu.SemaphoreType.DMA((LOADS + 4,)),
        ],
        compiler_params=pltpu.CompilerParams(vmem_limit_bytes=VMEM_LIMIT),
    )(ids[2], *(pltpu.with_memory_space_constraint(x, pltpu.HBM) for x in (*ids[:2], source, rhs, dual)))


def second_columns_kernel(
    index_ref, tiles_ref, near, far, loc, mine, other, colown, colother, rownew, colnew, cacc, rowf
):
    row = jnp.maximum(near[0:RT], far[0:RT])
    new = 1.0 / jnp.sqrt(row + EPS)
    rownew[...] = new
    split_to(rowf, new)
    for lo, hi, src in ((0, CT, loc), (CT, OWN, mine), (OWN, CW, other)):
        colnew[lo:hi] = 1.0 / jnp.sqrt(src[0 : hi - lo] + EPS)
    cacc[...] = jnp.zeros_like(cacc)

    def visit(t, col, row):
        col_pass(tiles_ref, t, col, row, rowf, cacc, jnp.maximum, True)

    each_tile(index_ref, visit)
    put_columns(cacc, colown, colother)


def second_rows_kernel(index_ref, tiles_ref, col_scale, rowout, racc, colf):
    split_to(colf, col_scale[...])
    racc[...] = jnp.zeros_like(racc)

    def visit(t, col, row):
        row_pass(tiles_ref, t, col, row, colf, racc, jnp.maximum, True)

    each_tile(index_ref, visit)
    join_from(racc, rowout, 0, RT)


def third_rows_kernel(
    index_ref, tiles_ref, near, far, loc, mine, other, rowold, colold, rowout, rownew,
    colnew, racc, colf,
):
    row = jnp.maximum(near[...], far[...])
    old = rowold[...]
    rownew[...] = old / jnp.sqrt(old * row + EPS)
    for lo, hi, src in ((0, CT, loc), (CT, OWN, mine), (OWN, CW, other)):
        old = colold[lo:hi]
        new = old / jnp.sqrt(old * src[0 : hi - lo] + EPS)
        colnew[lo:hi] = new
        split_to(colf, new, lo)
    racc[...] = jnp.zeros_like(racc)

    def visit(t, col, row):
        row_pass(tiles_ref, t, col, row, colf, racc, jnp.add, True)

    each_tile(index_ref, visit)
    join_from(racc, rowout, 0, RT)


def third_columns_kernel(index_ref, tiles_ref, row_scale, colown, colother, cacc, rowf):
    split_to(rowf, row_scale[...])
    cacc[...] = jnp.zeros_like(cacc)

    def visit(t, col, row):
        col_pass(tiles_ref, t, col, row, rowf, cacc, jnp.add, True)

    each_tile(index_ref, visit)
    put_columns(cacc, colown, colother)


def first_backward_kernel(
    index_ref, tiles_ref, near, far, after, colown, colother, rhsout, dualout, cacc, work
):
    for k, ref, start in ((0, near, RT), (1, near, RT + 2 * SHARE), (3, far, RT), (2, far, RT + 2 * SHARE)):
        at = pl.ds(pl.multiple_of((index_ref[PLACE + 2] ^ k) * SHARE, SHARE), SHARE)
        rhsout[at, :] = ref[start : start + SHARE]
        dualout[at, :] = ref[start + SHARE : start + 2 * SHARE]
    split_to(work, dualout[...])
    cacc[...] = jnp.zeros_like(cacc)

    def visit(t, col, row):
        col_pass(tiles_ref, t, col, row, work, cacc, jnp.add, False)

    each_tile(index_ref, visit)
    put_columns(cacc, colown, colother)


def backward_kernel(
    index_ref, tiles_ref, steps, r0, r1, r3, r2, dual, rhs, rowf, colown, colother, dualnew,
    cacc, work,
):
    total = tree(jnp.add, r0[...], (r1[...], r2[...], r3[...]))
    new = dual[...] + steps[1:2] * (rhs[...] - rowf[...] * total)
    dualnew[...] = new
    split_to(work, rowf[...] * new)
    cacc[...] = jnp.zeros_like(cacc)

    def visit(t, col, row):
        col_pass(tiles_ref, t, col, row, work, cacc, jnp.add, False)

    each_tile(index_ref, visit)
    put_columns(cacc, colown, colother)


def forward_kernel(index, grad_at, index_ref, tiles_ref, *rest):
    if index == 0:
        c0, c1, c3, c2, rhs_square, *rest = rest
    else:
        steps, *rest = rest
    loc, mine, other, primal, cost, upper, colf, *rest = rest
    if index == 0:
        steps, *rest = rest
        total = tree(jnp.add, c0[...], (c1[...], c2[...], c3[...]))
        cost_sum = jnp.sum(total, axis=(0, 1), keepdims=True)
        rhs_sum = jnp.sum(rhs_square[...], axis=(0, 1), keepdims=True)
        ratio = jnp.sqrt((cost_sum + EPS) / (rhs_sum + EPS))
        steps[...] = jnp.zeros_like(steps)
        steps[0:1] = jnp.broadcast_to(STEP / ratio, (1, TILE))
        steps[1:2] = jnp.broadcast_to(STEP * ratio, (1, TILE))
    if index < ITERS - 1:
        rowout, fresh, racc, work = rest
    else:
        dual, rhs, rowf, local_hbm, link_hbm, dualout, rhsout, rowfout, p0, p1, p2, p3, *rest = rest
        racc, work, local, link, sems = rest
        own = pl.ds(pl.multiple_of(index_ref[PLACE + 2] * SHARE, SHARE), SHARE)
        for ref, out in ((dual, dualout), (rhs, rhsout), (rowf, rowfout)):
            out[...] = ref[own, :]
    for lo, hi, src, first in ((0, CT, loc, 0), (CT, OWN, mine, grad_at), (OWN, CW, other, grad_at)):
        at = slice(lo, hi)
        x, scale = primal[at], colf[at]
        grad = scale * src[first : first + hi - lo]
        new = jnp.clip(x - steps[0:1] * (cost[at] - grad), 0.0, upper[at])
        if index < ITERS - 1:
            fresh[at] = new
        elif lo == 0:
            local[...] = scale * new
        else:
            half = index_ref[PLACE + 0] if lo == CT else 1 - index_ref[PLACE + 0]
            link[pl.ds(pl.multiple_of(half * HALF, HALF), HALF), :] = scale * new
        split_to(work, scale * (2.0 * new - x), lo)
    leaving = []
    if index == ITERS - 1:
        leaving = [
            pltpu.make_async_copy(src, dst, sems.at[i])
            for i, (src, dst) in enumerate(((local, local_hbm), (link, link_hbm)))
        ]
    for copy in leaving:
        copy.start()
    racc[...] = jnp.zeros_like(racc)

    def visit(t, col, row):
        row_pass(tiles_ref, t, col, row, work, racc, jnp.add, False)

    each_tile(index_ref, visit)
    if index < ITERS - 1:
        join_from(racc, rowout, 0, RT)
    else:
        for k, out in enumerate((p0, p1, p2, p3)):
            at = pl.ds(pl.multiple_of((index_ref[PLACE + 2] ^ k) * SHARE, SHARE), SHARE)
            for w in range(2):
                out[:, w * LANES : (w + 1) * LANES] = racc[w, at, :]
    for copy in leaving:
        copy.wait()


def core_kernel(op, tiles_ref, colown, got, out):
    out[...] = op(colown[CT:OWN], got[...])


def core_after_kernel(tiles_ref, colown, got, after, out):
    out[...] = jnp.maximum(colown[CT:OWN], got[...])


def merge_kernel(op, tiles_ref, own, r1, r3, r2, out):
    out[...] = tree(op, own[...], (r1[...], r2[...], r3[...]))


def merge_rows_kernel(tiles_ref, own, r1, r3, r2, mine, got, out, near):
    out[...] = tree(jnp.maximum, own[...], (r1[...], r2[...], r3[...]))
    near[0:RT] = jnp.maximum(mine[0:RT], got[0:RT])
    near[RT : RT + 2 * SHARE] = mine[RT:]
    near[RT + 2 * SHARE :] = got[RT:]


def merge_grad_kernel(
    index_ref, tiles_ref, own, r1, r3, r2, gradown, gradgot, mine, got, m0, m1, m2, m3, near, half
):
    near[...] = jnp.maximum(mine[...], got[...])
    link = tree(jnp.maximum, own[...], (r1[...], r2[...], r3[...]))
    half[...] = gradown[CT:OWN] + gradgot[...]
    for k, out in enumerate((m0, m1, m2, m3)):
        out[0:HALF] = link
        out[HALF:] = half[pl.ds(pl.multiple_of((index_ref[PLACE + 1] ^ k) * CHUNK, CHUNK), CHUNK), :]


def merge_chunk_kernel(tiles_ref, own, r2, r1, r3, link, chunk):
    link[...] = tree(jnp.maximum, own[0:HALF], (r1[0:HALF], r2[0:HALF], r3[0:HALF]))
    chunk[...] = tree(jnp.add, own[HALF:], (r1[HALF:], r2[HALF:], r3[HALF:]))


def rows_kernel(
    tiles_ref, r0, r1, r3, r2, rowold, rhs, dual, colown, got, colold, cost, chunk, rownew, rhs_scaled,
    dual_scaled, out,
):
    total = tree(jnp.add, r0[...], (r1[...], r2[...], r3[...]))
    old = rowold[...]
    new = old / jnp.sqrt(old * total + EPS)
    rownew[...] = new
    scaled = new * rhs[...]
    rhs_scaled[...] = scaled
    dual_scaled[...] = dual[...] / new
    out[0:HALF] = colown[CT:OWN] + got[...]
    out[HALF:OWN] = jnp.sum((scaled * scaled).reshape(RT // 8, 8, TILE), axis=0)
    old = colold[0:CT]
    part = old / jnp.sqrt(old * colown[0:CT] + EPS) * cost[...]
    out[OWN : OWN + CT] = part * part
    out[OWN + CT :] = chunk[...]


def merge_all_kernel(index_ref, tiles_ref, own, r1, r3, r2, out):
    at = slice(0, HALF + EIGHT)
    out[at] = tree(jnp.add, own[at], (r1[at], r2[at], r3[at]))
    for k, ref in enumerate((own, r1, r2, r3)):
        start = pl.multiple_of((index_ref[PLACE + 1] ^ k) * CHUNK, CHUNK)
        out[pl.ds(HALF + EIGHT + start, CHUNK), :] = ref[HALF + EIGHT :]


def setup_kernel(
    index_ref, tiles_ref, own, back, colown, colold, cost_loc, cost_lnk, bound_loc, bound_lnk, start_loc, start_lnk,
    colnew, cost, upper, primal, rhs_square, cost_square,
):
    squares = own[HALF : HALF + EIGHT] + back[HALF : HALF + EIGHT]
    rhs_square[...] = squares[0:CT]
    sums = []
    for lo, hi, stat, half in (
        (0, CT, colown, None),
        (CT, OWN, own, index_ref[PLACE + 0]),
        (OWN, CW, back, 1 - index_ref[PLACE + 0]),
    ):
        at = slice(lo, hi)
        if half is None:
            c, b, x = cost_loc[...], bound_loc[...], start_loc[...]
        else:
            rows = pl.ds(pl.multiple_of(half * HALF, HALF), HALF)
            c, b, x = cost_lnk[rows, :], bound_lnk[rows, :], start_lnk[rows, :]
        old = colold[at]
        new = old / jnp.sqrt(old * stat[0 : hi - lo] + EPS)
        colnew[at] = new
        c = new * c
        cost[at] = c
        upper[at] = b / new
        primal[at] = x / new
        if half is not None:
            sums.append(jnp.sum((c * c).reshape(HALF // 8, 8, TILE), axis=0))
    cost_square[...] = squares[CT:] + (sums[0] + sums[1])


def end_kernel(steps, p0, p2, p1, p3, dual, rhs, rowf, out):
    total = tree(jnp.add, p0[...], (p1[...], p2[...], p3[...]))
    scale = rowf[...]
    out[...] = scale * (dual[...] + steps[1:2] * (rhs[...] - scale * total))


def body(
    tile_values,
    tile_rows,
    tile_cols,
    cost_local,
    cost_link,
    bound_local,
    bound_link,
    rhs,
    start_local,
    start_link,
    start_dual,
):
    scen = lax.axis_index("scen")
    core = scen % 2
    x_at, z_at = scen // 8, (scen // 2) % 4
    place = jnp.stack([core, jnp.where(core == 0, z_at, x_at), lax.axis_index("col")])
    ids = (tile_rows[0, 0], tile_cols[0, 0], place)

    def over(swap, x):
        got = {k: swap(x, k) for k in (2, 1, 3)}
        return x, got[1], got[3], got[2]

    row_part, colown, colother, tiles, index = first_stats(ids, tile_values[0, 0], rhs[0], start_dual[0])

    def run(kernel, smem, operands, outs, scratch=(), to_hbm=0):
        return call(kernel, smem, tiles, operands, outs, scratch, to_hbm)

    (link,) = run(functools.partial(core_kernel, jnp.maximum), (), (colown, swap_core(colother)), (HALF,))
    link, near = run(
        merge_rows_kernel, (), (*over(swap_first, link), row_part, swap_y(row_part, 1)), (HALF, RT + 4 * SHARE)
    )
    far = swap_y(near, 3)
    (link,) = run(functools.partial(merge_kernel, jnp.maximum), (), over(swap_second, link), (HALF,))

    gathered = (near, far)
    colown, colother, row_scale, col_scale = run(
        second_columns_kernel,
        (index,),
        (near, far, colown, link, swap_core(link)),
        (OWN, HALF, RT, CW),
        (COLS, ROWS),
    )
    colgot = swap_core(colother)
    (row_part,) = run(second_rows_kernel, (index,), (col_scale,), (RT,), (ROWS, COLS))
    (link,) = run(core_after_kernel, (), (colown, colgot, row_part), (HALF,))
    got = over(swap_first, link)
    gradown, gradother, rhs_rows, dual_rows = run(
        first_backward_kernel, (index,), (*gathered, got[2]), (OWN, HALF, RT, RT), (COLS, ROWS)
    )
    *sent, near = run(
        merge_grad_kernel,
        (index,),
        (*got, gradown, swap_core(gradother), row_part, swap_y(row_part, 1)),
        (HALF + CHUNK,) * 4 + (RT,),
        (pltpu.VMEM((HALF, TILE), F32),),
    )
    far = swap_y(near, 3)
    got = {k: swap_second(sent[k], k) for k in (2, 1, 3)}
    link, chunk = run(merge_chunk_kernel, (), (sent[0], got[2], got[1], got[3]), (HALF, CHUNK))

    row_part, row_scale, col_scale = run(
        third_rows_kernel,
        (index,),
        (near, far, colown, link, swap_core(link), row_scale, col_scale),
        (RT, RT, CW),
        (ROWS, COLS),
    )
    rows = over(swap_y, row_part)
    colown, colother = run(third_columns_kernel, (index,), (row_scale,), (OWN, HALF), (COLS, ROWS))
    row_scale, rhs_scaled, dual_scaled, both = run(
        rows_kernel,
        (),
        (*rows, row_scale, rhs_rows, dual_rows, colown, swap_core(colother), col_scale, cost_local[0, 0], chunk),
        (RT, RT, RT, HALF + EIGHT + CHUNK),
    )
    (both,) = run(
        functools.partial(merge_kernel, jnp.add), (), over(swap_first, both), (HALF + EIGHT + CHUNK,)
    )
    (mine,) = run(merge_all_kernel, (index,), over(swap_second, both), (LT + EIGHT,))
    other = swap_core(mine)
    col_scale, cost, upper, primal, rhs_square, cost_square = run(
        setup_kernel,
        (index,),
        (
            mine,
            other,
            colown,
            col_scale,
            cost_local[0, 0],
            cost_link[0],
            bound_local[0, 0],
            bound_link[0],
            start_local[0, 0],
            start_link[0],
        ),
        (CW, CW, CW, CW, CT, CT),
    )
    norms = (*over(swap_y, cost_square), rhs_square)

    grads, grad_at = (gradown, mine, other), HALF + EIGHT
    leaving = (pltpu.VMEM((CT, TILE), F32), pltpu.VMEM((LT, TILE), F32), pltpu.SemaphoreType.DMA((2,)))
    for step in range(ITERS):
        given = norms if step == 0 else (steps,)
        extra = (dual_scaled, rhs_scaled, row_scale) if step == ITERS - 1 else ()
        outs = (RT, CW) if step < ITERS - 1 else (CT, LT) + (SHARE,) * 7
        result = run(
            functools.partial(forward_kernel, step, grad_at),
            (index,),
            (*given, *grads, primal, cost, upper, col_scale, *extra),
            ((CT,) if step == 0 else ()) + outs,
            (ROWS, COLS) + (leaving if step == ITERS - 1 else ()),
            2 if step == ITERS - 1 else 0,
        )
        if step == 0:
            steps, *result = result
        if step == ITERS - 1:
            break
        row_part, primal = result
        colown, colother, dual_scaled = run(
            backward_kernel,
            (index,),
            (steps, *over(swap_y, row_part), dual_scaled, rhs_scaled, row_scale),
            (OWN, HALF, RT),
            (COLS, ROWS),
        )
        (link,) = run(functools.partial(core_kernel, jnp.add), (), (colown, swap_core(colother)), (HALF,))
        (link,) = run(functools.partial(merge_kernel, jnp.add), (), over(swap_first, link), (HALF,))
        (link,) = run(functools.partial(merge_kernel, jnp.add), (), over(swap_second, link), (HALF,))
        grads, grad_at = (colown, link, swap_core(link)), 0

    local, link, dual, rhs_own, scale, *pieces = result
    got = {k: swap_y(pieces[k], k) for k in (2, 1, 3)}
    vmem = pl.BlockSpec(memory_space=pltpu.VMEM)
    multipliers = pl.pallas_call(
        end_kernel,
        out_shape=jax.ShapeDtypeStruct((SHARE, TILE), F32),
        in_specs=[vmem] * 8,
        out_specs=vmem,
        compiler_params=pltpu.CompilerParams(vmem_limit_bytes=1024 * 1024),
    )(steps, pieces[0], got[2], got[1], got[3], dual, rhs_own, scale)
    return local[None, None], link[None], multipliers[None]


def solution(mesh):
    placed = (
        P("scen", "col", None, None, None),
        P("scen", "col", None),
        P("scen", "col", None),
        P("scen", "col", None, None),
        P("col", None, None),
        P("scen", "col", None, None),
        P("col", None, None),
        P("scen", "col", None),
        P("scen", "col", None, None),
        P("col", None, None),
        P("scen", "col", None),
    )
    return jax.shard_map(
        body,
        mesh=mesh,
        in_specs=placed,
        out_specs=(P("scen", "col", None, None), P("col", None, None), P("scen", "col", None)),
        check_vma=False,
    )
```

```python
import functools

import jax
import jax.numpy as jnp
from jax import lax
from jax.experimental import pallas as pl
from jax.experimental.pallas import tpu as pltpu
from jax.sharding import PartitionSpec as P

TILE = 256
RT = 128
CT = 8
LT = 256
ITERS = 3
NT = 64
HALF = LT // 2
SHARE = RT // 4
CW = CT + LT
GROUP = 8
STEPS = NT // GROUP
PIECE = GROUP // 2
LOADS = NT // PIECE

EPS = 1e-06
STEP = 0.9
F32 = jnp.float32
LANES = 128
VMEM_LIMIT = 24 * 1024 * 1024


def swap_core(x):
    return lax.ppermute(x, "scen", [(i, i ^ 1) for i in range(32)])


def swap_first(x, k):
    return lax.ppermute(x, "scen", [(i, i ^ (k << (1 if i % 2 else 3))) for i in range(32)])


def swap_second(x, k):
    return lax.ppermute(x, "scen", [(i, i ^ (k << (3 if i % 2 else 1))) for i in range(32)])


def swap_y(x, k):
    return lax.ppermute(x, "col", [(i, i ^ k) for i in range(4)])


def tree(op, own, got):
    return op(op(own, got[0]), op(got[1], got[2]))


def row_pass(tiles_ref, t, col, row, colf_ref, rowout_ref, op, magnitude):
    for h in range(2):
        a = tiles_ref[t, h * LANES : (h + 1) * LANES, 0:LANES]
        b = tiles_ref[t, h * LANES : (h + 1) * LANES, LANES:TILE]
        if magnitude:
            a, b = jnp.abs(a), jnp.abs(b)
        if colf_ref is not None:
            a = a * colf_ref[0, pl.ds(col, 1), :]
            b = b * colf_ref[1, pl.ds(col, 1), :]
        m = op(a, b).T
        s = jnp.max(m, axis=0, keepdims=True) if op is jnp.maximum else jnp.sum(m, axis=0, keepdims=True)
        at = (h, pl.ds(row, 1), slice(None))
        rowout_ref[at] = op(rowout_ref[at], s)


def col_pass(tiles_ref, t, col, row, rowf_ref, colout_ref, op, magnitude):
    parts = [None, None]
    for h in range(2):
        if rowf_ref is not None:
            f = jnp.broadcast_to(rowf_ref[h, pl.ds(row, 1), :], (LANES, LANES)).T
        for w in range(2):
            a = tiles_ref[t, h * LANES : (h + 1) * LANES, w * LANES : (w + 1) * LANES]
            if magnitude:
                a = jnp.abs(a)
            if rowf_ref is not None:
                a = a * f
            a = a.reshape(16, 8, LANES)
            s = jnp.max(a, axis=0) if op is jnp.maximum else jnp.sum(a, axis=0)
            parts[w] = s if parts[w] is None else op(parts[w], s)
    for w in range(2):
        s = parts[w]
        s = jnp.max(s, axis=0, keepdims=True) if op is jnp.maximum else jnp.sum(s, axis=0, keepdims=True)
        at = (w, pl.ds(col, 1), slice(None))
        colout_ref[at] = op(colout_ref[at], s)


def both_pass(tiles_ref, t, col, row, rowf_ref, colf_ref, rowout_ref, colout_ref):
    parts = [None, None]
    for h in range(2):
        at = slice(h * LANES, (h + 1) * LANES)
        blocks = [jnp.abs(tiles_ref[t, at, w * LANES : (w + 1) * LANES]) for w in range(2)]
        factor = None if rowf_ref is None else jnp.broadcast_to(rowf_ref[h, pl.ds(row, 1), :], (LANES, LANES)).T
        scaled = blocks if colf_ref is None else [a * colf_ref[w, pl.ds(col, 1), :] for w, a in enumerate(blocks)]
        s = jnp.max(jnp.maximum(scaled[0], scaled[1]).T, axis=0, keepdims=True)
        at = (h, pl.ds(row, 1), slice(None))
        rowout_ref[at] = jnp.maximum(rowout_ref[at], s)
        for w, a in enumerate(blocks):
            a = a if factor is None else a * factor
            s = jnp.max(a.reshape(16, 8, LANES), axis=0)
            parts[w] = s if parts[w] is None else jnp.maximum(parts[w], s)
    for w in range(2):
        at = (w, pl.ds(col, 1), slice(None))
        colout_ref[at] = jnp.maximum(colout_ref[at], jnp.max(parts[w], axis=0, keepdims=True))


def split_to(ref, value, lo=0):
    for w in range(2):
        ref[w, lo : lo + value.shape[0], :] = value[:, w * LANES : (w + 1) * LANES]


def join_from(ref, out, lo, hi):
    for w in range(2):
        out[0 : hi - lo, w * LANES : (w + 1) * LANES] = ref[w, lo:hi, :]


ROWS = pltpu.VMEM((2, RT, LANES), F32)
COLS = pltpu.VMEM((2, CW, LANES), F32)
OWN = CT + HALF
PLACE = 2 * NT
EIGHT = 2 * CT
CHUNK = HALF // 4


def call(kernel, smem, tiles, operands, outs, scratch=(), to_hbm=0):
    operands = [pltpu.with_memory_space_constraint(tiles, pltpu.VMEM)] + list(operands)
    smem = [pltpu.with_memory_space_constraint(x, pltpu.SMEM) for x in smem]
    vmem = pl.BlockSpec(memory_space=pltpu.VMEM)
    return pl.pallas_call(
        kernel,
        out_shape=tuple(jax.ShapeDtypeStruct((n, TILE), F32) for n in outs),
        in_specs=[pl.BlockSpec(memory_space=pltpu.SMEM) for _ in smem] + [vmem for _ in operands],
        out_specs=tuple(pl.BlockSpec(memory_space=pltpu.HBM) if i < to_hbm else vmem for i in range(len(outs))),
        scratch_shapes=list(scratch),
        compiler_params=pltpu.CompilerParams(vmem_limit_bytes=VMEM_LIMIT),
    )(*smem, *operands)


def each_tile(index_ref, visit, ready=None):
    def group(step, carry):
        for i in range(GROUP):
            if ready is not None and i % PIECE == 0:
                ready(step * (GROUP // PIECE) + i // PIECE)
            t = step * GROUP + i
            visit(t, index_ref[NT + t], index_ref[t])
        return carry

    lax.fori_loop(0, STEPS, group, 0)


def put_columns(cacc, colown, colother):
    join_from(cacc, colown, 0, OWN)
    join_from(cacc, colother, OWN, CW)


def first_stats_kernel(
    place, rows_hbm, cols_hbm, source, dual, rowout, colown, colother, tiles_ref, index_ref, racc, cacc,
    rows_ref, cols_ref, sems,
):
    indices = [
        pltpu.make_async_copy(src, dst, sems.at[LOADS + 2 + i])
        for i, (src, dst) in enumerate(((rows_hbm, rows_ref), (cols_hbm, cols_ref)))
    ]
    for copy in indices:
        copy.start()
    for i in range(3):
        index_ref[PLACE + i] = place[i]

    def load(step):
        part = pl.ds(step * PIECE, PIECE)
        return pltpu.make_async_copy(source.at[part], tiles_ref.at[part], sems.at[step])

    for step in range(LOADS):
        load(step).start()
    extra = [
        pltpu.make_async_copy(src, rowout.at[pl.ds(RT + i * SHARE, SHARE)], sems.at[LOADS + i])
        for i, src in enumerate((dual,))
    ]
    for copy in extra:
        copy.start()
    racc[...] = jnp.zeros_like(racc)
    cacc[...] = jnp.zeros_like(cacc)

    for copy in indices:
        copy.wait()
    turn = place[0] * HALF

    def enter(t, carry):
        col = cols_ref[t]
        index_ref[t] = rows_ref[t]
        index_ref[NT + t] = jnp.where(col < CT, col, CT + ((col - CT) ^ turn))
        return carry

    lax.fori_loop(0, NT, enter, 0)

    def visit(t, col, row):
        both_pass(tiles_ref, t, col, row, None, None, racc, cacc)

    each_tile(index_ref, visit, lambda step: load(step).wait())
    join_from(racc, rowout, 0, RT)
    put_columns(cacc, colown, colother)
    for copy in extra:
        copy.wait()


def first_stats(ids, source, dual):
    vmem = pl.BlockSpec(memory_space=pltpu.VMEM)
    shapes = [jax.ShapeDtypeStruct((n, TILE), F32) for n in (RT + SHARE, OWN, HALF)]
    return pl.pallas_call(
        first_stats_kernel,
        out_shape=(*shapes, pltpu.VMEM((NT, TILE, TILE), F32), pltpu.SMEM((PLACE + 8,), jnp.int32)),
        in_specs=[pl.BlockSpec(memory_space=pltpu.SMEM)] + [pl.BlockSpec(memory_space=pltpu.HBM)] * 4,
        out_specs=(vmem,) * 4 + (pl.BlockSpec(memory_space=pltpu.SMEM),),
        scratch_shapes=[
            ROWS,
            COLS,
            pltpu.SMEM((NT,), jnp.int32),
            pltpu.SMEM((NT,), jnp.int32),
            pltpu.SemaphoreType.DMA((LOADS + 4,)),
        ],
        compiler_params=pltpu.CompilerParams(vmem_limit_bytes=VMEM_LIMIT),
    )(ids[2], *(pltpu.with_memory_space_constraint(x, pltpu.HBM) for x in (*ids[:2], source, dual)))


def gather_rows(index_ref, near, far, out):
    for k, ref, start in ((0, near, RT), (1, near, RT + SHARE), (3, far, RT), (2, far, RT + SHARE)):
        at = pl.ds(pl.multiple_of((index_ref[PLACE + 2] ^ k) * SHARE, SHARE), SHARE)
        out[at, :] = ref[start : start + SHARE]


def merge_near(mine, got, near):
    near[0:RT] = jnp.maximum(mine[0:RT], got[0:RT])
    near[RT : RT + SHARE] = mine[RT:]
    near[RT + SHARE :] = got[RT:]


def second_columns_kernel(
    index_ref, tiles_ref, near, far, loc, mine, other, colown, colother, rownew, colnew, cacc, rowf
):
    row = jnp.maximum(near[0:RT], far[0:RT])
    new = 1.0 / jnp.sqrt(row + EPS)
    rownew[...] = new
    split_to(rowf, new)
    for lo, hi, src in ((0, CT, loc), (CT, OWN, mine), (OWN, CW, other)):
        colnew[lo:hi] = 1.0 / jnp.sqrt(src[0 : hi - lo] + EPS)
    cacc[...] = jnp.zeros_like(cacc)

    def visit(t, col, row):
        col_pass(tiles_ref, t, col, row, rowf, cacc, jnp.maximum, True)

    each_tile(index_ref, visit)
    put_columns(cacc, colown, colother)


def second_rows_kernel(index_ref, tiles_ref, col_scale, rhs, rowout, racc, colf):
    rowout[RT:] = rhs[...]
    split_to(colf, col_scale[...])
    racc[...] = jnp.zeros_like(racc)

    def visit(t, col, row):
        row_pass(tiles_ref, t, col, row, colf, racc, jnp.maximum, True)

    each_tile(index_ref, visit)
    join_from(racc, rowout, 0, RT)


def third_rows_kernel(
    index_ref, tiles_ref, near, far, loc, mine, other, rowold, colold, rowout, rownew,
    colnew, rhsout, racc, colf,
):
    gather_rows(index_ref, near, far, rhsout)
    row = jnp.maximum(near[0:RT], far[0:RT])
    old = rowold[...]
    rownew[...] = old / jnp.sqrt(old * row + EPS)
    for lo, hi, src in ((0, CT, loc), (CT, OWN, mine), (OWN, CW, other)):
        old = colold[lo:hi]
        new = old / jnp.sqrt(old * src[0 : hi - lo] + EPS)
        colnew[lo:hi] = new
        split_to(colf, new, lo)
    racc[...] = jnp.zeros_like(racc)

    def visit(t, col, row):
        row_pass(tiles_ref, t, col, row, colf, racc, jnp.add, True)

    each_tile(index_ref, visit)
    join_from(racc, rowout, 0, RT)


def third_columns_kernel(index_ref, tiles_ref, row_scale, colown, colother, cacc, rowf):
    split_to(rowf, row_scale[...])
    cacc[...] = jnp.zeros_like(cacc)

    def visit(t, col, row):
        col_pass(tiles_ref, t, col, row, rowf, cacc, jnp.add, True)

    each_tile(index_ref, visit)
    put_columns(cacc, colown, colother)


def first_backward_kernel(
    index_ref, tiles_ref, near, far, after, colown, colother, dualout, cacc, work
):
    gather_rows(index_ref, near, far, dualout)
    split_to(work, dualout[...])
    cacc[...] = jnp.zeros_like(cacc)

    def visit(t, col, row):
        col_pass(tiles_ref, t, col, row, work, cacc, jnp.add, False)

    each_tile(index_ref, visit)
    put_columns(cacc, colown, colother)


def backward_kernel(
    index_ref, tiles_ref, steps, r0, r1, r3, r2, dual, rhs, rowf, colown, colother, dualnew,
    cacc, work,
):
    total = tree(jnp.add, r0[...], (r1[...], r2[...], r3[...]))
    new = dual[...] + steps[1:2] * (rhs[...] - rowf[...] * total)
    dualnew[...] = new
    split_to(work, rowf[...] * new)
    cacc[...] = jnp.zeros_like(cacc)

    def visit(t, col, row):
        col_pass(tiles_ref, t, col, row, work, cacc, jnp.add, False)

    each_tile(index_ref, visit)
    put_columns(cacc, colown, colother)


def forward_kernel(index, grad_at, index_ref, tiles_ref, *rest):
    if index == 0:
        c0, c1, c3, c2, rhs_square, *rest = rest
    else:
        steps, *rest = rest
    loc, mine, other, primal, cost, upper, colf, *rest = rest
    if index == 0:
        steps, *rest = rest
        total = tree(jnp.add, c0[...], (c1[...], c2[...], c3[...]))
        cost_sum = jnp.sum(total, axis=(0, 1), keepdims=True)
        rhs_sum = jnp.sum(rhs_square[...], axis=(0, 1), keepdims=True)
        ratio = jnp.sqrt((cost_sum + EPS) / (rhs_sum + EPS))
        steps[...] = jnp.zeros_like(steps)
        steps[0:1] = jnp.broadcast_to(STEP / ratio, (1, TILE))
        steps[1:2] = jnp.broadcast_to(STEP * ratio, (1, TILE))
    if index < ITERS - 1:
        rowout, fresh, racc, work = rest
    else:
        dual, rhs, rowf, local_hbm, link_hbm, dualout, rhsout, rowfout, p0, p1, p2, p3, *rest = rest
        racc, work, local, link, sems = rest
        own = pl.ds(pl.multiple_of(index_ref[PLACE + 2] * SHARE, SHARE), SHARE)
        for ref, out in ((dual, dualout), (rhs, rhsout), (rowf, rowfout)):
            out[...] = ref[own, :]
    for lo, hi, src, first in ((0, CT, loc, 0), (CT, OWN, mine, grad_at), (OWN, CW, other, grad_at)):
        at = slice(lo, hi)
        x, scale = primal[at], colf[at]
        grad = scale * src[first : first + hi - lo]
        new = jnp.clip(x - steps[0:1] * (cost[at] - grad), 0.0, upper[at])
        if index < ITERS - 1:
            fresh[at] = new
        elif lo == 0:
            local[...] = scale * new
        else:
            half = index_ref[PLACE + 0] if lo == CT else 1 - index_ref[PLACE + 0]
            link[pl.ds(pl.multiple_of(half * HALF, HALF), HALF), :] = scale * new
        split_to(work, scale * (2.0 * new - x), lo)
    leaving = []
    if index == ITERS - 1:
        leaving = [
            pltpu.make_async_copy(src, dst, sems.at[i])
            for i, (src, dst) in enumerate(((local, local_hbm), (link, link_hbm)))
        ]
    for copy in leaving:
        copy.start()
    racc[...] = jnp.zeros_like(racc)

    def visit(t, col, row):
        row_pass(tiles_ref, t, col, row, work, racc, jnp.add, False)

    each_tile(index_ref, visit)
    if index < ITERS - 1:
        join_from(racc, rowout, 0, RT)
    else:
        for k, out in enumerate((p0, p1, p2, p3)):
            at = pl.ds(pl.multiple_of((index_ref[PLACE + 2] ^ k) * SHARE, SHARE), SHARE)
            for w in range(2):
                out[:, w * LANES : (w + 1) * LANES] = racc[w, at, :]
    for copy in leaving:
        copy.wait()


def core_kernel(op, tiles_ref, colown, got, out):
    out[...] = op(colown[CT:OWN], got[...])


def core_after_kernel(tiles_ref, colown, got, after, out):
    out[...] = jnp.maximum(colown[CT:OWN], got[...])


def merge_kernel(op, tiles_ref, own, r1, r3, r2, out):
    out[...] = tree(op, own[...], (r1[...], r2[...], r3[...]))


def merge_rows_kernel(tiles_ref, own, r1, r3, r2, mine, got, out, near):
    out[...] = tree(jnp.maximum, own[...], (r1[...], r2[...], r3[...]))
    merge_near(mine, got, near)


def merge_grad_kernel(
    index_ref, tiles_ref, own, r1, r3, r2, gradown, gradgot, mine, got, m0, m1, m2, m3, near, half
):
    merge_near(mine, got, near)
    link = tree(jnp.maximum, own[...], (r1[...], r2[...], r3[...]))
    half[...] = gradown[CT:OWN] + gradgot[...]
    for k, out in enumerate((m0, m1, m2, m3)):
        out[0:HALF] = link
        out[HALF:] = half[pl.ds(pl.multiple_of((index_ref[PLACE + 1] ^ k) * CHUNK, CHUNK), CHUNK), :]


def merge_chunk_kernel(tiles_ref, own, r2, r1, r3, link, chunk):
    link[...] = tree(jnp.maximum, own[0:HALF], (r1[0:HALF], r2[0:HALF], r3[0:HALF]))
    chunk[...] = tree(jnp.add, own[HALF:], (r1[HALF:], r2[HALF:], r3[HALF:]))


def rows_kernel(
    tiles_ref, r0, r1, r3, r2, rowold, rhs, dual, colown, got, colold, cost, chunk, rownew, rhs_scaled,
    dual_scaled, out,
):
    total = tree(jnp.add, r0[...], (r1[...], r2[...], r3[...]))
    old = rowold[...]
    new = old / jnp.sqrt(old * total + EPS)
    rownew[...] = new
    scaled = new * rhs[...]
    rhs_scaled[...] = scaled
    dual_scaled[...] = dual[...] / new
    out[0:HALF] = colown[CT:OWN] + got[...]
    out[HALF:OWN] = jnp.sum((scaled * scaled).reshape(RT // 8, 8, TILE), axis=0)
    old = colold[0:CT]
    part = old / jnp.sqrt(old * colown[0:CT] + EPS) * cost[...]
    out[OWN : OWN + CT] = part * part
    out[OWN + CT :] = chunk[...]


def merge_all_kernel(index_ref, tiles_ref, own, r1, r3, r2, out):
    at = slice(0, HALF + EIGHT)
    out[at] = tree(jnp.add, own[at], (r1[at], r2[at], r3[at]))
    for k, ref in enumerate((own, r1, r2, r3)):
        start = pl.multiple_of((index_ref[PLACE + 1] ^ k) * CHUNK, CHUNK)
        out[pl.ds(HALF + EIGHT + start, CHUNK), :] = ref[HALF + EIGHT :]


def setup_kernel(
    index_ref, tiles_ref, own, back, colown, colold, cost_loc, cost_lnk, bound_loc, bound_lnk, start_loc, start_lnk,
    colnew, cost, upper, primal, rhs_square, cost_square,
):
    squares = own[HALF : HALF + EIGHT] + back[HALF : HALF + EIGHT]
    rhs_square[...] = squares[0:CT]
    sums = []
    for lo, hi, stat, half in (
        (0, CT, colown, None),
        (CT, OWN, own, index_ref[PLACE + 0]),
        (OWN, CW, back, 1 - index_ref[PLACE + 0]),
    ):
        at = slice(lo, hi)
        if half is None:
            c, b, x = cost_loc[...], bound_loc[...], start_loc[...]
        else:
            rows = pl.ds(pl.multiple_of(half * HALF, HALF), HALF)
            c, b, x = cost_lnk[rows, :], bound_lnk[rows, :], start_lnk[rows, :]
        old = colold[at]
        new = old / jnp.sqrt(old * stat[0 : hi - lo] + EPS)
        colnew[at] = new
        c = new * c
        cost[at] = c
        upper[at] = b / new
        primal[at] = x / new
        if half is not None:
            sums.append(jnp.sum((c * c).reshape(HALF // 8, 8, TILE), axis=0))
    cost_square[...] = squares[CT:] + (sums[0] + sums[1])


def end_kernel(steps, p0, p2, p1, p3, dual, rhs, rowf, out):
    total = tree(jnp.add, p0[...], (p1[...], p2[...], p3[...]))
    scale = rowf[...]
    out[...] = scale * (dual[...] + steps[1:2] * (rhs[...] - scale * total))


def body(
    tile_values,
    tile_rows,
    tile_cols,
    cost_local,
    cost_link,
    bound_local,
    bound_link,
    rhs,
    start_local,
    start_link,
    start_dual,
):
    scen = lax.axis_index("scen")
    core = scen % 2
    x_at, z_at = scen // 8, (scen // 2) % 4
    place = jnp.stack([core, jnp.where(core == 0, z_at, x_at), lax.axis_index("col")])
    ids = (tile_rows[0, 0], tile_cols[0, 0], place)

    def over(swap, x):
        got = {k: swap(x, k) for k in (2, 1, 3)}
        return x, got[1], got[3], got[2]

    row_part, colown, colother, tiles, index = first_stats(ids, tile_values[0, 0], start_dual[0])

    def run(kernel, smem, operands, outs, scratch=(), to_hbm=0):
        return call(kernel, smem, tiles, operands, outs, scratch, to_hbm)

    (link,) = run(functools.partial(core_kernel, jnp.maximum), (), (colown, swap_core(colother)), (HALF,))
    link, near = run(
        merge_rows_kernel, (), (*over(swap_first, link), row_part, swap_y(row_part, 1)), (HALF, RT + 2 * SHARE)
    )
    far = swap_y(near, 3)
    (link,) = run(functools.partial(merge_kernel, jnp.maximum), (), over(swap_second, link), (HALF,))

    gathered = (near, far)
    colown, colother, row_scale, col_scale = run(
        second_columns_kernel,
        (index,),
        (near, far, colown, link, swap_core(link)),
        (OWN, HALF, RT, CW),
        (COLS, ROWS),
    )
    colgot = swap_core(colother)
    (row_part,) = run(second_rows_kernel, (index,), (col_scale, rhs[0]), (RT + SHARE,), (ROWS, COLS))
    (link,) = run(core_after_kernel, (), (colown, colgot, row_part), (HALF,))
    got = over(swap_first, link)
    gradown, gradother, dual_rows = run(
        first_backward_kernel, (index,), (*gathered, got[2]), (OWN, HALF, RT), (COLS, ROWS)
    )
    *sent, near = run(
        merge_grad_kernel,
        (index,),
        (*got, gradown, swap_core(gradother), row_part, swap_y(row_part, 1)),
        (HALF + CHUNK,) * 4 + (RT + 2 * SHARE,),
        (pltpu.VMEM((HALF, TILE), F32),),
    )
    far = swap_y(near, 3)
    got = {k: swap_second(sent[k], k) for k in (2, 1, 3)}
    link, chunk = run(merge_chunk_kernel, (), (sent[0], got[2], got[1], got[3]), (HALF, CHUNK))

    row_part, row_scale, col_scale, rhs_rows = run(
        third_rows_kernel,
        (index,),
        (near, far, colown, link, swap_core(link), row_scale, col_scale),
        (RT, RT, CW, RT),
        (ROWS, COLS),
    )
    rows = over(swap_y, row_part)
    colown, colother = run(third_columns_kernel, (index,), (row_scale,), (OWN, HALF), (COLS, ROWS))
    row_scale, rhs_scaled, dual_scaled, both = run(
        rows_kernel,
        (),
        (*rows, row_scale, rhs_rows, dual_rows, colown, swap_core(colother), col_scale, cost_local[0, 0], chunk),
        (RT, RT, RT, HALF + EIGHT + CHUNK),
    )
    (both,) = run(
        functools.partial(merge_kernel, jnp.add), (), over(swap_first, both), (HALF + EIGHT + CHUNK,)
    )
    (mine,) = run(merge_all_kernel, (index,), over(swap_second, both), (LT + EIGHT,))
    other = swap_core(mine)
    col_scale, cost, upper, primal, rhs_square, cost_square = run(
        setup_kernel,
        (index,),
        (
            mine,
            other,
            colown,
            col_scale,
            cost_local[0, 0],
            cost_link[0],
            bound_local[0, 0],
            bound_link[0],
            start_local[0, 0],
            start_link[0],
        ),
        (CW, CW, CW, CW, CT, CT),
    )
    norms = (*over(swap_y, cost_square), rhs_square)

    grads, grad_at = (gradown, mine, other), HALF + EIGHT
    leaving = (pltpu.VMEM((CT, TILE), F32), pltpu.VMEM((LT, TILE), F32), pltpu.SemaphoreType.DMA((2,)))
    for step in range(ITERS):
        given = norms if step == 0 else (steps,)
        extra = (dual_scaled, rhs_scaled, row_scale) if step == ITERS - 1 else ()
        outs = (RT, CW) if step < ITERS - 1 else (CT, LT) + (SHARE,) * 7
        result = run(
            functools.partial(forward_kernel, step, grad_at),
            (index,),
            (*given, *grads, primal, cost, upper, col_scale, *extra),
            ((CT,) if step == 0 else ()) + outs,
            (ROWS, COLS) + (leaving if step == ITERS - 1 else ()),
            2 if step == ITERS - 1 else 0,
        )
        if step == 0:
            steps, *result = result
        if step == ITERS - 1:
            break
        row_part, primal = result
        colown, colother, dual_scaled = run(
            backward_kernel,
            (index,),
            (steps, *over(swap_y, row_part), dual_scaled, rhs_scaled, row_scale),
            (OWN, HALF, RT),
            (COLS, ROWS),
        )
        (link,) = run(functools.partial(core_kernel, jnp.add), (), (colown, swap_core(colother)), (HALF,))
        (link,) = run(functools.partial(merge_kernel, jnp.add), (), over(swap_first, link), (HALF,))
        (link,) = run(functools.partial(merge_kernel, jnp.add), (), over(swap_second, link), (HALF,))
        grads, grad_at = (colown, link, swap_core(link)), 0

    local, link, dual, rhs_own, scale, *pieces = result
    got = {k: swap_y(pieces[k], k) for k in (2, 1, 3)}
    vmem = pl.BlockSpec(memory_space=pltpu.VMEM)
    multipliers = pl.pallas_call(
        end_kernel,
        out_shape=jax.ShapeDtypeStruct((SHARE, TILE), F32),
        in_specs=[vmem] * 8,
        out_specs=vmem,
        compiler_params=pltpu.CompilerParams(vmem_limit_bytes=1024 * 1024),
    )(steps, pieces[0], got[2], got[1], got[3], dual, rhs_own, scale)
    return local[None, None], link[None], multipliers[None]


def solution(mesh):
    placed = (
        P("scen", "col", None, None, None),
        P("scen", "col", None),
        P("scen", "col", None),
        P("scen", "col", None, None),
        P("col", None, None),
        P("scen", "col", None, None),
        P("col", None, None),
        P("scen", "col", None),
        P("scen", "col", None, None),
        P("col", None, None),
        P("scen", "col", None),
    )
    return jax.shard_map(
        body,
        mesh=mesh,
        in_specs=placed,
        out_specs=(P("scen", "col", None, None), P("col", None, None), P("scen", "col", None)),
        check_vma=False,
    )
```
